512 devices in a mesh: lat: 16 (over y_lo, x, core), lon: 32 (over z, y_hi).
Axes of the slice: x: 4, y: 4 (y_hi: 2, y_lo: 2; y = y_hi * 2 + y_lo), z: 16, core: 2. Of those that a mesh axis runs over, the one named last changes fastest.
Arguments:
- tracers: float32 [4, 8, 256, 4096], P(None, None, 'lat', 'lon'), may hold values from -6 to 6
- velocity: float32 [2, 8, 256, 4096], P(None, None, 'lat', 'lon'), may hold values from -3 to 3
- surface: float32 [256, 4096], P('lat', 'lon'), may hold values from -2 to 2
- wind: float32 [2, 256, 4096], P(None, 'lat', 'lon'), may hold values from -5 to 5
- bottom: int32 [256, 4096], P('lat', 'lon'), may hold values from 0 to 8
Outputs:
- tracers_new: float32 [4, 8, 256, 4096], P(None, None, 'lat', 'lon')
- velocity_new: float32 [2, 8, 256, 4096], P(None, None, 'lat', 'lon')
- height: float32 [256, 4096], P('lat', 'lon')
- streamfunction: float32 [256, 4096], P('lat', 'lon')
The draws below stay inside these ranges and needn't reach their ends.
All inputs are finite; a program needn't handle non-finite values.
Results may differ from the reference program's by a relative error of at most 0.0003.
Values sent between devices are 32-bit elements; how exact they have to be, the bound alone decides.
No kernel may reach another device: no remote copies, remote signals or barrier semaphores. Data moves between devices by JAX's collectives and lax.ppermute only.
A program may use at most 64 MiB of HBM per device.

```python
import jax
import jax.numpy as jnp
from jax import lax

TRACERS = 4
LEVELS = 8
SUBSTEPS = 30
NLAT = 256
NLON = 4096


def touch_ends(drawn, stream_key, smallest, largest):
    shape = drawn.shape
    index_at = [jax.random.randint(jax.random.fold_in(stream_key, axis), (), 0, shape[axis]) for axis in range(len(shape))]
    drawn = drawn.at[tuple(index_at)].set(smallest)
    longest = shape.index(max(shape))
    index_at[longest] = (index_at[longest] + 1) % shape[longest]
    return drawn.at[tuple(index_at)].set(largest)


def shard_levels(own_key, extent, split, low, high):
    loudness = 1.0
    for axis_at, parts in split:
        steps = jax.random.uniform(jax.random.fold_in(jax.random.fold_in(own_key, 6), axis_at), (parts,), jnp.float32, low / len(split), high / len(split))
        loudness = loudness * jnp.repeat(jnp.exp(steps), extent[axis_at] // parts).reshape((-1,) + (1,) * (len(extent) - 1 - axis_at))
    return loudness


def centred(own_key, extent, scale, most, pieces=(), held_as=jnp.bfloat16):
    entries = scale * jax.random.normal(own_key, extent, jnp.float32)
    if pieces:
        entries = entries * shard_levels(own_key, extent, pieces, -0.22, 0.18)
    return jnp.clip(entries, -most, most).astype(held_as)


def setup_inputs(seed: int = 0) -> dict:
    arg_keys = jax.random.split(jax.random.key(seed), 6)
    return {
        "tracers": centred(arg_keys[0], (TRACERS, LEVELS, NLAT, NLON), 1.0, 6.0, ((2, 16), (3, 32)), jnp.float32),
        "velocity": centred(arg_keys[1], (2, LEVELS, NLAT, NLON), 0.5, 3.0, ((2, 16), (3, 32)), jnp.float32),
        "surface": centred(arg_keys[2], (NLAT, NLON), 0.3, 2.0, ((0, 16), (1, 32)), jnp.float32),
        "wind": centred(arg_keys[3], (2, NLAT, NLON), 1.0, 5.0, ((1, 16), (2, 32)), jnp.float32),
        "bottom": touch_ends(jax.random.randint(arg_keys[4], (NLAT, NLON), 0, LEVELS + 1), jax.random.fold_in(arg_keys[4], 1), 0, LEVELS).astype(jnp.int32),
    }


time_step = 0.2
tracer_diffusion = 0.2
viscosity = 0.2
thermal_expansion = 2.0
haline_contraction = 1.5
coriolis_base = 1.0
gravity = 140.0
surface_scale = 40.0


def window(values, rim, row_lo, row_hi, col_lo, col_hi):
    return values[..., rim + row_lo: rim + row_hi, rim + col_lo: rim + col_hi]


def baroclinic(tracer_wide, current_wide, bottom_wide, row_start, rows_total, wind):
    levels = tracer_wide.shape[1]
    row_count = bottom_wide.shape[0] - 6
    col_count = bottom_wide.shape[1] - 6
    thickness = 1.0 / levels
    level_ids = lax.broadcasted_iota(jnp.int32, (levels, 1, 1), 0)
    wet_mask = (level_ids < bottom_wide[None]).astype(jnp.float32)
    tracer_vals = tracer_wide * wet_mask

    def wet_win(row_lo, row_hi, col_lo, col_hi):
        return window(wet_mask, 3, row_lo, row_hi, col_lo, col_hi)

    def tracer_win(row_lo, row_hi, col_lo, col_hi):
        return window(tracer_vals, 3, row_lo, row_hi, col_lo, col_hi)

    zonal_flow = current_wide[0] * wet_win(-1, row_count + 1, -1, col_count + 1) * wet_win(-1, row_count + 1, 0, col_count + 2)
    merid_flow = current_wide[1] * wet_win(-1, row_count + 1, -1, col_count + 1) * wet_win(0, row_count + 2, -1, col_count + 1)

    def zonal_win(row_lo, row_hi, col_lo, col_hi):
        return window(zonal_flow, 1, row_lo, row_hi, col_lo, col_hi)

    def merid_win(row_lo, row_hi, col_lo, col_hi):
        return window(merid_flow, 1, row_lo, row_hi, col_lo, col_hi)

    east_face = wet_win(0, row_count, -1, col_count) * wet_win(0, row_count, 0, col_count + 1)
    east_value = (37.0 * (tracer_win(0, row_count, -1, col_count) + tracer_win(0, row_count, 0, col_count + 1))
                  - 8.0 * (tracer_win(0, row_count, -2, col_count - 1) + tracer_win(0, row_count, 1, col_count + 2))
                  + (tracer_win(0, row_count, -3, col_count - 2) + tracer_win(0, row_count, 2, col_count + 3))) / 60.0
    east_flux = (tracer_diffusion * east_face * (tracer_win(0, row_count, 0, col_count + 1) - tracer_win(0, row_count, -1, col_count))
                 - zonal_win(0, row_count, -1, col_count) * east_value)
    north_face = wet_win(-1, row_count, 0, col_count) * wet_win(0, row_count + 1, 0, col_count)
    north_value = (37.0 * (tracer_win(-1, row_count, 0, col_count) + tracer_win(0, row_count + 1, 0, col_count))
                   - 8.0 * (tracer_win(-2, row_count - 1, 0, col_count) + tracer_win(1, row_count + 2, 0, col_count))
                   + (tracer_win(-3, row_count - 2, 0, col_count) + tracer_win(2, row_count + 3, 0, col_count))) / 60.0
    north_flux = (tracer_diffusion * north_face * (tracer_win(0, row_count + 1, 0, col_count) - tracer_win(-1, row_count, 0, col_count))
                  - merid_win(-1, row_count, 0, col_count) * north_value)
    tendency = east_flux[..., 1:] - east_flux[..., :-1] + north_flux[..., 1:, :] - north_flux[..., :-1, :]
    wet_inner = wet_win(0, row_count, 0, col_count)
    tracers_new = (tracer_win(0, row_count, 0, col_count) + time_step * tendency) * wet_inner

    upper = tracer_win(0, row_count + 1, 0, col_count + 1)
    density = haline_contraction * upper[1] - thermal_expansion * upper[0]
    pressure = thickness * jnp.cumsum(density, axis=0)
    grad_x = pressure[:, :row_count, 1:] - pressure[:, :row_count, :col_count]
    grad_y = pressure[:, 1:, :col_count] - pressure[:, :row_count, :col_count]

    row_index = (row_start + lax.iota(jnp.int32, row_count)).astype(jnp.float32)[:, None]
    coriolis_u = coriolis_base * (0.5 + (row_index + 0.5) / rows_total)
    coriolis_v = coriolis_base * (0.5 + (row_index + 1.0) / rows_total)
    surface_level = (level_ids == 0).astype(jnp.float32)
    east_inner = east_face[..., 1:]
    north_inner = north_face[..., 1:, :]
    old_u = zonal_win(0, row_count, 0, col_count)
    old_v = merid_win(0, row_count, 0, col_count)
    v_at_u = 0.25 * (old_v + merid_win(0, row_count, 1, col_count + 1)
                     + merid_win(-1, row_count - 1, 0, col_count) + merid_win(-1, row_count - 1, 1, col_count + 1))
    u_at_v = 0.25 * (old_u + zonal_win(1, row_count + 1, 0, col_count)
                     + zonal_win(0, row_count, -1, col_count - 1) + zonal_win(1, row_count + 1, -1, col_count - 1))
    smooth_u = (zonal_win(0, row_count, 1, col_count + 1) + zonal_win(0, row_count, -1, col_count - 1)
                + zonal_win(1, row_count + 1, 0, col_count) + zonal_win(-1, row_count - 1, 0, col_count) - 4.0 * old_u)
    smooth_v = (merid_win(0, row_count, 1, col_count + 1) + merid_win(0, row_count, -1, col_count - 1)
                + merid_win(1, row_count + 1, 0, col_count) + merid_win(-1, row_count - 1, 0, col_count) - 4.0 * old_v)
    tend_u = east_inner * (coriolis_u * v_at_u - grad_x + viscosity * smooth_u + surface_level * wind[0])
    tend_v = north_inner * (-coriolis_v * u_at_v - grad_y + viscosity * smooth_v + surface_level * wind[1])
    star_u = old_u + time_step * tend_u
    star_v = old_v + time_step * tend_v
    column_u = jnp.maximum(thickness * jnp.sum(east_inner, axis=0), thickness)
    column_v = jnp.maximum(thickness * jnp.sum(north_inner, axis=0), thickness)

    def column_mean(values, column):
        return thickness * jnp.sum(values, axis=0) / column

    means = (column_mean(old_u, column_u), column_mean(old_v, column_v),
             column_mean(tend_u, column_u), column_mean(tend_v, column_v),
             column_mean(star_u, column_u), column_mean(star_v, column_v))
    return tracers_new, star_u, star_v, east_inner, north_inner, means


def substep(height, zonal_flow, merid_flow, force_u, force_v, depth_u, depth_v, coriolis_u, coriolis_v, neighbour):
    sub_step = time_step / SUBSTEPS
    flux_u = depth_u * zonal_flow
    flux_v = depth_v * merid_flow
    height = height - sub_step * surface_scale * (flux_u - neighbour(flux_u, 0, -1) + flux_v - neighbour(flux_v, -1, 0))
    open_u = (depth_u > 0.0).astype(jnp.float32)
    open_v = (depth_v > 0.0).astype(jnp.float32)
    v_at_u = 0.25 * (merid_flow + neighbour(merid_flow, 0, 1) + neighbour(merid_flow, -1, 0) + neighbour(merid_flow, -1, 1))
    u_at_v = 0.25 * (zonal_flow + neighbour(zonal_flow, 1, 0) + neighbour(zonal_flow, 0, -1) + neighbour(zonal_flow, 1, -1))
    new_u = open_u * (zonal_flow + sub_step * (coriolis_u * v_at_u - gravity * (neighbour(height, 0, 1) - height) + force_u))
    new_v = open_v * (merid_flow + sub_step * (-coriolis_v * u_at_v - gravity * (neighbour(height, 1, 0) - height) + force_v))
    return height, new_u, new_v


def ref_move(values, row_shift, col_shift):
    rolled = jnp.roll(values, -col_shift, axis=-1)
    padded = jnp.pad(rolled, ((1, 1), (0, 0)))
    return padded[1 + row_shift: 1 + row_shift + values.shape[0], :]


def wrap_pad(values, width):
    pad_spec = [(0, 0)] * (values.ndim - 2) + [(width, width), (0, 0)]
    lat_pad = jnp.pad(values, pad_spec)
    return jnp.concatenate([lat_pad[..., -width:], lat_pad, lat_pad[..., :width]], axis=-1)


def reference(tracers, velocity, surface, wind, bottom):
    rows_total = NLAT
    tracers_new, star_u, star_v, east_inner, north_inner, means = baroclinic(
        wrap_pad(tracers, 3), wrap_pad(velocity, 1), wrap_pad(bottom, 3), 0, rows_total, wind)
    start_u, start_v, force_u, force_v, mean_u, mean_v = means
    thickness = 1.0 / LEVELS
    depth_u = thickness * jnp.minimum(bottom, ref_move(bottom, 0, 1)).astype(jnp.float32)
    depth_v = thickness * jnp.minimum(bottom, ref_move(bottom, 1, 0)).astype(jnp.float32)
    row_index = lax.iota(jnp.int32, rows_total).astype(jnp.float32)[:, None]
    coriolis_u = coriolis_base * (0.5 + (row_index + 0.5) / rows_total)
    coriolis_v = coriolis_base * (0.5 + (row_index + 1.0) / rows_total)
    height, flow_u, flow_v = surface, start_u, start_v
    running_u = jnp.zeros_like(start_u)
    running_v = jnp.zeros_like(start_v)
    for turn_index in range(SUBSTEPS):
        height, flow_u, flow_v = substep(height, flow_u, flow_v, force_u, force_v, depth_u, depth_v,
                                         coriolis_u, coriolis_v, ref_move)
        running_u = running_u + flow_u
        running_v = running_v + flow_v
    average_u = running_u / SUBSTEPS
    average_v = running_v / SUBSTEPS
    velocity_new = jnp.stack([east_inner * (star_u - mean_u + average_u),
                              north_inner * (star_v - mean_v + average_v)])
    streamfunction = -jnp.cumsum(depth_u * average_u, axis=0)
    return tracers_new, velocity_new, height, streamfunction
```

```python
import jax
import jax.numpy as jnp
from jax import lax
from jax.experimental import pallas as pl
from jax.experimental.pallas import tpu as pltpu
from jax.sharding import PartitionSpec as P

TRACERS = 4
LEVELS = 8
SUBSTEPS = 30
ROWS = 16
COLS = 128
MEMBERS = 16
HALO = 32
SLAB = 72
NLAT = ROWS * MEMBERS

time_step = 0.2
tracer_diffusion = 0.2
viscosity = 0.2
thermal_expansion = 2.0
haline_contraction = 1.5
coriolis_base = 1.0
gravity = 140.0
surface_scale = 40.0
thickness = 1.0 / LEVELS
f32 = jnp.float32

PRESSURE, EAST, NORTH, WIND, SURFACE, BOTTOM = 0, 8, 16, 24, 26, 27
PLANES = 28
MAIL_N, MAIL_S, EDGE, CHUNK = SLAB, SLAB + 8, SLAB + 16, SLAB + 24
BACK = 24


def at(values, step, axis):
    size = values.shape[axis]
    step %= size
    return values if step == 0 else pltpu.roll(values, size - step, axis)


def ids(shape, axis):
    return lax.broadcasted_iota(jnp.int32, shape, axis)


def wide(own, beside):
    return jnp.concatenate([own, beside], axis=1)


def tracer_planes(tracers_ref, bottom):
    return [
        [jnp.where(bottom > k, tracers_ref[t, k], 0.0) for k in range(LEVELS)]
        for t in range(TRACERS)
    ]


def pressures(salt, heat):
    total, out = None, []
    for k in range(LEVELS):
        density = haline_contraction * salt[k] - thermal_expansion * heat[k]
        total = density if total is None else total + density
        out.append(thickness * total)
    return out


def pack_kernel(tracers_ref, velocity_ref, surface_ref, wind_ref, bottom_ref, right_ref, left_ref):
    bottom = bottom_ref[...]
    c = tracer_planes(tracers_ref, bottom)
    planes = pressures(c[1], c[0])
    planes += [velocity_ref[d, k] for d in range(2) for k in range(LEVELS)]
    planes += [wind_ref[0], wind_ref[1], surface_ref[...], bottom.astype(f32)]
    lane = ids((ROWS, COLS), 1)
    for q in range(PLANES // 4):
        right = left = jnp.zeros((ROWS, COLS), f32)
        for s in range(4):
            moved = at(planes[4 * q + s], -32 * s, 1)
            right = jnp.where(lane // 32 == (s + 3) % 4, moved, right)
            left = jnp.where(lane // 32 == s, moved, left)
        right_ref[q] = right
        left_ref[q] = left
    right = left = jnp.zeros((ROWS, COLS), f32)
    for n in range(TRACERS * LEVELS):
        moved = at(c[n // LEVELS][n % LEVELS], -4 * n, 1)
        right = jnp.where(lane // 4 == (n + 31) % 32, moved, right)
        left = jnp.where(lane // 4 == n, moved, left)
    right_ref[PLANES // 4] = right
    left_ref[PLANES // 4] = left


def beside_plane(west_ref, east_ref, plane):
    q, s = divmod(plane, 4)
    block = ids((ROWS, COLS), 1) // 32
    both = jnp.where(
        block == s, east_ref[q], jnp.where(block == (s + 3) % 4, west_ref[q], 0.0)
    )
    return at(both, 32 * s, 1)


def beside_tracer(west_ref, east_ref, n):
    block = ids((ROWS, COLS), 1) // 4
    last = PLANES // 4
    both = jnp.where(
        block == n, east_ref[last], jnp.where(block == (n + 31) % 32, west_ref[last], 0.0)
    )
    return at(both, 4 * n, 1)


def momentum(k, u, v, p, wind, east, north, f_u, f_v, up, down):
    pair_v = v + down(v)
    pair_u = u + at(u, -1, 1)
    tend_u = (
        (0.25 * f_u) * (pair_v + at(pair_v, 1, 1))
        - (at(p, 1, 1) - p)
        + viscosity * (at(u, 1, 1) + at(u, -1, 1) + up(u) + down(u) - 4.0 * u)
    )
    tend_v = (
        (-0.25 * f_v) * (pair_u + up(pair_u))
        - (up(p) - p)
        + viscosity * (at(v, 1, 1) + at(v, -1, 1) + up(v) + down(v) - 4.0 * v)
    )
    if k == 0:
        tend_u = tend_u + wind[0]
        tend_v = tend_v + wind[1]
    return jnp.where(east, tend_u, 0.0), jnp.where(north, tend_v, 0.0)


def coriolis(rows, offset):
    return coriolis_base * (0.5 + (rows.astype(f32) + offset) / NLAT)


def send_kernel(
    place_ref, tracers_ref, velocity_ref, surface_ref, wind_ref, bottom_ref, west_ref, east_ref,
    out_ref, stack_ref, edge_ref, turned_ref,
):
    place = place_ref[0]
    bottom_own = bottom_ref[...]
    c = tracer_planes(tracers_ref, bottom_own)
    p_own = pressures(c[1], c[0])

    def whole(own, plane):
        return wide(own, beside_plane(west_ref, east_ref, plane))

    shape = (ROWS, 2 * COLS)
    row = ids(shape, 0)
    bottom = whole(bottom_own.astype(f32), BOTTOM)
    wind = [whole(wind_ref[d], WIND + d) for d in range(2)]

    def up(x):
        return jnp.where(row == ROWS - 1, 0.0, at(x, 1, 0))

    def down(x):
        return jnp.where(row == 0, 0.0, at(x, -1, 0))

    count_u = jnp.minimum(bottom, at(bottom, 1, 1))
    count_v = jnp.minimum(bottom, up(bottom))
    f_u = coriolis(place * ROWS + row, 0.5)
    f_v = coriolis(place * ROWS + row, 1.0)
    sums = [jnp.zeros(shape, f32) for _ in range(4)]
    us, vs, raws = [], [], []
    for k in range(LEVELS):
        east, north = count_u > k, count_v > k
        u = jnp.where(east, whole(velocity_ref[0, k], EAST + k), 0.0)
        raw = jnp.where(bottom > k, whole(velocity_ref[1, k], NORTH + k), 0.0)
        v = jnp.where(north, raw, 0.0)
        p = whole(p_own[k], PRESSURE + k)
        tend_u, tend_v = momentum(k, u, v, p, wind, east, north, f_u, f_v, up, down)
        sums = [a + b for a, b in zip(sums, (u, v, tend_u, tend_v))]
        us.append(u)
        vs.append(v)
        raws.append(raw)
        pair = u + at(u, -1, 1)
        last = p[8:] + (-0.25 * f_v[8:]) * pair[8:] + viscosity * at(v, -1, 0)[8:]
        if k == 0:
            last = last + wind[1][8:]
        first = (-0.25 * (f_v[:8] - 1.0 / NLAT)) * pair[:8] - p[:8] + viscosity * v[:8]
        edge_ref[k : k + 1] = u[15:16]
        edge_ref[8 + k : 9 + k] = raw[15:16]
        edge_ref[16 + k : 17 + k] = last[7:8]
        edge_ref[24 + k : 25 + k] = u[0:1]
        edge_ref[32 + k : 33 + k] = first[0:1]
    surface = whole(surface_ref[...], SURFACE)
    blocks = [surface, *sums, bottom, edge_ref[0:16], edge_ref[16:32]]
    for n, block in enumerate(blocks):
        spot = pl.multiple_of(lax.rem(n + place, 8) * ROWS, ROWS)
        stack_ref[pl.ds(spot, ROWS)] = block
    turned_ref[HALO : HALO + COLS] = stack_ref[:, :COLS].T
    beyond = stack_ref[:, COLS:].T
    turned_ref[:HALO] = beyond[COLS - HALO :]
    turned_ref[HALO + COLS :] = beyond[:HALO]
    edge = edge_ref[32:40]
    for d in range(MEMBERS):
        out_ref[d, :SLAB] = turned_ref[8 * d : 8 * d + SLAB]
        out_ref[d, EDGE:CHUNK] = at(edge, 8 * d - HALO, 1)[:, :COLS]

    sub = ids((8, COLS), 0)

    def spare(n):
        t, k = divmod(n, LEVELS)
        if t == 0:
            return us[k][:, :COLS], us[k][:, :COLS]
        if t == 1:
            return raws[k][:, :COLS], vs[k][:, :COLS]
        if t == 2:
            return raws[k][:, COLS:], us[k][:, COLS:]
        if k < 2:
            own = bottom[:, COLS * k : COLS * (k + 1)]
            return own, own
        return None

    def tops(n):
        own = c[n // LEVELS][n % LEVELS][8:]
        more = spare(n)
        return own if more is None else jnp.where(sub == 4, at(more[0][8:], 3, 0), own)

    def bottoms(n):
        own = c[n // LEVELS][n % LEVELS][:8]
        more = spare(n)
        return own if more is None else jnp.where(sub == 3, at(more[1][:8], -3, 0), own)

    for m in range(MEMBERS):
        out_ref[m, MAIL_N:MAIL_S] = jnp.where(sub >= 4, tops(2 * m), at(tops(2 * m + 1), 4, 0))
        out_ref[m, MAIL_S:EDGE] = jnp.where(sub < 4, bottoms(2 * m), at(bottoms(2 * m + 1), 4, 0))


def slab_kernel(in_ref, out_ref, edge_ref):
    shape = (SLAB, 2 * COLS)
    block = ids((SLAB, COLS), 1) // ROWS

    def plane(n):
        halves = []
        for h in range(2):
            half = in_ref[8 * h, :SLAB]
            for a in range(1, 8):
                half = jnp.where(block == (n + a) % 8, in_ref[8 * h + a, :SLAB], half)
            halves.append(at(half, 16 * n, 1))
        return jnp.concatenate(halves, axis=1)

    surface, start_u, start_v, force_u, force_v, bottom, first, second = map(plane, range(8))
    zeros = jnp.zeros((8, COLS), f32)
    for a in range(MEMBERS):
        edge_ref[ROWS * a : ROWS * a + 8] = in_ref[a + 1, EDGE:CHUNK] if a < MEMBERS - 1 else zeros
        edge_ref[ROWS * a + 8 : ROWS * a + 16] = zeros
    third = jnp.concatenate([edge_ref[:COLS].T[:SLAB], edge_ref[COLS:].T[:SLAB]], axis=1)

    lane = ids(shape, 1)
    r = lane % ROWS
    count_u = jnp.minimum(bottom, at(bottom, 1, 0))
    count_v = jnp.where(lane == NLAT - 1, 0.0, jnp.minimum(bottom, at(bottom, 1, 1)))

    def levels_of(values, row):
        one = at(jnp.where(r == row % ROWS, values, 0.0), row - 7, 1)
        for step in (1, 2, 4):
            one = one + at(one, step, 1)
        return one

    def summed(values, row):
        one = jnp.where(r < 8, values, 0.0)
        for step in (1, 2, 4):
            one = one + at(one, -step, 1)
        one = at(one, 7 - row, 1)
        return jnp.where(r == row % ROWS, one, 0.0)

    level = r.astype(f32)
    count_ua = levels_of(count_u, 15)
    count_ub = levels_of(count_u, 16)
    count_va = levels_of(count_v, 15)
    count_vb = levels_of(count_v, 16)
    count_vc = levels_of(count_v, 14)
    top = lane >= NLAT - ROWS
    v_a = jnp.where(count_va > level, at(first, 8, 1), 0.0)
    u_a = jnp.where(top, 0.0, first)
    u_b = jnp.where(top, 0.0, at(second, 24, 1))
    f_a = 0.25 * coriolis(lane - r + 15, 0.5)
    f_b = f_a + 0.25 * coriolis_base / NLAT
    pair = v_a + at(v_a, 1, 0)
    force_u = (
        force_u
        + summed(jnp.where(count_ua > level, f_a * pair + viscosity * u_b, 0.0), 15)
        + summed(jnp.where(count_ub > level, f_b * pair + viscosity * u_a, 0.0), 16)
    )
    spread = viscosity * (at(v_a, 1, 0) + at(v_a, -1, 0) - 4.0 * v_a)
    force_v = (
        force_v
        + summed(jnp.where(count_vc > level, viscosity * v_a, 0.0), 14)
        + summed(jnp.where(count_va > level, second + third + spread, 0.0), 15)
        + summed(jnp.where(count_vb > level, viscosity * v_a, 0.0), 16)
    )
    start_v = start_v + summed(v_a, 15)

    sub_step = time_step / SUBSTEPS
    per_u = 1.0 / jnp.maximum(count_u, 1.0)
    per_v = 1.0 / jnp.maximum(count_v, 1.0)
    open_u = jnp.where(count_u > 0.0, sub_step, 0.0)
    open_v = jnp.where(count_v > 0.0, sub_step, 0.0)
    flux_u = (sub_step * surface_scale * thickness) * count_u
    flux_v = (sub_step * surface_scale * thickness) * count_v
    held = (
        flux_u,
        at(flux_u, -1, 0),
        flux_v,
        at(flux_v, -1, 1),
        (0.25 * open_u) * coriolis(lane, 0.5),
        gravity * open_u,
        open_u * (force_u * per_u),
        (-0.25 * open_v) * coriolis(lane, 1.0),
        gravity * open_v,
        open_v * (force_v * per_v),
    )
    state = (surface, start_u * per_u, start_v * per_v)
    total_u = total_v = jnp.zeros((8, 2 * COLS), f32)
    low = 0
    for low, steps in ((0, 6), (8, 8), (16, 8), (24, 8)):
        high = SLAB - low
        cut = 8 if low else 0
        state = tuple(x[cut : x.shape[0] - cut] for x in state)
        du, du_w, dv, dv_s, cu, gu, fu, cv, gv, fv = (x[low:high] for x in held)
        centre = HALO - low

        def advance(_, carry):
            height, u, v, sum_u, sum_v = carry
            u_w = at(u, -1, 0)
            v_s = at(v, -1, 1)
            height = height - ((du * u - du_w * u_w) + (dv * v - dv_s * v_s))
            pair_v = v + v_s
            pair_u = u + u_w
            u_new = u + (cu * (pair_v + at(pair_v, 1, 0)) - gu * (at(height, 1, 0) - height) + fu)
            v_new = v + (cv * (pair_u + at(pair_u, 1, 1)) - gv * (at(height, 1, 1) - height) + fv)
            sum_u = sum_u + u_new[centre : centre + 8]
            sum_v = sum_v + v_new[centre : centre + 8]
            return height, u_new, v_new, sum_u, sum_v

        *state, total_u, total_v = lax.fori_loop(0, steps, advance, (*state, total_u, total_v))
    height = state[0][8:16]
    average_u = total_u * (1.0 / SUBSTEPS)
    average_v = total_v * (1.0 / SUBSTEPS)
    stream = (-thickness * count_u[HALO : HALO + 8]) * average_u
    lane_own = ids((8, 2 * COLS), 1)
    step = 1
    while step < NLAT:
        stream = stream + jnp.where(lane_own >= step, at(stream, -step, 1), 0.0)
        step *= 2
    block_own = ids((8, COLS), 1) // ROWS
    results = (height, stream, average_u, average_v)
    for e in range(MEMBERS):
        half = COLS * (e // 8)
        packed = zeros
        for n, values in enumerate(results):
            moved = at(values[:, half : half + COLS], -ROWS * n, 1)
            packed = jnp.where(block_own == (e + n) % 8, moved, packed)
        out_ref[e, 0:8] = packed
        out_ref[e, 8:16] = in_ref[(e + 15) % MEMBERS, MAIL_N:MAIL_S]
        out_ref[e, 16:24] = in_ref[(e + 1) % MEMBERS, MAIL_S:EDGE]


def finish_kernel(
    place_ref, in_ref, tracers_ref, velocity_ref, wind_ref, bottom_ref, west_ref, east_ref,
    tracers_out, velocity_out, height_out, stream_out, turned_ref,
):
    place = place_ref[0]
    turned_ref[...] = in_ref[:, 0:8].reshape(COLS, COLS).T

    def result(n):
        spot = pl.multiple_of(lax.rem(n + place, 8) * ROWS, ROWS)
        return turned_ref[pl.ds(spot, ROWS)]

    height_out[...] = result(0)
    stream_out[...] = result(1)
    average_u, average_v = result(2), result(3)

    sub = ids((8, COLS), 0)
    tall = (ROWS + 8, 2 * COLS)
    row = ids(tall, 0)
    first, last = place == 0, place == MEMBERS - 1

    def lat_tile(n):
        south = jnp.where(first, 0.0, in_ref[n // 2, 8:16])
        north = jnp.where(last, 0.0, in_ref[n // 2, 16:24])
        if n % 2 == 0:
            return jnp.where(sub < 4, north, south)
        return at(jnp.where(sub < 4, south, north), 4, 0)

    def spare_north(tile):
        return jnp.where(sub == 0, at(tile, 3, 0), 0.0)

    def spare_south(tile):
        return jnp.where(sub == 7, at(tile, -3, 0), 0.0)

    def tallen(own, tile):
        return jnp.concatenate([own, tile], axis=0)

    def whole(own, plane):
        return wide(own, beside_plane(west_ref, east_ref, plane))

    tiles = [[lat_tile(LEVELS * t + k) for k in range(LEVELS)] for t in range(TRACERS)]
    bottom_own = bottom_ref[...]
    c = tracer_planes(tracers_ref, bottom_own)
    p_own = pressures(c[1], c[0])
    p_tile = pressures(tiles[1], tiles[0])
    both = wide(
        spare_north(tiles[3][0]) + spare_south(tiles[3][0]),
        spare_north(tiles[3][1]) + spare_south(tiles[3][1]),
    )
    bottom = tallen(whole(bottom_own.astype(f32), BOTTOM), both)
    count_u = jnp.minimum(bottom, at(bottom, 1, 1))
    count_v = jnp.minimum(bottom, at(bottom, 1, 0))
    f_u = coriolis(place * ROWS + row, 0.5)
    f_v = coriolis(place * ROWS + row, 1.0)
    none = jnp.zeros((8, COLS), f32)
    wind = [tallen(wide(wind_ref[d], jnp.zeros((ROWS, COLS), f32)), jnp.zeros((8, 2 * COLS), f32)) for d in range(2)]

    def up(x):
        return at(x, 1, 0)

    def down(x):
        return at(x, -1, 0)

    stars_u, stars_v = [], []
    own_u, own_v = count_u[:ROWS, :COLS], count_v[:ROWS, :COLS]
    mean_u = mean_v = jnp.zeros((ROWS, COLS), f32)
    for k in range(LEVELS):
        east, north = count_u > k, count_v > k
        t0, t1, t2 = tiles[0][k], tiles[1][k], tiles[2][k]
        u_lat = wide(spare_north(t0) + spare_south(t0), spare_north(t2))
        v_lat = wide(spare_north(t1) + spare_south(t1), spare_south(t2))
        u = tallen(whole(velocity_ref[0, k], EAST + k), u_lat)
        u = jnp.where(east | (row >= ROWS), u, 0.0)
        v = tallen(whole(velocity_ref[1, k], NORTH + k), v_lat)
        v = jnp.where(north | (row == ROWS), v, 0.0)
        p = tallen(whole(p_own[k], PRESSURE + k), wide(p_tile[k], none))
        tend_u, tend_v = momentum(k, u, v, p, wind, east, north, f_u, f_v, up, down)
        star_u = (u + time_step * tend_u)[:ROWS, :COLS]
        star_v = (v + time_step * tend_v)[:ROWS, :COLS]
        stars_u.append(star_u)
        stars_v.append(star_v)
        mean_u = mean_u + star_u
        mean_v = mean_v + star_v

        u_own, v_own = u[:ROWS], v[:, :COLS]
        diff_e = jnp.where(east[:ROWS], tracer_diffusion, 0.0)
        diff_n = jnp.where(north[:, :COLS], tracer_diffusion, 0.0)
        for t in range(TRACERS):
            ce = wide(c[t][k], beside_tracer(west_ref, east_ref, LEVELS * t + k))
            cn = tallen(c[t][k], tiles[t][k])
            change = None
            for values, axis, flow, diffusion in ((ce, 1, u_own, diff_e), (cn, 0, v_own, diff_n)):
                ahead = at(values, 1, axis)
                face = (
                    37.0 * (values + ahead)
                    - 8.0 * (at(values, -1, axis) + at(values, 2, axis))
                    + (at(values, -2, axis) + at(values, 3, axis))
                ) * (1.0 / 60.0)
                flux = diffusion * (ahead - values) - flow * face
                gain = (flux - at(flux, -1, axis))[:ROWS, :COLS]
                change = gain if change is None else change + gain
            tracers_out[t, k] = jnp.where(bottom_own > k, c[t][k] + time_step * change, 0.0)
    shift_u = average_u - mean_u / jnp.maximum(own_u, 1.0)
    shift_v = average_v - mean_v / jnp.maximum(own_v, 1.0)
    for k in range(LEVELS):
        velocity_out[0, k] = jnp.where(own_u > k, stars_u[k] + shift_u, 0.0)
        velocity_out[1, k] = jnp.where(own_v > k, stars_v[k] + shift_v, 0.0)


def ring(axis, step):
    count = lax.axis_size(axis)
    return [(i, (i + step) % count) for i in range(count)]


def struct(*shape):
    return jax.ShapeDtypeStruct(shape, f32)


def vmem(*shape):
    return pltpu.VMEM(shape, f32)


def specs(count, scalars=0):
    return [pl.BlockSpec(memory_space=pltpu.SMEM)] * scalars + [
        pl.BlockSpec(memory_space=pltpu.VMEM)
    ] * count


PARAMS = pltpu.CompilerParams(vmem_limit_bytes=32 * 1024 * 1024)


def shards(tracers, velocity, surface, wind, bottom):
    place = lax.axis_index("lat").astype(jnp.int32).reshape(1)
    payload = struct(PLANES // 4 + 1, ROWS, COLS)
    to_right, to_left = pl.pallas_call(
        pack_kernel,
        out_shape=(payload, payload),
        in_specs=specs(5),
        out_specs=tuple(specs(2)),
        compiler_params=PARAMS,
        name="pack",
    )(tracers, velocity, surface, wind, bottom)
    west = lax.ppermute(to_right, "lon", ring("lon", 1))
    east = lax.ppermute(to_left, "lon", ring("lon", -1))
    chunks = pl.pallas_call(
        send_kernel,
        out_shape=struct(MEMBERS, CHUNK, COLS),
        in_specs=specs(7, 1),
        out_specs=specs(1)[0],
        scratch_shapes=[vmem(8 * ROWS, 2 * COLS), vmem(40, 2 * COLS), vmem(COLS + 2 * HALO, COLS)],
        compiler_params=PARAMS,
        name="columns",
    )(place, tracers, velocity, surface, wind, bottom, west, east)
    slabs = lax.all_to_all(chunks, "lat", 0, 0, tiled=True)
    answers = pl.pallas_call(
        slab_kernel,
        out_shape=struct(MEMBERS, BACK, COLS),
        in_specs=specs(1),
        out_specs=specs(1)[0],
        scratch_shapes=[vmem(2 * COLS, COLS)],
        compiler_params=PARAMS,
        name="substeps",
    )(slabs)
    home = lax.all_to_all(answers, "lat", 0, 0, tiled=True)
    return pl.pallas_call(
        finish_kernel,
        out_shape=(
            struct(TRACERS, LEVELS, ROWS, COLS),
            struct(2, LEVELS, ROWS, COLS),
            struct(ROWS, COLS),
            struct(ROWS, COLS),
        ),
        in_specs=specs(7, 1),
        out_specs=tuple(specs(4)),
        scratch_shapes=[vmem(COLS, COLS)],
        compiler_params=PARAMS,
        name="finish",
    )(place, home, tracers, velocity, wind, bottom, west, east)


def solution(mesh):
    placed = (
        P(None, None, "lat", "lon"),
        P(None, None, "lat", "lon"),
        P("lat", "lon"),
        P(None, "lat", "lon"),
        P("lat", "lon"),
    )
    return jax.shard_map(
        shards,
        mesh=mesh,
        in_specs=placed,
        out_specs=(
            P(None, None, "lat", "lon"),
            P(None, None, "lat", "lon"),
            P("lat", "lon"),
            P("lat", "lon"),
        ),
        check_vma=False,
    )
```

```python
import jax
import jax.numpy as jnp
from jax import lax
from jax.experimental import pallas as pl
from jax.experimental.pallas import tpu as pltpu
from jax.sharding import PartitionSpec as P

TRACERS = 4
LEVELS = 8
SUBSTEPS = 30
ROWS = 16
COLS = 128
MEMBERS = 16
HALO = 32
SLAB = 72
NLAT = ROWS * MEMBERS

time_step = 0.2
tracer_diffusion = 0.2
viscosity = 0.2
thermal_expansion = 2.0
haline_contraction = 1.5
coriolis_base = 1.0
gravity = 140.0
surface_scale = 40.0
thickness = 1.0 / LEVELS
f32 = jnp.float32

PRESSURE, EAST, NORTH, WIND, SURFACE, BOTTOM = 0, 8, 16, 24, 26, 27
PLANES = 28
OWN_EAST, OWN_NORTH, OWN_SURFACE, OWN_WIND, OWN_BOTTOM, OWN = 32, 40, 48, 49, 51, 52
MAIL_N, MAIL_S, EDGE, CHUNK = SLAB, SLAB + 8, SLAB + 16, SLAB + 24
BACK = 24


def at(values, step, axis):
    size = values.shape[axis]
    step %= size
    return values if step == 0 else pltpu.roll(values, size - step, axis)


def ids(shape, axis):
    return lax.broadcasted_iota(jnp.int32, shape, axis)


def wide(own, beside):
    return jnp.concatenate([own, beside], axis=1)


def tracer_planes(own_ref):
    bottom = own_ref[OWN_BOTTOM]
    return [
        [jnp.where(bottom > k, own_ref[LEVELS * t + k], 0.0) for k in range(LEVELS)]
        for t in range(TRACERS)
    ]


def pressures(salt, heat):
    total, out = None, []
    for k in range(LEVELS):
        density = haline_contraction * salt[k] - thermal_expansion * heat[k]
        total = density if total is None else total + density
        out.append(thickness * total)
    return out


def pack_kernel(own_ref, right_ref, left_ref):
    c = tracer_planes(own_ref)
    planes = pressures(c[1], c[0])
    planes += [own_ref[n] for n in range(OWN_EAST, OWN_SURFACE)]
    planes += [own_ref[n] for n in (OWN_WIND, OWN_WIND + 1, OWN_SURFACE, OWN_BOTTOM)]
    lane = ids((ROWS, COLS), 1)
    for q in range(PLANES // 4):
        right = left = jnp.zeros((ROWS, COLS), f32)
        for s in range(4):
            moved = at(planes[4 * q + s], -32 * s, 1)
            right = jnp.where(lane // 32 == (s + 3) % 4, moved, right)
            left = jnp.where(lane // 32 == s, moved, left)
        right_ref[q] = right
        left_ref[q] = left
    right = left = jnp.zeros((ROWS, COLS), f32)
    for n in range(TRACERS * LEVELS):
        moved = at(c[n // LEVELS][n % LEVELS], -4 * n, 1)
        right = jnp.where(lane // 4 == (n + 31) % 32, moved, right)
        left = jnp.where(lane // 4 == n, moved, left)
    right_ref[PLANES // 4] = right
    left_ref[PLANES // 4] = left


def beside_plane(west_ref, east_ref, plane):
    q, s = divmod(plane, 4)
    block = ids((ROWS, COLS), 1) // 32
    both = jnp.where(
        block == s, east_ref[q], jnp.where(block == (s + 3) % 4, west_ref[q], 0.0)
    )
    return at(both, 32 * s, 1)


def beside_tracer(west_ref, east_ref, n):
    block = ids((ROWS, COLS), 1) // 4
    last = PLANES // 4
    both = jnp.where(
        block == n, east_ref[last], jnp.where(block == (n + 31) % 32, west_ref[last], 0.0)
    )
    return at(both, 4 * n, 1)


def momentum(k, u, v, p, wind, east, north, f_u, f_v, up, down):
    pair_v = v + down(v)
    pair_u = u + at(u, -1, 1)
    tend_u = (
        (0.25 * f_u) * (pair_v + at(pair_v, 1, 1))
        - (at(p, 1, 1) - p)
        + viscosity * (at(u, 1, 1) + at(u, -1, 1) + up(u) + down(u) - 4.0 * u)
    )
    tend_v = (
        (-0.25 * f_v) * (pair_u + up(pair_u))
        - (up(p) - p)
        + viscosity * (at(v, 1, 1) + at(v, -1, 1) + up(v) + down(v) - 4.0 * v)
    )
    if k == 0:
        tend_u = tend_u + wind[0]
        tend_v = tend_v + wind[1]
    return jnp.where(east, tend_u, 0.0), jnp.where(north, tend_v, 0.0)


def coriolis(rows, offset):
    return coriolis_base * (0.5 + (rows.astype(f32) + offset) / NLAT)


def send_kernel(
    place_ref, own_ref, west_ref, east_ref,
    out_ref, split_ref, stack_ref, edge_ref, turned_ref,
):
    place = place_ref[0]
    c = tracer_planes(own_ref)
    p_own = pressures(c[1], c[0])

    def whole(own, plane):
        return wide(own, beside_plane(west_ref, east_ref, plane))

    shape = (ROWS, 2 * COLS)
    row = ids(shape, 0)
    bottom = whole(own_ref[OWN_BOTTOM], BOTTOM)
    wind = [whole(own_ref[OWN_WIND + d], WIND + d) for d in range(2)]

    def up(x):
        return jnp.where(row == ROWS - 1, 0.0, at(x, 1, 0))

    def down(x):
        return jnp.where(row == 0, 0.0, at(x, -1, 0))

    count_u = jnp.minimum(bottom, at(bottom, 1, 1))
    count_v = jnp.minimum(bottom, up(bottom))
    f_u = coriolis(place * ROWS + row, 0.5)
    f_v = coriolis(place * ROWS + row, 1.0)
    sums = [jnp.zeros(shape, f32) for _ in range(4)]
    us, vs, raws = [], [], []
    for k in range(LEVELS):
        east, north = count_u > k, count_v > k
        u = jnp.where(east, whole(own_ref[OWN_EAST + k], EAST + k), 0.0)
        raw = jnp.where(bottom > k, whole(own_ref[OWN_NORTH + k], NORTH + k), 0.0)
        v = jnp.where(north, raw, 0.0)
        p = whole(p_own[k], PRESSURE + k)
        tend_u, tend_v = momentum(k, u, v, p, wind, east, north, f_u, f_v, up, down)
        sums = [a + b for a, b in zip(sums, (u, v, tend_u, tend_v))]
        us.append(u)
        vs.append(v)
        raws.append(raw)
        pair = u + at(u, -1, 1)
        last = p[8:] + (-0.25 * f_v[8:]) * pair[8:] + viscosity * at(v, -1, 0)[8:]
        if k == 0:
            last = last + wind[1][8:]
        first = (-0.25 * (f_v[:8] - 1.0 / NLAT)) * pair[:8] - p[:8] + viscosity * v[:8]
        edge_ref[k : k + 1] = u[15:16]
        edge_ref[8 + k : 9 + k] = raw[15:16]
        edge_ref[16 + k : 17 + k] = last[7:8]
        edge_ref[24 + k : 25 + k] = u[0:1]
        edge_ref[32 + k : 33 + k] = first[0:1]
    surface = whole(own_ref[OWN_SURFACE], SURFACE)
    for n, values in enumerate((surface, *sums, bottom)):
        split_ref[ROWS * n : ROWS * (n + 1)] = values[:, :COLS]
        split_ref[ROWS * (6 + n) : ROWS * (7 + n)] = values[:, COLS:]
    for q in range(16):
        spot = pl.multiple_of(lax.rem(q + place, 16) * 8, 8)
        for half in range(2):
            if q < 12:
                rows = split_ref[pl.ds(ROWS * (6 * half + q // 2) + q % 2, 8, 2), :]
            else:
                rows = edge_ref[8 * (q - 12) : 8 * (q - 11), COLS * half : COLS * (half + 1)]
            stack_ref[half, pl.ds(spot, 8)] = rows
    turned_ref[HALO : HALO + COLS] = stack_ref[0].T
    beyond = stack_ref[1].T
    turned_ref[:HALO] = beyond[COLS - HALO :]
    turned_ref[HALO + COLS :] = beyond[:HALO]
    edge = edge_ref[32:40]
    for d in range(MEMBERS):
        out_ref[d, :SLAB] = turned_ref[8 * d : 8 * d + SLAB]
        out_ref[d, EDGE:CHUNK] = at(edge, 8 * d - HALO, 1)[:, :COLS]

    sub = ids((8, COLS), 0)

    def spare(n):
        t, k = divmod(n, LEVELS)
        if t == 0:
            return us[k][:, :COLS], us[k][:, :COLS]
        if t == 1:
            return raws[k][:, :COLS], vs[k][:, :COLS]
        if t == 2:
            return raws[k][:, COLS:], us[k][:, COLS:]
        if k < 2:
            own = bottom[:, COLS * k : COLS * (k + 1)]
            return own, own
        return None

    def tops(n):
        own = c[n // LEVELS][n % LEVELS][8:]
        more = spare(n)
        return own if more is None else jnp.where(sub == 4, at(more[0][8:], 3, 0), own)

    def bottoms(n):
        own = c[n // LEVELS][n % LEVELS][:8]
        more = spare(n)
        return own if more is None else jnp.where(sub == 3, at(more[1][:8], -3, 0), own)

    for m in range(MEMBERS):
        out_ref[m, MAIL_N:MAIL_S] = jnp.where(sub >= 4, tops(2 * m), at(tops(2 * m + 1), 4, 0))
        out_ref[m, MAIL_S:EDGE] = jnp.where(sub < 4, bottoms(2 * m), at(bottoms(2 * m + 1), 4, 0))


def slab_kernel(in_ref, out_ref, edge_ref):
    shape = (SLAB, COLS)
    lane = ids(shape, 1)
    r = lane % 8
    block = ids((8, COLS), 1) // 8

    tiles = []
    for t in range(SLAB // 8):
        now = [in_ref[a, 8 * t : 8 * t + 8] for a in range(MEMBERS)]
        for bit in (1, 2, 4, 8):
            odd = (block & bit) > 0
            now = [jnp.where(odd, now[(a + bit) % MEMBERS], now[a]) for a in range(MEMBERS)]
        tiles.append([at(now[-q % MEMBERS], 8 * q, 1) for q in range(16)])
    blocks = [jnp.concatenate([tile[q] for tile in tiles], axis=0) for q in range(16)]
    surface, start_u, start_v, force_u, force_v, bottom = (blocks[2 * n : 2 * n + 2] for n in range(6))
    u_a, v_raw, near, u_next = blocks[12:]
    zeros = jnp.zeros((8, COLS), f32)
    for a in range(MEMBERS):
        edge_ref[8 * a : 8 * a + 8] = in_ref[a + 1, EDGE:CHUNK] if a < MEMBERS - 1 else zeros
    far = edge_ref[...].T[:SLAB]

    top = lane == COLS - 1
    count_u = [jnp.minimum(b, at(b, 1, 0)) for b in bottom]
    count_v = [
        jnp.minimum(*bottom),
        jnp.where(top, 0.0, jnp.minimum(bottom[1], at(bottom[0], 1, 1))),
    ]

    ahead = jnp.concatenate([count_u[0], count_v[0]], axis=0)
    first = (ids(ahead.shape, 1) % 8 == 0) & (ids(ahead.shape, 1) > 0)
    counts = jnp.concatenate(
        [
            jnp.where(r == 7, count_u[1], 0.0),
            jnp.where(r == 7, count_v[1], 0.0),
            jnp.where(r == 7, count_v[0], 0.0),
            at(jnp.where(first, ahead, 0.0), 1, 1),
        ],
        axis=0,
    )
    for step in (1, 2, 4):
        counts = counts + at(counts, step, 1)
    count_ua, count_va, count_vc, count_ub, count_vb = (
        counts[SLAB * n : SLAB * (n + 1)] for n in range(5)
    )
    level = r.astype(f32)
    last = lane >= COLS - 8
    v_a = jnp.where(count_va > level, v_raw, 0.0)
    u_a = jnp.where(last, 0.0, u_a)
    u_b = jnp.where(last, 0.0, at(u_next, 8, 1))
    f_a = 0.25 * coriolis(lane // 8 * ROWS + 15, 0.5)
    f_b = f_a + 0.25 * coriolis_base / NLAT
    pair = v_a + at(v_a, 1, 0)
    spread = viscosity * (at(v_a, 1, 0) + at(v_a, -1, 0) - 4.0 * v_a)
    terms = jnp.concatenate(
        [
            jnp.where(count_ua > level, f_a * pair + viscosity * u_b, 0.0),
            jnp.where(count_ub > level, f_b * pair + viscosity * u_a, 0.0),
            jnp.where(count_vb > level, viscosity * v_a, 0.0),
            jnp.where(count_vc > level, viscosity * v_a, 0.0),
            jnp.where(count_va > level, near + far + spread, 0.0),
            v_a,
        ],
        axis=0,
    )
    for step in (1, 2, 4):
        terms = terms + at(terms, -step, 1)
    shifted = at(terms[SLAB : 3 * SLAB], -1, 1)
    u_15, v_14, v_15, begin_15 = (
        jnp.where(r == 7, terms[SLAB * n : SLAB * (n + 1)], 0.0) for n in (0, 3, 4, 5)
    )
    u_16, v_16 = (jnp.where(r == 0, shifted[SLAB * n : SLAB * (n + 1)], 0.0) for n in range(2))
    force_u = [force_u[0] + u_16, force_u[1] + u_15]
    force_v = [force_v[0] + (v_14 + v_16), force_v[1] + v_15]
    start_v = [start_v[0], start_v[1] + begin_15]

    sub_step = time_step / SUBSTEPS
    held_u, held_v, flux_u, flux_v, begin_u, begin_v = [], [], [], [], [], []
    for i in range(2):
        per = 1.0 / jnp.maximum(count_u[i], 1.0)
        open_face = jnp.where(count_u[i] > 0.0, sub_step, 0.0)
        flux_u.append((sub_step * surface_scale * thickness) * count_u[i])
        held_u.append(
            (
                (0.25 * open_face) * coriolis(2 * lane + i, 0.5),
                gravity * open_face,
                open_face * (force_u[i] * per),
            )
        )
        begin_u.append(start_u[i] * per)
        per = 1.0 / jnp.maximum(count_v[i], 1.0)
        open_face = jnp.where(count_v[i] > 0.0, sub_step, 0.0)
        flux_v.append((sub_step * surface_scale * thickness) * count_v[i])
        held_v.append(
            (
                (-0.25 * open_face) * coriolis(2 * lane + i, 1.0),
                gravity * open_face,
                open_face * (force_v[i] * per),
            )
        )
        begin_v.append(start_v[i] * per)
    held = (
        *flux_u, at(flux_u[0], 1, 1), *flux_v, at(flux_v[0], 1, 1), at(flux_v[1], -1, 1),
        *held_u[0], *held_u[1], *held_v[0], *held_v[1],
    )
    state = (*surface, at(surface[0], 1, 1), *begin_u, *begin_v)
    total = (zeros,) * 4
    for low, steps in ((0, 6), (8, 8), (16, 8), (24, 8)):
        cut = 8 if low else 0
        state = tuple(x[cut : x.shape[0] - cut] for x in state)
        (
            du0, du1, du2, dv0, dv1, dv2, dv_, cu0, gu0, fu0, cu1, gu1, fu1,
            cv0, gv0, fv0, cv1, gv1, fv1,
        ) = (x[low : SLAB - low] for x in held)
        centre = HALO - low

        def advance(_, carry):
            h0, h1, h2, u0, u1, v0, v1, *sums = carry
            v_ = at(v1, -1, 1)
            u2 = at(u0, 1, 1)
            v2 = at(v0, 1, 1)
            x0, x1, x2 = du0 * u0, du1 * u1, du2 * u2
            y0, y1 = dv0 * v0, dv1 * v1
            h1 = h1 - ((x1 - at(x1, -1, 0)) + (y1 - y0))
            h0 = h0 - ((x0 - at(x0, -1, 0)) + (y0 - dv_ * v_))
            h2 = h2 - ((x2 - at(x2, -1, 0)) + (dv2 * v2 - y1))
            p0, p1, p2 = u0 + at(u0, -1, 0), u1 + at(u1, -1, 0), u2 + at(u2, -1, 0)
            q0, q1 = v0 + v_, v1 + v0
            u0 = (u0 + fu0) + (cu0 * (q0 + at(q0, 1, 0)) - gu0 * (at(h0, 1, 0) - h0))
            u1 = (u1 + fu1) + (cu1 * (q1 + at(q1, 1, 0)) - gu1 * (at(h1, 1, 0) - h1))
            v0 = (v0 + fv0) + (cv0 * (p0 + p1) - gv0 * (h1 - h0))
            v1 = (v1 + fv1) + (cv1 * (p1 + p2) - gv1 * (h2 - h1))
            sums = [a + b[centre : centre + 8] for a, b in zip(sums, (u0, u1, v0, v1))]
            return (h0, h1, h2, u0, u1, v0, v1, *sums)

        *state, a0, a1, a2, a3 = lax.fori_loop(0, steps, advance, (*state, *total))
        total = (a0, a1, a2, a3)
    height = [x[8:16] for x in state[:2]]
    average = [x * (1.0 / SUBSTEPS) for x in total]
    transport = [
        (-thickness * count_u[i][HALO : HALO + 8]) * average[i] for i in range(2)
    ]
    square = (COLS, COLS)
    before = (ids(square, 0) < ids(square, 1)).astype(f32)
    south = jnp.dot(
        transport[0] + transport[1],
        before,
        precision=lax.Precision.HIGHEST,
        preferred_element_type=f32,
    )
    stream = [south + transport[0], south + (transport[0] + transport[1])]
    results = [*height, *stream, *average]
    moved = [at(values, -8 * n, 1) for n, values in enumerate(results)]
    for e in range(MEMBERS):
        packed = moved[0]
        for n in range(1, 8):
            packed = jnp.where(block == (e + n) % 16, moved[n], packed)
        out_ref[e, 0:8] = packed
        out_ref[e, 8:16] = in_ref[(e + 15) % MEMBERS, MAIL_N:MAIL_S]
        out_ref[e, 16:24] = in_ref[(e + 1) % MEMBERS, MAIL_S:EDGE]


def gain(values, axis, flow, diffusion):
    ahead = at(values, 1, axis)
    sides = at(values, -1, axis) + at(values, 2, axis)
    far = at(values, -2, axis) + at(values, 3, axis)
    face = (37.0 * (values + ahead) - 8.0 * sides + far) * (1.0 / 60.0)
    flux = diffusion * (ahead - values) - flow * face
    return flux - at(flux, -1, axis)


def finish_kernel(
    place_ref, in_ref, own_ref, west_ref, east_ref,
    tracers_out, velocity_out, height_out, stream_out, turned_ref, rows_ref,
):
    place = place_ref[0]
    turned_ref[...] = in_ref[:, 0:8].reshape(COLS, COLS).T

    for q in range(8):
        spot = pl.multiple_of(lax.rem(q + place, 16) * 8, 8)
        rows_ref[pl.ds(ROWS * (q // 2) + q % 2, 8, 2), :] = turned_ref[pl.ds(spot, 8)]
    height_out[...] = rows_ref[:ROWS]
    stream_out[...] = rows_ref[ROWS : 2 * ROWS]
    average_u, average_v = rows_ref[2 * ROWS : 3 * ROWS], rows_ref[3 * ROWS :]

    sub = ids((8, COLS), 0)
    tall = (ROWS + 8, 2 * COLS)
    row = ids(tall, 0)
    first, last = place == 0, place == MEMBERS - 1

    def lat_tile(n):
        south = jnp.where(first, 0.0, in_ref[n // 2, 8:16])
        north = jnp.where(last, 0.0, in_ref[n // 2, 16:24])
        if n % 2 == 0:
            return jnp.where(sub < 4, north, south)
        return at(jnp.where(sub < 4, south, north), 4, 0)

    def spare_north(tile):
        return jnp.where(sub == 0, at(tile, 3, 0), 0.0)

    def spare_south(tile):
        return jnp.where(sub == 7, at(tile, -3, 0), 0.0)

    def tallen(own, tile):
        return jnp.concatenate([own, tile], axis=0)

    def whole(own, plane):
        return wide(own, beside_plane(west_ref, east_ref, plane))

    tiles = [[lat_tile(LEVELS * t + k) for k in range(LEVELS)] for t in range(TRACERS)]
    bottom_own = own_ref[OWN_BOTTOM]
    c = tracer_planes(own_ref)
    p_own = pressures(c[1], c[0])
    p_tile = pressures(tiles[1], tiles[0])
    both = wide(
        spare_north(tiles[3][0]) + spare_south(tiles[3][0]),
        spare_north(tiles[3][1]) + spare_south(tiles[3][1]),
    )
    bottom = tallen(whole(bottom_own, BOTTOM), both)
    count_u = jnp.minimum(bottom, at(bottom, 1, 1))
    count_v = jnp.minimum(bottom, at(bottom, 1, 0))
    f_u = coriolis(place * ROWS + row, 0.5)
    f_v = coriolis(place * ROWS + row, 1.0)
    none = jnp.zeros((8, COLS), f32)
    wind = [tallen(wide(own_ref[OWN_WIND + d], jnp.zeros((ROWS, COLS), f32)), jnp.zeros((8, 2 * COLS), f32)) for d in range(2)]

    def up(x):
        return at(x, 1, 0)

    def down(x):
        return at(x, -1, 0)

    stars_u, stars_v, flows, gains = [], [], [], [None] * (TRACERS * LEVELS)
    own_u, own_v = count_u[:ROWS, :COLS], count_v[:ROWS, :COLS]
    mean_u = mean_v = jnp.zeros((ROWS, COLS), f32)
    for k in range(LEVELS):
        east, north = count_u > k, count_v > k
        t0, t1, t2 = tiles[0][k], tiles[1][k], tiles[2][k]
        u_lat = wide(spare_north(t0) + spare_south(t0), spare_north(t2))
        v_lat = wide(spare_north(t1) + spare_south(t1), spare_south(t2))
        u = tallen(whole(own_ref[OWN_EAST + k], EAST + k), u_lat)
        u = jnp.where(east | (row >= ROWS), u, 0.0)
        v = tallen(whole(own_ref[OWN_NORTH + k], NORTH + k), v_lat)
        v = jnp.where(north | (row == ROWS), v, 0.0)
        p = tallen(whole(p_own[k], PRESSURE + k), wide(p_tile[k], none))
        tend_u, tend_v = momentum(k, u, v, p, wind, east, north, f_u, f_v, up, down)
        star_u = (u + time_step * tend_u)[:ROWS, :COLS]
        star_v = (v + time_step * tend_v)[:ROWS, :COLS]
        stars_u.append(star_u)
        stars_v.append(star_v)
        mean_u = mean_u + star_u
        mean_v = mean_v + star_v

        flows.append((u[:ROWS], jnp.where(east[:ROWS], tracer_diffusion, 0.0)))
        diffusion = jnp.where(north[:, :COLS], tracer_diffusion, 0.0)
        for t in range(TRACERS):
            cn = tallen(c[t][k], tiles[t][k])
            gains[LEVELS * t + k] = gain(cn, 0, v[:, :COLS], diffusion)[:ROWS]
    planes = range(TRACERS * LEVELS)
    beside = [beside_tracer(west_ref, east_ref, n) for n in planes]
    values = jnp.concatenate([wide(c[n // LEVELS][n % LEVELS], beside[n]) for n in planes], axis=0)
    flow, diffusion = (
        jnp.concatenate([flows[n % LEVELS][i] for n in planes], axis=0) for i in range(2)
    )
    along = gain(values, 1, flow, diffusion)[:, :COLS]
    for n in planes:
        t, k = divmod(n, LEVELS)
        change = along[ROWS * n : ROWS * (n + 1)] + gains[n]
        tracers_out[t, k] = jnp.where(bottom_own > k, c[t][k] + time_step * change, 0.0)
    shift_u = average_u - mean_u / jnp.maximum(own_u, 1.0)
    shift_v = average_v - mean_v / jnp.maximum(own_v, 1.0)
    for k in range(LEVELS):
        velocity_out[0, k] = jnp.where(own_u > k, stars_u[k] + shift_u, 0.0)
        velocity_out[1, k] = jnp.where(own_v > k, stars_v[k] + shift_v, 0.0)


def ring(axis, step):
    count = lax.axis_size(axis)
    return [(i, (i + step) % count) for i in range(count)]


def struct(*shape):
    return jax.ShapeDtypeStruct(shape, f32)


def vmem(*shape):
    return pltpu.VMEM(shape, f32)


def specs(count, scalars=0):
    return [pl.BlockSpec(memory_space=pltpu.SMEM)] * scalars + [
        pl.BlockSpec(memory_space=pltpu.VMEM)
    ] * count


PARAMS = pltpu.CompilerParams(vmem_limit_bytes=32 * 1024 * 1024)


def stacked(tracers, velocity, surface, wind, bottom):
    def put(values, first):
        values = values.reshape(-1, ROWS, COLS)
        after = OWN - first - values.shape[0]
        return lax.pad(
            values, jnp.zeros((), values.dtype), ((first, after, 0), (0, 0, 0), (0, 0, 0))
        )

    return (
        put(tracers, 0)
        + put(velocity, OWN_EAST)
        + put(surface, OWN_SURFACE)
        + put(wind, OWN_WIND)
        + put(bottom, OWN_BOTTOM).astype(f32)
    )


def shards(tracers, velocity, surface, wind, bottom):
    place = lax.axis_index("lat").astype(jnp.int32).reshape(1)
    own = stacked(tracers, velocity, surface, wind, bottom)
    payload = struct(PLANES // 4 + 1, ROWS, COLS)
    to_right, to_left = pl.pallas_call(
        pack_kernel,
        out_shape=(payload, payload),
        in_specs=specs(1),
        out_specs=tuple(specs(2)),
        compiler_params=PARAMS,
        name="pack",
    )(own)
    west = lax.ppermute(to_right, "lon", ring("lon", 1))
    east = lax.ppermute(to_left, "lon", ring("lon", -1))
    chunks = pl.pallas_call(
        send_kernel,
        out_shape=struct(MEMBERS, CHUNK, COLS),
        in_specs=specs(3, 1),
        out_specs=specs(1)[0],
        scratch_shapes=[
            vmem(12 * ROWS, COLS),
            vmem(2, COLS, COLS),
            vmem(40, 2 * COLS),
            vmem(COLS + 2 * HALO, COLS),
        ],
        compiler_params=PARAMS,
        name="columns",
    )(place, own, west, east)
    slabs = lax.all_to_all(chunks, "lat", 0, 0, tiled=True)
    answers = pl.pallas_call(
        slab_kernel,
        out_shape=struct(MEMBERS, BACK, COLS),
        in_specs=specs(1),
        out_specs=specs(1)[0],
        scratch_shapes=[vmem(COLS, COLS)],
        compiler_params=PARAMS,
        name="substeps",
    )(slabs)
    home = lax.all_to_all(answers, "lat", 0, 0, tiled=True)
    return pl.pallas_call(
        finish_kernel,
        out_shape=(
            struct(TRACERS, LEVELS, ROWS, COLS),
            struct(2, LEVELS, ROWS, COLS),
            struct(ROWS, COLS),
            struct(ROWS, COLS),
        ),
        in_specs=specs(4, 1),
        out_specs=tuple(specs(4)),
        scratch_shapes=[vmem(COLS, COLS), vmem(4 * ROWS, COLS)],
        compiler_params=PARAMS,
        name="finish",
    )(place, home, own, west, east)


def solution(mesh):
    placed = (
        P(None, None, "lat", "lon"),
        P(None, None, "lat", "lon"),
        P("lat", "lon"),
        P(None, "lat", "lon"),
        P("lat", "lon"),
    )
    return jax.shard_map(
        shards,
        mesh=mesh,
        in_specs=placed,
        out_specs=(
            P(None, None, "lat", "lon"),
            P(None, None, "lat", "lon"),
            P("lat", "lon"),
            P("lat", "lon"),
        ),
        check_vma=False,
    )
```

```python
import jax
import jax.numpy as jnp
from jax import lax
from jax.experimental import pallas as pl
from jax.experimental.pallas import tpu as pltpu
from jax.sharding import PartitionSpec as P

TRACERS = 4
LEVELS = 8
SUBSTEPS = 30
ROWS = 16
COLS = 128
MEMBERS = 16
HALO = 32
SLAB = 72
NLAT = ROWS * MEMBERS

time_step = 0.2
tracer_diffusion = 0.2
viscosity = 0.2
thermal_expansion = 2.0
haline_contraction = 1.5
coriolis_base = 1.0
gravity = 140.0
surface_scale = 40.0
thickness = 1.0 / LEVELS
f32 = jnp.float32

PRESSURE, EAST, NORTH, WIND, SURFACE, BOTTOM = 0, 8, 16, 24, 26, 27
PLANES = 28
OWN_EAST, OWN_NORTH, OWN_SURFACE, OWN_WIND, OWN_BOTTOM, OWN = 32, 40, 48, 49, 51, 52
MAIL_N, MAIL_S, EDGE, CHUNK = SLAB, SLAB + 8, SLAB + 16, SLAB + 24
BACK = 24


def at(values, step, axis):
    size = values.shape[axis]
    step %= size
    return values if step == 0 else pltpu.roll(values, size - step, axis)


def ids(shape, axis):
    return lax.broadcasted_iota(jnp.int32, shape, axis)


def wide(own, beside):
    return jnp.concatenate([own, beside], axis=1)


def tracer_planes(own_ref):
    bottom = own_ref[OWN_BOTTOM]
    return [
        [jnp.where(bottom > k, own_ref[LEVELS * t + k], 0.0) for k in range(LEVELS)]
        for t in range(TRACERS)
    ]


def pressures(salt, heat):
    total, out = None, []
    for k in range(LEVELS):
        density = haline_contraction * salt[k] - thermal_expansion * heat[k]
        total = density if total is None else total + density
        out.append(thickness * total)
    return out


def pack_kernel(own_ref, right_ref, left_ref):
    c = tracer_planes(own_ref)
    planes = pressures(c[1], c[0])
    planes += [own_ref[n] for n in range(OWN_EAST, OWN_SURFACE)]
    planes += [own_ref[n] for n in (OWN_WIND, OWN_WIND + 1, OWN_SURFACE, OWN_BOTTOM)]
    lane = ids((ROWS, COLS), 1)
    for q in range(PLANES // 4):
        right = left = jnp.zeros((ROWS, COLS), f32)
        for s in range(4):
            moved = at(planes[4 * q + s], -32 * s, 1)
            right = jnp.where(lane // 32 == (s + 3) % 4, moved, right)
            left = jnp.where(lane // 32 == s, moved, left)
        right_ref[q] = right
        left_ref[q] = left
    right = left = jnp.zeros((ROWS, COLS), f32)
    for n in range(TRACERS * LEVELS):
        moved = at(c[n // LEVELS][n % LEVELS], -4 * n, 1)
        right = jnp.where(lane // 4 == (n + 31) % 32, moved, right)
        left = jnp.where(lane // 4 == n, moved, left)
    right_ref[PLANES // 4] = right
    left_ref[PLANES // 4] = left


def beside_plane(west_ref, east_ref, plane):
    q, s = divmod(plane, 4)
    block = ids((ROWS, COLS), 1) // 32
    both = jnp.where(
        block == s, east_ref[q], jnp.where(block == (s + 3) % 4, west_ref[q], 0.0)
    )
    return at(both, 32 * s, 1)


def momentum(k, u, v, p, wind, east, north, f_u, f_v, up, down):
    pair_v = v + down(v)
    pair_u = u + at(u, -1, 1)
    tend_u = (
        (0.25 * f_u) * (pair_v + at(pair_v, 1, 1))
        - (at(p, 1, 1) - p)
        + viscosity * (at(u, 1, 1) + at(u, -1, 1) + up(u) + down(u) - 4.0 * u)
    )
    tend_v = (
        (-0.25 * f_v) * (pair_u + up(pair_u))
        - (up(p) - p)
        + viscosity * (at(v, 1, 1) + at(v, -1, 1) + up(v) + down(v) - 4.0 * v)
    )
    if k == 0:
        tend_u = tend_u + wind[0]
        tend_v = tend_v + wind[1]
    return jnp.where(east, tend_u, 0.0), jnp.where(north, tend_v, 0.0)


def coriolis(rows, offset):
    return coriolis_base * (0.5 + (rows.astype(f32) + offset) / NLAT)


def send_kernel(
    place_ref, own_ref, west_ref, east_ref,
    out_ref, split_ref, stack_ref, edge_ref, turned_ref,
):
    place = place_ref[0]
    c = tracer_planes(own_ref)
    p_own = pressures(c[1], c[0])

    def whole(own, plane):
        return wide(own, beside_plane(west_ref, east_ref, plane))

    shape = (ROWS, 2 * COLS)
    row = ids(shape, 0)
    bottom = whole(own_ref[OWN_BOTTOM], BOTTOM)
    wind = [whole(own_ref[OWN_WIND + d], WIND + d) for d in range(2)]

    def up(x):
        return jnp.where(row == ROWS - 1, 0.0, at(x, 1, 0))

    def down(x):
        return jnp.where(row == 0, 0.0, at(x, -1, 0))

    count_u = jnp.minimum(bottom, at(bottom, 1, 1))
    count_v = jnp.minimum(bottom, up(bottom))
    f_u = coriolis(place * ROWS + row, 0.5)
    f_v = coriolis(place * ROWS + row, 1.0)
    sums = [jnp.zeros(shape, f32) for _ in range(4)]
    us, vs, raws = [], [], []
    for k in range(LEVELS):
        east, north = count_u > k, count_v > k
        u = jnp.where(east, whole(own_ref[OWN_EAST + k], EAST + k), 0.0)
        raw = jnp.where(bottom > k, whole(own_ref[OWN_NORTH + k], NORTH + k), 0.0)
        v = jnp.where(north, raw, 0.0)
        p = whole(p_own[k], PRESSURE + k)
        tend_u, tend_v = momentum(k, u, v, p, wind, east, north, f_u, f_v, up, down)
        sums = [a + b for a, b in zip(sums, (u, v, tend_u, tend_v))]
        us.append(u)
        vs.append(v)
        raws.append(raw)
        pair = u + at(u, -1, 1)
        last = p[8:] + (-0.25 * f_v[8:]) * pair[8:] + viscosity * at(v, -1, 0)[8:]
        if k == 0:
            last = last + wind[1][8:]
        first = (-0.25 * (f_v[:8] - 1.0 / NLAT)) * pair[:8] - p[:8] + viscosity * v[:8]
        edge_ref[k : k + 1] = u[15:16]
        edge_ref[8 + k : 9 + k] = raw[15:16]
        edge_ref[16 + k : 17 + k] = last[7:8]
        edge_ref[24 + k : 25 + k] = u[0:1]
        edge_ref[32 + k : 33 + k] = first[0:1]
    surface = whole(own_ref[OWN_SURFACE], SURFACE)
    for n, values in enumerate((surface, *sums, bottom)):
        split_ref[ROWS * n : ROWS * (n + 1)] = values[:, :COLS]
        split_ref[ROWS * (6 + n) : ROWS * (7 + n)] = values[:, COLS:]
    for q in range(16):
        spot = pl.multiple_of(lax.rem(q + place, 16) * 8, 8)
        for half in range(2):
            if q < 12:
                rows = split_ref[pl.ds(ROWS * (6 * half + q // 2) + q % 2, 8, 2), :]
            else:
                rows = edge_ref[8 * (q - 12) : 8 * (q - 11), COLS * half : COLS * (half + 1)]
            stack_ref[half, pl.ds(spot, 8)] = rows
    turned_ref[HALO : HALO + COLS] = stack_ref[0].T
    beyond = stack_ref[1].T
    turned_ref[:HALO] = beyond[COLS - HALO :]
    turned_ref[HALO + COLS :] = beyond[:HALO]
    edge = edge_ref[32:40]
    for d in range(MEMBERS):
        out_ref[d, :SLAB] = turned_ref[8 * d : 8 * d + SLAB]
        out_ref[d, EDGE:CHUNK] = at(edge, 8 * d - HALO, 1)[:, :COLS]

    sub = ids((8, COLS), 0)

    def spare(n):
        t, k = divmod(n, LEVELS)
        if t == 0:
            return us[k][:, :COLS], us[k][:, :COLS]
        if t == 1:
            return raws[k][:, :COLS], vs[k][:, :COLS]
        if t == 2:
            return raws[k][:, COLS:], us[k][:, COLS:]
        if k < 2:
            own = bottom[:, COLS * k : COLS * (k + 1)]
            return own, own
        return None

    def tops(n):
        own = c[n // LEVELS][n % LEVELS][8:]
        more = spare(n)
        return own if more is None else jnp.where(sub == 4, at(more[0][8:], 3, 0), own)

    def bottoms(n):
        own = c[n // LEVELS][n % LEVELS][:8]
        more = spare(n)
        return own if more is None else jnp.where(sub == 3, at(more[1][:8], -3, 0), own)

    for m in range(MEMBERS):
        out_ref[m, MAIL_N:MAIL_S] = jnp.where(sub >= 4, tops(2 * m), at(tops(2 * m + 1), 4, 0))
        out_ref[m, MAIL_S:EDGE] = jnp.where(sub < 4, bottoms(2 * m), at(bottoms(2 * m + 1), 4, 0))


def slab_kernel(in_ref, out_ref, edge_ref):
    shape = (SLAB, COLS)
    lane = ids(shape, 1)
    r = lane % 8
    block = ids((8, COLS), 1) // 8

    tiles = []
    for t in range(SLAB // 8):
        now = [in_ref[a, 8 * t : 8 * t + 8] for a in range(MEMBERS)]
        for bit in (1, 2, 4, 8):
            odd = (block & bit) > 0
            now = [jnp.where(odd, now[(a + bit) % MEMBERS], now[a]) for a in range(MEMBERS)]
        tiles.append([at(now[-q % MEMBERS], 8 * q, 1) for q in range(16)])
    blocks = [jnp.concatenate([tile[q] for tile in tiles], axis=0) for q in range(16)]
    surface, start_u, start_v, force_u, force_v, bottom = (blocks[2 * n : 2 * n + 2] for n in range(6))
    u_a, v_raw, near, u_next = blocks[12:]
    zeros = jnp.zeros((8, COLS), f32)
    for a in range(MEMBERS):
        edge_ref[8 * a : 8 * a + 8] = in_ref[a + 1, EDGE:CHUNK] if a < MEMBERS - 1 else zeros
    far = edge_ref[...].T[:SLAB]

    top = lane == COLS - 1
    count_u = [jnp.minimum(b, at(b, 1, 0)) for b in bottom]
    count_v = [
        jnp.minimum(*bottom),
        jnp.where(top, 0.0, jnp.minimum(bottom[1], at(bottom[0], 1, 1))),
    ]

    ahead = jnp.concatenate([count_u[0], count_v[0]], axis=0)
    first = (ids(ahead.shape, 1) % 8 == 0) & (ids(ahead.shape, 1) > 0)
    counts = jnp.concatenate(
        [
            jnp.where(r == 7, count_u[1], 0.0),
            jnp.where(r == 7, count_v[1], 0.0),
            jnp.where(r == 7, count_v[0], 0.0),
            at(jnp.where(first, ahead, 0.0), 1, 1),
        ],
        axis=0,
    )
    for step in (1, 2, 4):
        counts = counts + at(counts, step, 1)
    count_ua, count_va, count_vc, count_ub, count_vb = (
        counts[SLAB * n : SLAB * (n + 1)] for n in range(5)
    )
    level = r.astype(f32)
    last = lane >= COLS - 8
    v_a = jnp.where(count_va > level, v_raw, 0.0)
    u_a = jnp.where(last, 0.0, u_a)
    u_b = jnp.where(last, 0.0, at(u_next, 8, 1))
    f_a = 0.25 * coriolis(lane // 8 * ROWS + 15, 0.5)
    f_b = f_a + 0.25 * coriolis_base / NLAT
    pair = v_a + at(v_a, 1, 0)
    spread = viscosity * (at(v_a, 1, 0) + at(v_a, -1, 0) - 4.0 * v_a)
    terms = jnp.concatenate(
        [
            jnp.where(count_ua > level, f_a * pair + viscosity * u_b, 0.0),
            jnp.where(count_ub > level, f_b * pair + viscosity * u_a, 0.0),
            jnp.where(count_vb > level, viscosity * v_a, 0.0),
            jnp.where(count_vc > level, viscosity * v_a, 0.0),
            jnp.where(count_va > level, near + far + spread, 0.0),
            v_a,
        ],
        axis=0,
    )
    for step in (1, 2, 4):
        terms = terms + at(terms, -step, 1)
    shifted = at(terms[SLAB : 3 * SLAB], -1, 1)
    u_15, v_14, v_15, begin_15 = (
        jnp.where(r == 7, terms[SLAB * n : SLAB * (n + 1)], 0.0) for n in (0, 3, 4, 5)
    )
    u_16, v_16 = (jnp.where(r == 0, shifted[SLAB * n : SLAB * (n + 1)], 0.0) for n in range(2))
    force_u = [force_u[0] + u_16, force_u[1] + u_15]
    force_v = [force_v[0] + (v_14 + v_16), force_v[1] + v_15]
    start_v = [start_v[0], start_v[1] + begin_15]

    sub_step = time_step / SUBSTEPS
    held_u, held_v, flux_u, flux_v, begin_u, begin_v = [], [], [], [], [], []
    for i in range(2):
        per = 1.0 / jnp.maximum(count_u[i], 1.0)
        open_face = jnp.where(count_u[i] > 0.0, sub_step, 0.0)
        flux_u.append((sub_step * surface_scale * thickness) * count_u[i])
        held_u.append(
            (
                (0.25 * open_face) * coriolis(2 * lane + i, 0.5),
                gravity * open_face,
                open_face * (force_u[i] * per),
            )
        )
        begin_u.append(start_u[i] * per)
        per = 1.0 / jnp.maximum(count_v[i], 1.0)
        open_face = jnp.where(count_v[i] > 0.0, sub_step, 0.0)
        flux_v.append((sub_step * surface_scale * thickness) * count_v[i])
        held_v.append(
            (
                (-0.25 * open_face) * coriolis(2 * lane + i, 1.0),
                gravity * open_face,
                open_face * (force_v[i] * per),
            )
        )
        begin_v.append(start_v[i] * per)
    held = (
        *flux_u, at(flux_u[0], 1, 1), *flux_v, at(flux_v[0], 1, 1), at(flux_v[1], -1, 1),
        *held_u[0], *held_u[1], *held_v[0], *held_v[1],
    )
    state = (*surface, at(surface[0], 1, 1), *begin_u, *begin_v)
    total = (zeros,) * 4
    for low, steps in ((0, 6), (8, 8), (16, 8), (24, 8)):
        cut = 8 if low else 0
        state = tuple(x[cut : x.shape[0] - cut] for x in state)
        (
            du0, du1, du2, dv0, dv1, dv2, dv_, cu0, gu0, fu0, cu1, gu1, fu1,
            cv0, gv0, fv0, cv1, gv1, fv1,
        ) = (x[low : SLAB - low] for x in held)
        centre = HALO - low

        def advance(_, carry):
            h0, h1, h2, u0, u1, v0, v1, *sums = carry
            v_ = at(v1, -1, 1)
            u2 = at(u0, 1, 1)
            v2 = at(v0, 1, 1)
            x0, x1, x2 = du0 * u0, du1 * u1, du2 * u2
            y0, y1 = dv0 * v0, dv1 * v1
            h1 = h1 - ((x1 - at(x1, -1, 0)) + (y1 - y0))
            h0 = h0 - ((x0 - at(x0, -1, 0)) + (y0 - dv_ * v_))
            h2 = h2 - ((x2 - at(x2, -1, 0)) + (dv2 * v2 - y1))
            p0, p1, p2 = u0 + at(u0, -1, 0), u1 + at(u1, -1, 0), u2 + at(u2, -1, 0)
            q0, q1 = v0 + v_, v1 + v0
            u0 = (u0 + fu0) + (cu0 * (q0 + at(q0, 1, 0)) - gu0 * (at(h0, 1, 0) - h0))
            u1 = (u1 + fu1) + (cu1 * (q1 + at(q1, 1, 0)) - gu1 * (at(h1, 1, 0) - h1))
            v0 = (v0 + fv0) + (cv0 * (p0 + p1) - gv0 * (h1 - h0))
            v1 = (v1 + fv1) + (cv1 * (p1 + p2) - gv1 * (h2 - h1))
            sums = [a + b[centre : centre + 8] for a, b in zip(sums, (u0, u1, v0, v1))]
            return (h0, h1, h2, u0, u1, v0, v1, *sums)

        *state, a0, a1, a2, a3 = lax.fori_loop(
            0, steps, advance, (*state, *total), unroll=True
        )
        total = (a0, a1, a2, a3)
    height = [x[8:16] for x in state[:2]]
    average = [x * (1.0 / SUBSTEPS) for x in total]
    transport = [
        (-thickness * count_u[i][HALO : HALO + 8]) * average[i] for i in range(2)
    ]
    square = (COLS, COLS)
    before = (ids(square, 0) < ids(square, 1)).astype(f32)
    south = jnp.dot(
        transport[0] + transport[1],
        before,
        precision=lax.Precision.HIGHEST,
        preferred_element_type=f32,
    )
    stream = [south + transport[0], south + (transport[0] + transport[1])]
    results = [*height, *stream, *average]
    moved = [at(values, -8 * n, 1) for n, values in enumerate(results)]
    for e in range(MEMBERS):
        packed = moved[0]
        for n in range(1, 8):
            packed = jnp.where(block == (e + n) % 16, moved[n], packed)
        out_ref[e, 0:8] = packed
        out_ref[e, 8:16] = in_ref[(e + 15) % MEMBERS, MAIL_N:MAIL_S]
        out_ref[e, 16:24] = in_ref[(e + 1) % MEMBERS, MAIL_S:EDGE]


def gain(values, axis, flow, diffusion):
    ahead = at(values, 1, axis)
    sides = at(values, -1, axis) + at(values, 2, axis)
    far = at(values, -2, axis) + at(values, 3, axis)
    face = (37.0 * (values + ahead) - 8.0 * sides + far) * (1.0 / 60.0)
    flux = diffusion * (ahead - values) - flow * face
    return flux - at(flux, -1, axis)


def inner_kernel(own_ref, out_ref):
    bottom = own_ref[OWN_BOTTOM]
    c = tracer_planes(own_ref)
    count = jnp.minimum(bottom, at(bottom, 1, 1))
    values = jnp.concatenate([plane for tracer in c for plane in tracer], axis=0)
    flow, diffusion = [], []
    for k in range(LEVELS):
        flow.append(jnp.where(count > k, own_ref[OWN_EAST + k], 0.0))
        diffusion.append(jnp.where(count > k, tracer_diffusion, 0.0))
    flow, diffusion = (jnp.concatenate(x * TRACERS, axis=0) for x in (flow, diffusion))
    lane = ids(values.shape, 1)

    def moved(step):
        inside = lane < COLS - step if step > 0 else lane >= -step
        return jnp.where(inside, at(values, step, 1), 0.0)

    ahead = moved(1)
    face = (37.0 * (values + ahead) - 8.0 * (moved(-1) + moved(2)) + (moved(-2) + moved(3))) * (
        1.0 / 60.0
    )
    flux = jnp.where(lane < COLS - 1, diffusion * (ahead - values) - flow * face, 0.0)
    out_ref[...] = flux - at(flux, -1, 1)


def outer(west, east, left, right, flow_w, flow_l, flow_r, diff_w, diff_r):
    q = ids((ROWS, COLS), 1) % 4
    sixtieth = 1.0 / 60.0
    w1, w2, w3 = at(west, 3, 1), at(west, 2, 1), at(west, 1, 1)
    face = 37.0 * (w1 + left) - 8.0 * (w2 + at(left, 1, 1)) + (w3 + at(left, 2, 1))
    through = at(diff_w, 3, 1) * (left - w1) - at(flow_w, 3, 1) * (face * sixtieth)
    flux = jnp.where(q == 0, w2 - 8.0 * w1, jnp.where(q == 1, w2, 0.0)) * (-sixtieth) * flow_l
    low = flux - at(flux, -1, 1) - jnp.where(q == 0, through, 0.0)
    e1, e2, e3 = at(east, -3, 1), at(east, -2, 1), at(east, -1, 1)
    face = 37.0 * (right + e1) - 8.0 * (at(right, -1, 1) + e2) + (at(right, -2, 1) + e3)
    through = diff_r * (e1 - right) - flow_r * (face * sixtieth)
    flux = jnp.where(q == 2, e3 - 8.0 * e2, jnp.where(q == 1, e3, 0.0)) * (-sixtieth) * flow_r
    high = flux - at(flux, -1, 1) + jnp.where(q == 3, through, 0.0)
    return low, high


def finish_kernel(
    place_ref, in_ref, own_ref, west_ref, east_ref, right_ref, left_ref, inner_ref,
    tracers_out, velocity_out, height_out, stream_out, turned_ref, rows_ref,
):
    place = place_ref[0]
    turned_ref[...] = in_ref[:, 0:8].reshape(COLS, COLS).T

    for q in range(8):
        spot = pl.multiple_of(lax.rem(q + place, 16) * 8, 8)
        rows_ref[pl.ds(ROWS * (q // 2) + q % 2, 8, 2), :] = turned_ref[pl.ds(spot, 8)]
    height_out[...] = rows_ref[:ROWS]
    stream_out[...] = rows_ref[ROWS : 2 * ROWS]
    average_u, average_v = rows_ref[2 * ROWS : 3 * ROWS], rows_ref[3 * ROWS :]

    sub = ids((8, COLS), 0)
    tall = (ROWS + 8, 2 * COLS)
    row = ids(tall, 0)
    first, last = place == 0, place == MEMBERS - 1

    def lat_tile(n):
        south = jnp.where(first, 0.0, in_ref[n // 2, 8:16])
        north = jnp.where(last, 0.0, in_ref[n // 2, 16:24])
        if n % 2 == 0:
            return jnp.where(sub < 4, north, south)
        return at(jnp.where(sub < 4, south, north), 4, 0)

    def spare_north(tile):
        return jnp.where(sub == 0, at(tile, 3, 0), 0.0)

    def spare_south(tile):
        return jnp.where(sub == 7, at(tile, -3, 0), 0.0)

    def tallen(own, tile):
        return jnp.concatenate([own, tile], axis=0)

    def whole(own, plane):
        return wide(own, beside_plane(west_ref, east_ref, plane))

    tiles = [[lat_tile(LEVELS * t + k) for k in range(LEVELS)] for t in range(TRACERS)]
    bottom_own = own_ref[OWN_BOTTOM]
    c = tracer_planes(own_ref)
    p_own = pressures(c[1], c[0])
    p_tile = pressures(tiles[1], tiles[0])
    both = wide(
        spare_north(tiles[3][0]) + spare_south(tiles[3][0]),
        spare_north(tiles[3][1]) + spare_south(tiles[3][1]),
    )
    bottom = tallen(whole(bottom_own, BOTTOM), both)
    count_u = jnp.minimum(bottom, at(bottom, 1, 1))
    count_v = jnp.minimum(bottom, at(bottom, 1, 0))
    f_u = coriolis(place * ROWS + row, 0.5)
    f_v = coriolis(place * ROWS + row, 1.0)
    none = jnp.zeros((8, COLS), f32)
    wind = [tallen(wide(own_ref[OWN_WIND + d], jnp.zeros((ROWS, COLS), f32)), jnp.zeros((8, 2 * COLS), f32)) for d in range(2)]

    def up(x):
        return at(x, 1, 0)

    def down(x):
        return at(x, -1, 0)

    stars_u, stars_v, flows, gains = [], [], [], [None] * (TRACERS * LEVELS)
    own_u, own_v = count_u[:ROWS, :COLS], count_v[:ROWS, :COLS]
    mean_u = mean_v = jnp.zeros((ROWS, COLS), f32)
    for k in range(LEVELS):
        east, north = count_u > k, count_v > k
        t0, t1, t2 = tiles[0][k], tiles[1][k], tiles[2][k]
        u_lat = wide(spare_north(t0) + spare_south(t0), spare_north(t2))
        v_lat = wide(spare_north(t1) + spare_south(t1), spare_south(t2))
        u = tallen(whole(own_ref[OWN_EAST + k], EAST + k), u_lat)
        u = jnp.where(east | (row >= ROWS), u, 0.0)
        v = tallen(whole(own_ref[OWN_NORTH + k], NORTH + k), v_lat)
        v = jnp.where(north | (row == ROWS), v, 0.0)
        p = tallen(whole(p_own[k], PRESSURE + k), wide(p_tile[k], none))
        tend_u, tend_v = momentum(k, u, v, p, wind, east, north, f_u, f_v, up, down)
        star_u = (u + time_step * tend_u)[:ROWS, :COLS]
        star_v = (v + time_step * tend_v)[:ROWS, :COLS]
        stars_u.append(star_u)
        stars_v.append(star_v)
        mean_u = mean_u + star_u
        mean_v = mean_v + star_v

        flows.append((u[:ROWS], jnp.where(east[:ROWS], tracer_diffusion, 0.0)))
        diffusion = jnp.where(north[:, :COLS], tracer_diffusion, 0.0)
        for t in range(TRACERS):
            cn = tallen(c[t][k], tiles[t][k])
            gains[LEVELS * t + k] = gain(cn, 0, v[:, :COLS], diffusion)[:ROWS]
    block = ids((ROWS, COLS), 1) // 4

    def packed(which, half, ahead):
        tile = jnp.zeros((ROWS, COLS), f32)
        for k in range(LEVELS):
            values = flows[k][which][:, COLS * half : COLS * (half + 1)]
            tile = jnp.where(block % LEVELS == k, at(values, -4 * (k + ahead), 1), tile)
        for step in (32, 64):
            tile = jnp.where(block * 4 % (2 * step) < step, tile, at(tile, -step, 1))
        return tile

    last = PLANES // 4
    low, high = outer(
        at(west_ref[last], -4, 1), east_ref[last], left_ref[last], at(right_ref[last], -4, 1),
        packed(0, 1, 1), packed(0, 0, 0), packed(0, 0, 1), packed(1, 1, 1), packed(1, 0, 1),
    )
    high = at(high, 4, 1)
    planes = range(TRACERS * LEVELS)
    sides = [
        at(jnp.where(block == n, low, jnp.where(block == (n + 31) % 32, high, 0.0)), 4 * n, 1)
        for n in planes
    ]
    for n in planes:
        t, k = divmod(n, LEVELS)
        change = inner_ref[ROWS * n : ROWS * (n + 1)] + sides[n] + gains[n]
        tracers_out[t, k] = jnp.where(bottom_own > k, c[t][k] + time_step * change, 0.0)
    shift_u = average_u - mean_u / jnp.maximum(own_u, 1.0)
    shift_v = average_v - mean_v / jnp.maximum(own_v, 1.0)
    for k in range(LEVELS):
        velocity_out[0, k] = jnp.where(own_u > k, stars_u[k] + shift_u, 0.0)
        velocity_out[1, k] = jnp.where(own_v > k, stars_v[k] + shift_v, 0.0)


def ring(axis, step):
    count = lax.axis_size(axis)
    return [(i, (i + step) % count) for i in range(count)]


def struct(*shape):
    return jax.ShapeDtypeStruct(shape, f32)


def vmem(*shape):
    return pltpu.VMEM(shape, f32)


def specs(count, scalars=0):
    return [pl.BlockSpec(memory_space=pltpu.SMEM)] * scalars + [
        pl.BlockSpec(memory_space=pltpu.VMEM)
    ] * count


PARAMS = pltpu.CompilerParams(vmem_limit_bytes=32 * 1024 * 1024)


def stacked(tracers, velocity, surface, wind, bottom):
    def put(values, first):
        values = values.reshape(-1, ROWS, COLS)
        after = OWN - first - values.shape[0]
        return lax.pad(
            values, jnp.zeros((), values.dtype), ((first, after, 0), (0, 0, 0), (0, 0, 0))
        )

    return (
        put(tracers, 0)
        + put(velocity, OWN_EAST)
        + put(surface, OWN_SURFACE)
        + put(wind, OWN_WIND)
        + put(bottom, OWN_BOTTOM).astype(f32)
    )


def shards(tracers, velocity, surface, wind, bottom):
    place = lax.axis_index("lat").astype(jnp.int32).reshape(1)
    own = stacked(tracers, velocity, surface, wind, bottom)
    payload = struct(PLANES // 4 + 1, ROWS, COLS)
    to_right, to_left = pl.pallas_call(
        pack_kernel,
        out_shape=(payload, payload),
        in_specs=specs(1),
        out_specs=tuple(specs(2)),
        compiler_params=PARAMS,
        name="pack",
    )(own)
    west = lax.ppermute(to_right, "lon", ring("lon", 1))
    east = lax.ppermute(to_left, "lon", ring("lon", -1))
    inner = pl.pallas_call(
        inner_kernel,
        out_shape=struct(TRACERS * LEVELS * ROWS, COLS),
        in_specs=specs(1),
        out_specs=specs(1)[0],
        compiler_params=PARAMS,
        cost_estimate=pl.CostEstimate(flops=1500000, bytes_accessed=3000000, transcendentals=0),
        name="inner",
    )(own)
    chunks = pl.pallas_call(
        send_kernel,
        out_shape=struct(MEMBERS, CHUNK, COLS),
        in_specs=specs(3, 1),
        out_specs=specs(1)[0],
        scratch_shapes=[
            vmem(12 * ROWS, COLS),
            vmem(2, COLS, COLS),
            vmem(40, 2 * COLS),
            vmem(COLS + 2 * HALO, COLS),
        ],
        compiler_params=PARAMS,
        name="columns",
    )(place, own, west, east)
    slabs = lax.all_to_all(chunks, "lat", 0, 0, tiled=True)
    answers = pl.pallas_call(
        slab_kernel,
        out_shape=struct(MEMBERS, BACK, COLS),
        in_specs=specs(1),
        out_specs=specs(1)[0],
        scratch_shapes=[vmem(COLS, COLS)],
        compiler_params=PARAMS,
        name="substeps",
    )(slabs)
    home = lax.all_to_all(answers, "lat", 0, 0, tiled=True)
    return pl.pallas_call(
        finish_kernel,
        out_shape=(
            struct(TRACERS, LEVELS, ROWS, COLS),
            struct(2, LEVELS, ROWS, COLS),
            struct(ROWS, COLS),
            struct(ROWS, COLS),
        ),
        in_specs=specs(7, 1),
        out_specs=tuple(specs(4)),
        scratch_shapes=[vmem(COLS, COLS), vmem(4 * ROWS, COLS)],
        compiler_params=PARAMS,
        name="finish",
    )(place, home, own, west, east, to_right, to_left, inner)


def solution(mesh):
    placed = (
        P(None, None, "lat", "lon"),
        P(None, None, "lat", "lon"),
        P("lat", "lon"),
        P(None, "lat", "lon"),
        P("lat", "lon"),
    )
    return jax.shard_map(
        shards,
        mesh=mesh,
        in_specs=placed,
        out_specs=(
            P(None, None, "lat", "lon"),
            P(None, None, "lat", "lon"),
            P("lat", "lon"),
            P("lat", "lon"),
        ),
        check_vma=False,
    )
```

```python
import jax
import jax.numpy as jnp
from jax import lax
from jax.experimental import pallas as pl
from jax.experimental.pallas import tpu as pltpu
from jax.sharding import PartitionSpec as P

TRACERS = 4
LEVELS = 8
SUBSTEPS = 30
ROWS = 16
COLS = 128
MEMBERS = 16
HALO = 32
SLAB = 72
NLAT = ROWS * MEMBERS

time_step = 0.2
tracer_diffusion = 0.2
viscosity = 0.2
thermal_expansion = 2.0
haline_contraction = 1.5
coriolis_base = 1.0
gravity = 140.0
surface_scale = 40.0
thickness = 1.0 / LEVELS
f32 = jnp.float32

PRESSURE, EAST, NORTH, WIND, SURFACE, BOTTOM = 0, 8, 16, 24, 26, 27
PLANES = 28
OWN_EAST, OWN_NORTH, OWN_SURFACE, OWN_WIND, OWN_BOTTOM, OWN = 32, 40, 48, 49, 51, 52
MAIL_N, MAIL_S, EDGE, CHUNK = SLAB, SLAB + 8, SLAB + 16, SLAB + 24
BACK = 24


def at(values, step, axis):
    size = values.shape[axis]
    step %= size
    return values if step == 0 else pltpu.roll(values, size - step, axis)


def ids(shape, axis):
    return lax.broadcasted_iota(jnp.int32, shape, axis)


def wide(own, beside):
    return jnp.concatenate([own, beside], axis=1)


def tracer_planes(own_ref):
    bottom = own_ref[OWN_BOTTOM]
    return [
        [jnp.where(bottom > k, own_ref[LEVELS * t + k], 0.0) for k in range(LEVELS)]
        for t in range(TRACERS)
    ]


def pressures(salt, heat):
    total, out = None, []
    for k in range(LEVELS):
        density = haline_contraction * salt[k] - thermal_expansion * heat[k]
        total = density if total is None else total + density
        out.append(thickness * total)
    return out


def pack_kernel(even_ref, own_ref, first_ref, second_ref):
    even = even_ref[0] > 0
    c = tracer_planes(own_ref)
    planes = pressures(c[1], c[0])
    planes += [own_ref[n] for n in range(OWN_EAST, OWN_SURFACE)]
    planes += [own_ref[n] for n in (OWN_WIND, OWN_WIND + 1, OWN_SURFACE, OWN_BOTTOM)]
    lane = ids((ROWS, COLS), 1)
    for q in range(PLANES // 4):
        right = left = jnp.zeros((ROWS, COLS), f32)
        for s in range(4):
            moved = at(planes[4 * q + s], -32 * s, 1)
            right = jnp.where(lane // 32 == (s + 3) % 4, moved, right)
            left = jnp.where(lane // 32 == s, moved, left)
        first_ref[q] = jnp.where(even, right, left)
        second_ref[q] = jnp.where(even, left, right)
    right = left = jnp.zeros((ROWS, COLS), f32)
    for n in range(TRACERS * LEVELS):
        moved = at(c[n // LEVELS][n % LEVELS], -4 * n, 1)
        right = jnp.where(lane // 4 == (n + 31) % 32, moved, right)
        left = jnp.where(lane // 4 == n, moved, left)
    first_ref[PLANES // 4] = jnp.where(even, right, left)
    second_ref[PLANES // 4] = jnp.where(even, left, right)


def sort_sides(even_ref, first_ref, second_ref, west_ref, east_ref):
    even = even_ref[0] > 0
    for q in range(PLANES // 4 + 1):
        west_ref[q] = jnp.where(even, second_ref[q], first_ref[q])
        east_ref[q] = jnp.where(even, first_ref[q], second_ref[q])


def beside_plane(west_ref, east_ref, plane):
    q, s = divmod(plane, 4)
    block = ids((ROWS, COLS), 1) // 32
    both = jnp.where(
        block == s, east_ref[q], jnp.where(block == (s + 3) % 4, west_ref[q], 0.0)
    )
    return at(both, 32 * s, 1)


def momentum(k, u, v, p, wind, east, north, f_u, f_v, up, down):
    pair_v = v + down(v)
    pair_u = u + at(u, -1, 1)
    tend_u = (
        (0.25 * f_u) * (pair_v + at(pair_v, 1, 1))
        - (at(p, 1, 1) - p)
        + viscosity * (at(u, 1, 1) + at(u, -1, 1) + up(u) + down(u) - 4.0 * u)
    )
    tend_v = (
        (-0.25 * f_v) * (pair_u + up(pair_u))
        - (up(p) - p)
        + viscosity * (at(v, 1, 1) + at(v, -1, 1) + up(v) + down(v) - 4.0 * v)
    )
    if k == 0:
        tend_u = tend_u + wind[0]
        tend_v = tend_v + wind[1]
    return jnp.where(east, tend_u, 0.0), jnp.where(north, tend_v, 0.0)


def coriolis(rows, offset):
    return coriolis_base * (0.5 + (rows.astype(f32) + offset) / NLAT)


def send_kernel(
    place_ref, even_ref, own_ref, first_ref, second_ref, _,
    out_ref, split_ref, stack_ref, edge_ref, turned_ref, west_ref, east_ref,
):
    place = place_ref[0]
    sort_sides(even_ref, first_ref, second_ref, west_ref, east_ref)
    c = tracer_planes(own_ref)
    p_own = pressures(c[1], c[0])

    def whole(own, plane):
        return wide(own, beside_plane(west_ref, east_ref, plane))

    shape = (ROWS, 2 * COLS)
    row = ids(shape, 0)
    bottom = whole(own_ref[OWN_BOTTOM], BOTTOM)
    wind = [whole(own_ref[OWN_WIND + d], WIND + d) for d in range(2)]

    def up(x):
        return jnp.where(row == ROWS - 1, 0.0, at(x, 1, 0))

    def down(x):
        return jnp.where(row == 0, 0.0, at(x, -1, 0))

    count_u = jnp.minimum(bottom, at(bottom, 1, 1))
    count_v = jnp.minimum(bottom, up(bottom))
    f_u = coriolis(place * ROWS + row, 0.5)
    f_v = coriolis(place * ROWS + row, 1.0)
    sums = [jnp.zeros(shape, f32) for _ in range(4)]
    us, vs, raws = [], [], []
    for k in range(LEVELS):
        east, north = count_u > k, count_v > k
        u = jnp.where(east, whole(own_ref[OWN_EAST + k], EAST + k), 0.0)
        raw = jnp.where(bottom > k, whole(own_ref[OWN_NORTH + k], NORTH + k), 0.0)
        v = jnp.where(north, raw, 0.0)
        p = whole(p_own[k], PRESSURE + k)
        tend_u, tend_v = momentum(k, u, v, p, wind, east, north, f_u, f_v, up, down)
        sums = [a + b for a, b in zip(sums, (u, v, tend_u, tend_v))]
        us.append(u)
        vs.append(v)
        raws.append(raw)
        pair = u + at(u, -1, 1)
        last = p[8:] + (-0.25 * f_v[8:]) * pair[8:] + viscosity * at(v, -1, 0)[8:]
        if k == 0:
            last = last + wind[1][8:]
        first = (-0.25 * (f_v[:8] - 1.0 / NLAT)) * pair[:8] - p[:8] + viscosity * v[:8]
        edge_ref[k : k + 1] = u[15:16]
        edge_ref[8 + k : 9 + k] = raw[15:16]
        edge_ref[16 + k : 17 + k] = last[7:8]
        edge_ref[24 + k : 25 + k] = u[0:1]
        edge_ref[32 + k : 33 + k] = first[0:1]
    surface = whole(own_ref[OWN_SURFACE], SURFACE)
    for n, values in enumerate((surface, *sums, bottom)):
        split_ref[ROWS * n : ROWS * (n + 1)] = values[:, :COLS]
        split_ref[ROWS * (6 + n) : ROWS * (7 + n)] = values[:, COLS:]
    for q in range(16):
        spot = pl.multiple_of(lax.rem(q + place, 16) * 8, 8)
        for half in range(2):
            if q < 12:
                rows = split_ref[pl.ds(ROWS * (6 * half + q // 2) + q % 2, 8, 2), :]
            else:
                rows = edge_ref[8 * (q - 12) : 8 * (q - 11), COLS * half : COLS * (half + 1)]
            stack_ref[half, pl.ds(spot, 8)] = rows
    turned_ref[HALO : HALO + COLS] = stack_ref[0].T
    beyond = stack_ref[1].T
    turned_ref[:HALO] = beyond[COLS - HALO :]
    turned_ref[HALO + COLS :] = beyond[:HALO]
    edge = edge_ref[32:40]
    for d in range(MEMBERS):
        out_ref[d, :SLAB] = turned_ref[8 * d : 8 * d + SLAB]
        out_ref[d, EDGE:CHUNK] = at(edge, 8 * d - HALO, 1)[:, :COLS]

    sub = ids((8, COLS), 0)

    def spare(n):
        t, k = divmod(n, LEVELS)
        if t == 0:
            return us[k][:, :COLS], us[k][:, :COLS]
        if t == 1:
            return raws[k][:, :COLS], vs[k][:, :COLS]
        if t == 2:
            return raws[k][:, COLS:], us[k][:, COLS:]
        if k < 2:
            own = bottom[:, COLS * k : COLS * (k + 1)]
            return own, own
        return None

    def tops(n):
        own = c[n // LEVELS][n % LEVELS][8:]
        more = spare(n)
        return own if more is None else jnp.where(sub == 4, at(more[0][8:], 3, 0), own)

    def bottoms(n):
        own = c[n // LEVELS][n % LEVELS][:8]
        more = spare(n)
        return own if more is None else jnp.where(sub == 3, at(more[1][:8], -3, 0), own)

    for m in range(MEMBERS):
        out_ref[m, MAIL_N:MAIL_S] = jnp.where(sub >= 4, tops(2 * m), at(tops(2 * m + 1), 4, 0))
        out_ref[m, MAIL_S:EDGE] = jnp.where(sub < 4, bottoms(2 * m), at(bottoms(2 * m + 1), 4, 0))


def slab_kernel(in_ref, out_ref, edge_ref):
    shape = (SLAB, COLS)
    lane = ids(shape, 1)
    r = lane % 8
    block = ids((8, COLS), 1) // 8

    tiles = []
    for t in range(SLAB // 8):
        now = [in_ref[a, 8 * t : 8 * t + 8] for a in range(MEMBERS)]
        for bit in (1, 2, 4, 8):
            odd = (block & bit) > 0
            now = [jnp.where(odd, now[(a + bit) % MEMBERS], now[a]) for a in range(MEMBERS)]
        tiles.append([at(now[-q % MEMBERS], 8 * q, 1) for q in range(16)])
    blocks = [jnp.concatenate([tile[q] for tile in tiles], axis=0) for q in range(16)]
    surface, start_u, start_v, force_u, force_v, bottom = (blocks[2 * n : 2 * n + 2] for n in range(6))
    u_a, v_raw, near, u_next = blocks[12:]
    zeros = jnp.zeros((8, COLS), f32)
    for a in range(MEMBERS):
        edge_ref[8 * a : 8 * a + 8] = in_ref[a + 1, EDGE:CHUNK] if a < MEMBERS - 1 else zeros
    far = edge_ref[...].T[:SLAB]

    top = lane == COLS - 1
    count_u = [jnp.minimum(b, at(b, 1, 0)) for b in bottom]
    count_v = [
        jnp.minimum(*bottom),
        jnp.where(top, 0.0, jnp.minimum(bottom[1], at(bottom[0], 1, 1))),
    ]

    ahead = jnp.concatenate([count_u[0], count_v[0]], axis=0)
    first = (ids(ahead.shape, 1) % 8 == 0) & (ids(ahead.shape, 1) > 0)
    counts = jnp.concatenate(
        [
            jnp.where(r == 7, count_u[1], 0.0),
            jnp.where(r == 7, count_v[1], 0.0),
            jnp.where(r == 7, count_v[0], 0.0),
            at(jnp.where(first, ahead, 0.0), 1, 1),
        ],
        axis=0,
    )
    for step in (1, 2, 4):
        counts = counts + at(counts, step, 1)
    count_ua, count_va, count_vc, count_ub, count_vb = (
        counts[SLAB * n : SLAB * (n + 1)] for n in range(5)
    )
    level = r.astype(f32)
    last = lane >= COLS - 8
    v_a = jnp.where(count_va > level, v_raw, 0.0)
    u_a = jnp.where(last, 0.0, u_a)
    u_b = jnp.where(last, 0.0, at(u_next, 8, 1))
    f_a = 0.25 * coriolis(lane // 8 * ROWS + 15, 0.5)
    f_b = f_a + 0.25 * coriolis_base / NLAT
    pair = v_a + at(v_a, 1, 0)
    spread = viscosity * (at(v_a, 1, 0) + at(v_a, -1, 0) - 4.0 * v_a)
    terms = jnp.concatenate(
        [
            jnp.where(count_ua > level, f_a * pair + viscosity * u_b, 0.0),
            jnp.where(count_ub > level, f_b * pair + viscosity * u_a, 0.0),
            jnp.where(count_vb > level, viscosity * v_a, 0.0),
            jnp.where(count_vc > level, viscosity * v_a, 0.0),
            jnp.where(count_va > level, near + far + spread, 0.0),
            v_a,
        ],
        axis=0,
    )
    for step in (1, 2, 4):
        terms = terms + at(terms, -step, 1)
    shifted = at(terms[SLAB : 3 * SLAB], -1, 1)
    u_15, v_14, v_15, begin_15 = (
        jnp.where(r == 7, terms[SLAB * n : SLAB * (n + 1)], 0.0) for n in (0, 3, 4, 5)
    )
    u_16, v_16 = (jnp.where(r == 0, shifted[SLAB * n : SLAB * (n + 1)], 0.0) for n in range(2))
    force_u = [force_u[0] + u_16, force_u[1] + u_15]
    force_v = [force_v[0] + (v_14 + v_16), force_v[1] + v_15]
    start_v = [start_v[0], start_v[1] + begin_15]

    sub_step = time_step / SUBSTEPS
    held_u, held_v, flux_u, flux_v, begin_u, begin_v = [], [], [], [], [], []
    for i in range(2):
        per = 1.0 / jnp.maximum(count_u[i], 1.0)
        open_face = jnp.where(count_u[i] > 0.0, sub_step, 0.0)
        flux_u.append((sub_step * surface_scale * thickness) * count_u[i])
        held_u.append(
            (
                (0.25 * open_face) * coriolis(2 * lane + i, 0.5),
                gravity * open_face,
                open_face * (force_u[i] * per),
            )
        )
        begin_u.append(start_u[i] * per)
        per = 1.0 / jnp.maximum(count_v[i], 1.0)
        open_face = jnp.where(count_v[i] > 0.0, sub_step, 0.0)
        flux_v.append((sub_step * surface_scale * thickness) * count_v[i])
        held_v.append(
            (
                (-0.25 * open_face) * coriolis(2 * lane + i, 1.0),
                gravity * open_face,
                open_face * (force_v[i] * per),
            )
        )
        begin_v.append(start_v[i] * per)
    held = (
        *flux_u, at(flux_u[0], 1, 1), *flux_v, at(flux_v[0], 1, 1), at(flux_v[1], -1, 1),
        *held_u[0], *held_u[1], *held_v[0], *held_v[1],
    )
    state = (*surface, at(surface[0], 1, 1), *begin_u, *begin_v)
    total = (zeros,) * 4
    for low, steps in ((0, 6), (8, 8), (16, 8), (24, 8)):
        cut = 8 if low else 0
        state = tuple(x[cut : x.shape[0] - cut] for x in state)
        (
            du0, du1, du2, dv0, dv1, dv2, dv_, cu0, gu0, fu0, cu1, gu1, fu1,
            cv0, gv0, fv0, cv1, gv1, fv1,
        ) = (x[low : SLAB - low] for x in held)
        centre = HALO - low

        def advance(_, carry):
            h0, h1, h2, u0, u1, v0, v1, *sums = carry
            v_ = at(v1, -1, 1)
            u2 = at(u0, 1, 1)
            v2 = at(v0, 1, 1)
            x0, x1, x2 = du0 * u0, du1 * u1, du2 * u2
            y0, y1 = dv0 * v0, dv1 * v1
            h1 = h1 - ((x1 - at(x1, -1, 0)) + (y1 - y0))
            h0 = h0 - ((x0 - at(x0, -1, 0)) + (y0 - dv_ * v_))
            h2 = h2 - ((x2 - at(x2, -1, 0)) + (dv2 * v2 - y1))
            p0, p1, p2 = u0 + at(u0, -1, 0), u1 + at(u1, -1, 0), u2 + at(u2, -1, 0)
            q0, q1 = v0 + v_, v1 + v0
            u0 = (u0 + fu0) + (cu0 * (q0 + at(q0, 1, 0)) - gu0 * (at(h0, 1, 0) - h0))
            u1 = (u1 + fu1) + (cu1 * (q1 + at(q1, 1, 0)) - gu1 * (at(h1, 1, 0) - h1))
            v0 = (v0 + fv0) + (cv0 * (p0 + p1) - gv0 * (h1 - h0))
            v1 = (v1 + fv1) + (cv1 * (p1 + p2) - gv1 * (h2 - h1))
            sums = [a + b[centre : centre + 8] for a, b in zip(sums, (u0, u1, v0, v1))]
            return (h0, h1, h2, u0, u1, v0, v1, *sums)

        *state, a0, a1, a2, a3 = lax.fori_loop(
            0, steps, advance, (*state, *total), unroll=True
        )
        total = (a0, a1, a2, a3)
    height = [x[8:16] for x in state[:2]]
    average = [x * (1.0 / SUBSTEPS) for x in total]
    transport = [
        (-thickness * count_u[i][HALO : HALO + 8]) * average[i] for i in range(2)
    ]
    square = (COLS, COLS)
    before = (ids(square, 0) < ids(square, 1)).astype(f32)
    south = jnp.dot(
        transport[0] + transport[1],
        before,
        precision=lax.Precision.HIGHEST,
        preferred_element_type=f32,
    )
    stream = [south + transport[0], south + (transport[0] + transport[1])]
    results = [*height, *stream, *average]
    moved = [at(values, -8 * n, 1) for n, values in enumerate(results)]
    for e in range(MEMBERS):
        packed = moved[0]
        for n in range(1, 8):
            packed = jnp.where(block == (e + n) % 16, moved[n], packed)
        out_ref[e, 0:8] = packed
        out_ref[e, 8:16] = in_ref[(e + 15) % MEMBERS, MAIL_N:MAIL_S]
        out_ref[e, 16:24] = in_ref[(e + 1) % MEMBERS, MAIL_S:EDGE]


def gain(values, axis, flow, diffusion):
    ahead = at(values, 1, axis)
    sides = at(values, -1, axis) + at(values, 2, axis)
    far = at(values, -2, axis) + at(values, 3, axis)
    face = (37.0 * (values + ahead) - 8.0 * sides + far) * (1.0 / 60.0)
    flux = diffusion * (ahead - values) - flow * face
    return flux - at(flux, -1, axis)


def inner_kernel(own_ref, out_ref):
    bottom = own_ref[OWN_BOTTOM]
    c = tracer_planes(own_ref)
    count = jnp.minimum(bottom, at(bottom, 1, 1))
    values = jnp.concatenate([plane for tracer in c for plane in tracer], axis=0)
    flow, diffusion = [], []
    for k in range(LEVELS):
        flow.append(jnp.where(count > k, own_ref[OWN_EAST + k], 0.0))
        diffusion.append(jnp.where(count > k, tracer_diffusion, 0.0))
    flow, diffusion = (jnp.concatenate(x * TRACERS, axis=0) for x in (flow, diffusion))
    lane = ids(values.shape, 1)

    def moved(step):
        inside = lane < COLS - step if step > 0 else lane >= -step
        return jnp.where(inside, at(values, step, 1), 0.0)

    ahead = moved(1)
    face = (37.0 * (values + ahead) - 8.0 * (moved(-1) + moved(2)) + (moved(-2) + moved(3))) * (
        1.0 / 60.0
    )
    flux = jnp.where(lane < COLS - 1, diffusion * (ahead - values) - flow * face, 0.0)
    out_ref[...] = flux - at(flux, -1, 1)


def outer(west, east, left, right, flow_w, flow_l, flow_r, diff_w, diff_r):
    q = ids((ROWS, COLS), 1) % 4
    sixtieth = 1.0 / 60.0
    w1, w2, w3 = at(west, 3, 1), at(west, 2, 1), at(west, 1, 1)
    face = 37.0 * (w1 + left) - 8.0 * (w2 + at(left, 1, 1)) + (w3 + at(left, 2, 1))
    through = at(diff_w, 3, 1) * (left - w1) - at(flow_w, 3, 1) * (face * sixtieth)
    flux = jnp.where(q == 0, w2 - 8.0 * w1, jnp.where(q == 1, w2, 0.0)) * (-sixtieth) * flow_l
    low = flux - at(flux, -1, 1) - jnp.where(q == 0, through, 0.0)
    e1, e2, e3 = at(east, -3, 1), at(east, -2, 1), at(east, -1, 1)
    face = 37.0 * (right + e1) - 8.0 * (at(right, -1, 1) + e2) + (at(right, -2, 1) + e3)
    through = diff_r * (e1 - right) - flow_r * (face * sixtieth)
    flux = jnp.where(q == 2, e3 - 8.0 * e2, jnp.where(q == 1, e3, 0.0)) * (-sixtieth) * flow_r
    high = flux - at(flux, -1, 1) + jnp.where(q == 3, through, 0.0)
    return low, high


def finish_kernel(
    place_ref, even_ref, in_ref, own_ref, first_ref, second_ref, one_ref, two_ref, inner_ref,
    tracers_out, velocity_out, height_out, stream_out, turned_ref, rows_ref, west_ref, east_ref,
):
    place = place_ref[0]
    sort_sides(even_ref, first_ref, second_ref, west_ref, east_ref)
    turned_ref[...] = in_ref[:, 0:8].reshape(COLS, COLS).T

    for q in range(8):
        spot = pl.multiple_of(lax.rem(q + place, 16) * 8, 8)
        rows_ref[pl.ds(ROWS * (q // 2) + q % 2, 8, 2), :] = turned_ref[pl.ds(spot, 8)]
    height_out[...] = rows_ref[:ROWS]
    stream_out[...] = rows_ref[ROWS : 2 * ROWS]
    average_u, average_v = rows_ref[2 * ROWS : 3 * ROWS], rows_ref[3 * ROWS :]

    sub = ids((8, COLS), 0)
    tall = (ROWS + 8, 2 * COLS)
    row = ids(tall, 0)
    first, last = place == 0, place == MEMBERS - 1

    def lat_tile(n):
        south = jnp.where(first, 0.0, in_ref[n // 2, 8:16])
        north = jnp.where(last, 0.0, in_ref[n // 2, 16:24])
        if n % 2 == 0:
            return jnp.where(sub < 4, north, south)
        return at(jnp.where(sub < 4, south, north), 4, 0)

    def spare_north(tile):
        return jnp.where(sub == 0, at(tile, 3, 0), 0.0)

    def spare_south(tile):
        return jnp.where(sub == 7, at(tile, -3, 0), 0.0)

    def tallen(own, tile):
        return jnp.concatenate([own, tile], axis=0)

    def whole(own, plane):
        return wide(own, beside_plane(west_ref, east_ref, plane))

    tiles = [[lat_tile(LEVELS * t + k) for k in range(LEVELS)] for t in range(TRACERS)]
    bottom_own = own_ref[OWN_BOTTOM]
    c = tracer_planes(own_ref)
    p_own = pressures(c[1], c[0])
    p_tile = pressures(tiles[1], tiles[0])
    both = wide(
        spare_north(tiles[3][0]) + spare_south(tiles[3][0]),
        spare_north(tiles[3][1]) + spare_south(tiles[3][1]),
    )
    bottom = tallen(whole(bottom_own, BOTTOM), both)
    count_u = jnp.minimum(bottom, at(bottom, 1, 1))
    count_v = jnp.minimum(bottom, at(bottom, 1, 0))
    f_u = coriolis(place * ROWS + row, 0.5)
    f_v = coriolis(place * ROWS + row, 1.0)
    none = jnp.zeros((8, COLS), f32)
    wind = [tallen(wide(own_ref[OWN_WIND + d], jnp.zeros((ROWS, COLS), f32)), jnp.zeros((8, 2 * COLS), f32)) for d in range(2)]

    def up(x):
        return at(x, 1, 0)

    def down(x):
        return at(x, -1, 0)

    stars_u, stars_v, flows, gains = [], [], [], [None] * (TRACERS * LEVELS)
    own_u, own_v = count_u[:ROWS, :COLS], count_v[:ROWS, :COLS]
    mean_u = mean_v = jnp.zeros((ROWS, COLS), f32)
    for k in range(LEVELS):
        east, north = count_u > k, count_v > k
        t0, t1, t2 = tiles[0][k], tiles[1][k], tiles[2][k]
        u_lat = wide(spare_north(t0) + spare_south(t0), spare_north(t2))
        v_lat = wide(spare_north(t1) + spare_south(t1), spare_south(t2))
        u = tallen(whole(own_ref[OWN_EAST + k], EAST + k), u_lat)
        u = jnp.where(east | (row >= ROWS), u, 0.0)
        v = tallen(whole(own_ref[OWN_NORTH + k], NORTH + k), v_lat)
        v = jnp.where(north | (row == ROWS), v, 0.0)
        p = tallen(whole(p_own[k], PRESSURE + k), wide(p_tile[k], none))
        tend_u, tend_v = momentum(k, u, v, p, wind, east, north, f_u, f_v, up, down)
        star_u = (u + time_step * tend_u)[:ROWS, :COLS]
        star_v = (v + time_step * tend_v)[:ROWS, :COLS]
        stars_u.append(star_u)
        stars_v.append(star_v)
        mean_u = mean_u + star_u
        mean_v = mean_v + star_v

        flows.append((u[:ROWS], jnp.where(east[:ROWS], tracer_diffusion, 0.0)))
        diffusion = jnp.where(north[:, :COLS], tracer_diffusion, 0.0)
        for t in range(TRACERS):
            cn = tallen(c[t][k], tiles[t][k])
            gains[LEVELS * t + k] = gain(cn, 0, v[:, :COLS], diffusion)[:ROWS]
    block = ids((ROWS, COLS), 1) // 4

    def packed(which, half, ahead):
        tile = jnp.zeros((ROWS, COLS), f32)
        for k in range(LEVELS):
            values = flows[k][which][:, COLS * half : COLS * (half + 1)]
            tile = jnp.where(block % LEVELS == k, at(values, -4 * (k + ahead), 1), tile)
        for step in (32, 64):
            tile = jnp.where(block * 4 % (2 * step) < step, tile, at(tile, -step, 1))
        return tile

    last = PLANES // 4
    even = even_ref[0] > 0
    left = jnp.where(even, two_ref[last], one_ref[last])
    right = jnp.where(even, one_ref[last], two_ref[last])
    low, high = outer(
        at(west_ref[last], -4, 1), east_ref[last], left, at(right, -4, 1),
        packed(0, 1, 1), packed(0, 0, 0), packed(0, 0, 1), packed(1, 1, 1), packed(1, 0, 1),
    )
    high = at(high, 4, 1)
    planes = range(TRACERS * LEVELS)
    sides = [
        at(jnp.where(block == n, low, jnp.where(block == (n + 31) % 32, high, 0.0)), 4 * n, 1)
        for n in planes
    ]
    for n in planes:
        t, k = divmod(n, LEVELS)
        change = inner_ref[ROWS * n : ROWS * (n + 1)] + sides[n] + gains[n]
        tracers_out[t, k] = jnp.where(bottom_own > k, c[t][k] + time_step * change, 0.0)
    shift_u = average_u - mean_u / jnp.maximum(own_u, 1.0)
    shift_v = average_v - mean_v / jnp.maximum(own_v, 1.0)
    for k in range(LEVELS):
        velocity_out[0, k] = jnp.where(own_u > k, stars_u[k] + shift_u, 0.0)
        velocity_out[1, k] = jnp.where(own_v > k, stars_v[k] + shift_v, 0.0)


def swaps(axis, first):
    count = lax.axis_size(axis)
    pairs = [((i + first) % count, (i + first + 1) % count) for i in range(0, count, 2)]
    return pairs + [(b, a) for a, b in pairs]


def struct(*shape):
    return jax.ShapeDtypeStruct(shape, f32)


def vmem(*shape):
    return pltpu.VMEM(shape, f32)


def specs(count, scalars=0):
    return [pl.BlockSpec(memory_space=pltpu.SMEM)] * scalars + [
        pl.BlockSpec(memory_space=pltpu.VMEM)
    ] * count


PARAMS = pltpu.CompilerParams(vmem_limit_bytes=32 * 1024 * 1024)


def stacked(tracers, velocity, surface, wind, bottom):
    def put(values, first):
        values = values.reshape(-1, ROWS, COLS)
        after = OWN - first - values.shape[0]
        return lax.pad(
            values, jnp.zeros((), values.dtype), ((first, after, 0), (0, 0, 0), (0, 0, 0))
        )

    return (
        put(tracers, 0)
        + put(velocity, OWN_EAST)
        + put(surface, OWN_SURFACE)
        + put(wind, OWN_WIND)
        + put(bottom, OWN_BOTTOM).astype(f32)
    )


def shards(tracers, velocity, surface, wind, bottom):
    place = lax.axis_index("lat").astype(jnp.int32).reshape(1)
    even = (1 - lax.axis_index("lon") % 2).astype(jnp.int32).reshape(1)
    own = stacked(tracers, velocity, surface, wind, bottom)
    payload = struct(PLANES // 4 + 1, ROWS, COLS)
    one, two = pl.pallas_call(
        pack_kernel,
        out_shape=(payload, payload),
        in_specs=specs(1, 1),
        out_specs=tuple(specs(2)),
        compiler_params=PARAMS,
        name="pack",
    )(even, own)
    second = lax.ppermute(two, "lon", swaps("lon", 1))
    first = lax.ppermute(one, "lon", swaps("lon", 0))
    inner = pl.pallas_call(
        inner_kernel,
        out_shape=struct(TRACERS * LEVELS * ROWS, COLS),
        in_specs=specs(1),
        out_specs=specs(1)[0],
        compiler_params=PARAMS,
        cost_estimate=pl.CostEstimate(flops=1500000, bytes_accessed=3000000, transcendentals=0),
        name="inner",
    )(own)
    chunks = pl.pallas_call(
        send_kernel,
        out_shape=struct(MEMBERS, CHUNK, COLS),
        in_specs=specs(3, 2) + [pl.BlockSpec(memory_space=pl.ANY)],
        out_specs=specs(1)[0],
        scratch_shapes=[
            vmem(12 * ROWS, COLS),
            vmem(2, COLS, COLS),
            vmem(40, 2 * COLS),
            vmem(COLS + 2 * HALO, COLS),
            vmem(PLANES // 4 + 1, ROWS, COLS),
            vmem(PLANES // 4 + 1, ROWS, COLS),
        ],
        compiler_params=PARAMS,
        name="columns",
    )(place, even, own, first, second, inner)
    slabs = lax.all_to_all(chunks, "lat", 0, 0, tiled=True)
    answers = pl.pallas_call(
        slab_kernel,
        out_shape=struct(MEMBERS, BACK, COLS),
        in_specs=specs(1),
        out_specs=specs(1)[0],
        scratch_shapes=[vmem(COLS, COLS)],
        compiler_params=PARAMS,
        name="substeps",
    )(slabs)
    home = lax.all_to_all(answers, "lat", 0, 0, tiled=True)
    return pl.pallas_call(
        finish_kernel,
        out_shape=(
            struct(TRACERS, LEVELS, ROWS, COLS),
            struct(2, LEVELS, ROWS, COLS),
            struct(ROWS, COLS),
            struct(ROWS, COLS),
        ),
        in_specs=specs(7, 2),
        out_specs=tuple(specs(4)),
        scratch_shapes=[
            vmem(COLS, COLS),
            vmem(4 * ROWS, COLS),
            vmem(PLANES // 4 + 1, ROWS, COLS),
            vmem(PLANES // 4 + 1, ROWS, COLS),
        ],
        compiler_params=PARAMS,
        name="finish",
    )(place, even, home, own, first, second, one, two, inner)


def solution(mesh):
    placed = (
        P(None, None, "lat", "lon"),
        P(None, None, "lat", "lon"),
        P("lat", "lon"),
        P(None, "lat", "lon"),
        P("lat", "lon"),
    )
    return jax.shard_map(
        shards,
        mesh=mesh,
        in_specs=placed,
        out_specs=(
            P(None, None, "lat", "lon"),
            P(None, None, "lat", "lon"),
            P("lat", "lon"),
            P("lat", "lon"),
        ),
        check_vma=False,
    )
```

```python
import jax
import jax.numpy as jnp
from jax import lax
from jax.experimental import pallas as pl
from jax.experimental.pallas import tpu as pltpu
from jax.sharding import PartitionSpec as P

TRACERS = 4
LEVELS = 8
SUBSTEPS = 30
ROWS = 16
COLS = 128
MEMBERS = 16
HALO = 32
SLAB = 72
NLAT = ROWS * MEMBERS

time_step = 0.2
tracer_diffusion = 0.2
viscosity = 0.2
thermal_expansion = 2.0
haline_contraction = 1.5
coriolis_base = 1.0
gravity = 140.0
surface_scale = 40.0
thickness = 1.0 / LEVELS
f32 = jnp.float32

PRESSURE, EAST, NORTH, WIND, SURFACE, BOTTOM = 0, 8, 16, 24, 26, 27
PLANES = 28
OWN_EAST, OWN_NORTH, OWN_SURFACE, OWN_WIND, OWN_BOTTOM, OWN = 32, 40, 48, 49, 51, 52
MAIL_N, MAIL_S, EDGE, CHUNK = SLAB, SLAB + 8, SLAB + 16, SLAB + 24
BACK = 24


def at(values, step, axis):
    size = values.shape[axis]
    step %= size
    return values if step == 0 else pltpu.roll(values, size - step, axis)


def ids(shape, axis):
    return lax.broadcasted_iota(jnp.int32, shape, axis)


def wide(own, beside):
    return jnp.concatenate([own, beside], axis=1)


def tracer_planes(own_ref):
    bottom = own_ref[OWN_BOTTOM]
    return [
        [jnp.where(bottom > k, own_ref[LEVELS * t + k], 0.0) for k in range(LEVELS)]
        for t in range(TRACERS)
    ]


def pressures(salt, heat):
    total, out = None, []
    for k in range(LEVELS):
        density = haline_contraction * salt[k] - thermal_expansion * heat[k]
        total = density if total is None else total + density
        out.append(thickness * total)
    return out


def pack_kernel(own_ref, right_ref, left_ref):
    c = tracer_planes(own_ref)
    planes = pressures(c[1], c[0])
    planes += [own_ref[n] for n in range(OWN_EAST, OWN_SURFACE)]
    planes += [own_ref[n] for n in (OWN_WIND, OWN_WIND + 1, OWN_SURFACE, OWN_BOTTOM)]
    lane = ids((ROWS, COLS), 1)
    for q in range(PLANES // 4):
        right = left = jnp.zeros((ROWS, COLS), f32)
        for s in range(4):
            moved = at(planes[4 * q + s], -32 * s, 1)
            right = jnp.where(lane // 32 == (s + 3) % 4, moved, right)
            left = jnp.where(lane // 32 == s, moved, left)
        right_ref[q] = right
        left_ref[q] = left
    right = left = jnp.zeros((ROWS, COLS), f32)
    for n in range(TRACERS * LEVELS):
        moved = at(c[n // LEVELS][n % LEVELS], -4 * n, 1)
        right = jnp.where(lane // 4 == (n + 31) % 32, moved, right)
        left = jnp.where(lane // 4 == n, moved, left)
    right_ref[PLANES // 4] = right
    left_ref[PLANES // 4] = left


def beside_plane(west_ref, east_ref, plane):
    q, s = divmod(plane, 4)
    block = ids((ROWS, COLS), 1) // 32
    both = jnp.where(
        block == s, east_ref[q], jnp.where(block == (s + 3) % 4, west_ref[q], 0.0)
    )
    return at(both, 32 * s, 1)


def momentum(k, u, v, p, wind, east, north, f_u, f_v, up, down):
    pair_v = v + down(v)
    pair_u = u + at(u, -1, 1)
    tend_u = (
        (0.25 * f_u) * (pair_v + at(pair_v, 1, 1))
        - (at(p, 1, 1) - p)
        + viscosity * (at(u, 1, 1) + at(u, -1, 1) + up(u) + down(u) - 4.0 * u)
    )
    tend_v = (
        (-0.25 * f_v) * (pair_u + up(pair_u))
        - (up(p) - p)
        + viscosity * (at(v, 1, 1) + at(v, -1, 1) + up(v) + down(v) - 4.0 * v)
    )
    if k == 0:
        tend_u = tend_u + wind[0]
        tend_v = tend_v + wind[1]
    return jnp.where(east, tend_u, 0.0), jnp.where(north, tend_v, 0.0)


def coriolis(rows, offset):
    return coriolis_base * (0.5 + (rows.astype(f32) + offset) / NLAT)


def send_kernel(
    place_ref, own_ref, west_ref, east_ref, right_ref, left_ref, inner_ref,
    out_ref, along_ref, split_ref, stack_ref, edge_ref, turned_ref,
):
    place = place_ref[0]
    c = tracer_planes(own_ref)
    p_own = pressures(c[1], c[0])

    def whole(own, plane):
        return wide(own, beside_plane(west_ref, east_ref, plane))

    shape = (ROWS, 2 * COLS)
    row = ids(shape, 0)
    bottom = whole(own_ref[OWN_BOTTOM], BOTTOM)
    wind = [whole(own_ref[OWN_WIND + d], WIND + d) for d in range(2)]

    def up(x):
        return jnp.where(row == ROWS - 1, 0.0, at(x, 1, 0))

    def down(x):
        return jnp.where(row == 0, 0.0, at(x, -1, 0))

    count_u = jnp.minimum(bottom, at(bottom, 1, 1))
    count_v = jnp.minimum(bottom, up(bottom))
    f_u = coriolis(place * ROWS + row, 0.5)
    f_v = coriolis(place * ROWS + row, 1.0)
    sums = [jnp.zeros(shape, f32) for _ in range(4)]
    us, vs, raws = [], [], []
    for k in range(LEVELS):
        east, north = count_u > k, count_v > k
        u = jnp.where(east, whole(own_ref[OWN_EAST + k], EAST + k), 0.0)
        raw = jnp.where(bottom > k, whole(own_ref[OWN_NORTH + k], NORTH + k), 0.0)
        v = jnp.where(north, raw, 0.0)
        p = whole(p_own[k], PRESSURE + k)
        tend_u, tend_v = momentum(k, u, v, p, wind, east, north, f_u, f_v, up, down)
        sums = [a + b for a, b in zip(sums, (u, v, tend_u, tend_v))]
        us.append(u)
        vs.append(v)
        raws.append(raw)
        pair = u + at(u, -1, 1)
        last = p[8:] + (-0.25 * f_v[8:]) * pair[8:] + viscosity * at(v, -1, 0)[8:]
        if k == 0:
            last = last + wind[1][8:]
        first = (-0.25 * (f_v[:8] - 1.0 / NLAT)) * pair[:8] - p[:8] + viscosity * v[:8]
        edge_ref[k : k + 1] = u[15:16]
        edge_ref[8 + k : 9 + k] = raw[15:16]
        edge_ref[16 + k : 17 + k] = last[7:8]
        edge_ref[24 + k : 25 + k] = u[0:1]
        edge_ref[32 + k : 33 + k] = first[0:1]
    surface = whole(own_ref[OWN_SURFACE], SURFACE)
    for n, values in enumerate((surface, *sums, bottom)):
        split_ref[ROWS * n : ROWS * (n + 1)] = values[:, :COLS]
        split_ref[ROWS * (6 + n) : ROWS * (7 + n)] = values[:, COLS:]
    for q in range(16):
        spot = pl.multiple_of(lax.rem(q + place, 16) * 8, 8)
        for half in range(2):
            if q < 12:
                rows = split_ref[pl.ds(ROWS * (6 * half + q // 2) + q % 2, 8, 2), :]
            else:
                rows = edge_ref[8 * (q - 12) : 8 * (q - 11), COLS * half : COLS * (half + 1)]
            stack_ref[half, pl.ds(spot, 8)] = rows
    turned_ref[HALO : HALO + COLS] = stack_ref[0].T
    beyond = stack_ref[1].T
    turned_ref[:HALO] = beyond[COLS - HALO :]
    turned_ref[HALO + COLS :] = beyond[:HALO]
    edge = edge_ref[32:40]
    for d in range(MEMBERS):
        out_ref[d, :SLAB] = turned_ref[8 * d : 8 * d + SLAB]
        out_ref[d, EDGE:CHUNK] = at(edge, 8 * d - HALO, 1)[:, :COLS]

    block = ids((ROWS, COLS), 1) // 4
    flows = [(us[k], jnp.where(count_u > k, tracer_diffusion, 0.0)) for k in range(LEVELS)]

    def packed(which, half, ahead):
        tile = jnp.zeros((ROWS, COLS), f32)
        for k in range(LEVELS):
            values = flows[k][which][:, COLS * half : COLS * (half + 1)]
            tile = jnp.where(block % LEVELS == k, at(values, -4 * (k + ahead), 1), tile)
        for step in (32, 64):
            tile = jnp.where(block * 4 % (2 * step) < step, tile, at(tile, -step, 1))
        return tile

    last = PLANES // 4
    low, high = outer(
        at(west_ref[last], -4, 1), east_ref[last], left_ref[last], at(right_ref[last], -4, 1),
        packed(0, 1, 1), packed(0, 0, 0), packed(0, 0, 1), packed(1, 1, 1), packed(1, 0, 1),
    )
    high = at(high, 4, 1)
    for n in range(TRACERS * LEVELS):
        both = jnp.where(block == n, low, jnp.where(block == (n + 31) % 32, high, 0.0))
        rows = slice(ROWS * n, ROWS * (n + 1))
        along_ref[rows] = inner_ref[rows] + at(both, 4 * n, 1)

    sub = ids((8, COLS), 0)

    def spare(n):
        t, k = divmod(n, LEVELS)
        if t == 0:
            return us[k][:, :COLS], us[k][:, :COLS]
        if t == 1:
            return raws[k][:, :COLS], vs[k][:, :COLS]
        if t == 2:
            return raws[k][:, COLS:], us[k][:, COLS:]
        if k < 2:
            own = bottom[:, COLS * k : COLS * (k + 1)]
            return own, own
        return None

    def tops(n):
        own = c[n // LEVELS][n % LEVELS][8:]
        more = spare(n)
        return own if more is None else jnp.where(sub == 4, at(more[0][8:], 3, 0), own)

    def bottoms(n):
        own = c[n // LEVELS][n % LEVELS][:8]
        more = spare(n)
        return own if more is None else jnp.where(sub == 3, at(more[1][:8], -3, 0), own)

    for m in range(MEMBERS):
        out_ref[m, MAIL_N:MAIL_S] = jnp.where(sub >= 4, tops(2 * m), at(tops(2 * m + 1), 4, 0))
        out_ref[m, MAIL_S:EDGE] = jnp.where(sub < 4, bottoms(2 * m), at(bottoms(2 * m + 1), 4, 0))


def slab_kernel(in_ref, out_ref, edge_ref):
    shape = (SLAB, COLS)
    lane = ids(shape, 1)
    r = lane % 8
    block = ids((8, COLS), 1) // 8

    tiles = []
    for t in range(SLAB // 8):
        now = [in_ref[a, 8 * t : 8 * t + 8] for a in range(MEMBERS)]
        for bit in (1, 2, 4, 8):
            odd = (block & bit) > 0
            now = [jnp.where(odd, now[(a + bit) % MEMBERS], now[a]) for a in range(MEMBERS)]
        tiles.append([at(now[-q % MEMBERS], 8 * q, 1) for q in range(16)])
    blocks = [jnp.concatenate([tile[q] for tile in tiles], axis=0) for q in range(16)]
    surface, start_u, start_v, force_u, force_v, bottom = (blocks[2 * n : 2 * n + 2] for n in range(6))
    u_a, v_raw, near, u_next = blocks[12:]
    zeros = jnp.zeros((8, COLS), f32)
    for a in range(MEMBERS):
        edge_ref[8 * a : 8 * a + 8] = in_ref[a + 1, EDGE:CHUNK] if a < MEMBERS - 1 else zeros
    far = edge_ref[...].T[:SLAB]

    top = lane == COLS - 1
    count_u = [jnp.minimum(b, at(b, 1, 0)) for b in bottom]
    count_v = [
        jnp.minimum(*bottom),
        jnp.where(top, 0.0, jnp.minimum(bottom[1], at(bottom[0], 1, 1))),
    ]

    ahead = jnp.concatenate([count_u[0], count_v[0]], axis=0)
    first = (ids(ahead.shape, 1) % 8 == 0) & (ids(ahead.shape, 1) > 0)
    counts = jnp.concatenate(
        [
            jnp.where(r == 7, count_u[1], 0.0),
            jnp.where(r == 7, count_v[1], 0.0),
            jnp.where(r == 7, count_v[0], 0.0),
            at(jnp.where(first, ahead, 0.0), 1, 1),
        ],
        axis=0,
    )
    for step in (1, 2, 4):
        counts = counts + at(counts, step, 1)
    count_ua, count_va, count_vc, count_ub, count_vb = (
        counts[SLAB * n : SLAB * (n + 1)] for n in range(5)
    )
    level = r.astype(f32)
    last = lane >= COLS - 8
    v_a = jnp.where(count_va > level, v_raw, 0.0)
    u_a = jnp.where(last, 0.0, u_a)
    u_b = jnp.where(last, 0.0, at(u_next, 8, 1))
    f_a = 0.25 * coriolis(lane // 8 * ROWS + 15, 0.5)
    f_b = f_a + 0.25 * coriolis_base / NLAT
    pair = v_a + at(v_a, 1, 0)
    spread = viscosity * (at(v_a, 1, 0) + at(v_a, -1, 0) - 4.0 * v_a)
    terms = jnp.concatenate(
        [
            jnp.where(count_ua > level, f_a * pair + viscosity * u_b, 0.0),
            jnp.where(count_ub > level, f_b * pair + viscosity * u_a, 0.0),
            jnp.where(count_vb > level, viscosity * v_a, 0.0),
            jnp.where(count_vc > level, viscosity * v_a, 0.0),
            jnp.where(count_va > level, near + far + spread, 0.0),
            v_a,
        ],
        axis=0,
    )
    for step in (1, 2, 4):
        terms = terms + at(terms, -step, 1)
    shifted = at(terms[SLAB : 3 * SLAB], -1, 1)
    u_15, v_14, v_15, begin_15 = (
        jnp.where(r == 7, terms[SLAB * n : SLAB * (n + 1)], 0.0) for n in (0, 3, 4, 5)
    )
    u_16, v_16 = (jnp.where(r == 0, shifted[SLAB * n : SLAB * (n + 1)], 0.0) for n in range(2))
    force_u = [force_u[0] + u_16, force_u[1] + u_15]
    force_v = [force_v[0] + (v_14 + v_16), force_v[1] + v_15]
    start_v = [start_v[0], start_v[1] + begin_15]

    sub_step = time_step / SUBSTEPS
    held_u, held_v, flux_u, flux_v, begin_u, begin_v = [], [], [], [], [], []
    for i in range(2):
        per = 1.0 / jnp.maximum(count_u[i], 1.0)
        open_face = jnp.where(count_u[i] > 0.0, sub_step, 0.0)
        flux_u.append((sub_step * surface_scale * thickness) * count_u[i])
        held_u.append(
            (
                (0.25 * open_face) * coriolis(2 * lane + i, 0.5),
                gravity * open_face,
                open_face * (force_u[i] * per),
            )
        )
        begin_u.append(start_u[i] * per)
        per = 1.0 / jnp.maximum(count_v[i], 1.0)
        open_face = jnp.where(count_v[i] > 0.0, sub_step, 0.0)
        flux_v.append((sub_step * surface_scale * thickness) * count_v[i])
        held_v.append(
            (
                (-0.25 * open_face) * coriolis(2 * lane + i, 1.0),
                gravity * open_face,
                open_face * (force_v[i] * per),
            )
        )
        begin_v.append(start_v[i] * per)
    held = (
        *flux_u, at(flux_u[0], 1, 1), *flux_v, at(flux_v[0], 1, 1), at(flux_v[1], -1, 1),
        *held_u[0], *held_u[1], *held_v[0], *held_v[1],
    )
    state = (*surface, at(surface[0], 1, 1), *begin_u, *begin_v)
    total = (zeros,) * 4
    for low, steps in ((0, 6), (8, 8), (16, 8), (24, 8)):
        cut = 8 if low else 0
        state = tuple(x[cut : x.shape[0] - cut] for x in state)
        (
            du0, du1, du2, dv0, dv1, dv2, dv_, cu0, gu0, fu0, cu1, gu1, fu1,
            cv0, gv0, fv0, cv1, gv1, fv1,
        ) = (x[low : SLAB - low] for x in held)
        centre = HALO - low

        def advance(_, carry):
            h0, h1, h2, u0, u1, v0, v1, *sums = carry
            v_ = at(v1, -1, 1)
            u2 = at(u0, 1, 1)
            v2 = at(v0, 1, 1)
            x0, x1, x2 = du0 * u0, du1 * u1, du2 * u2
            y0, y1 = dv0 * v0, dv1 * v1
            h1 = h1 - ((x1 - at(x1, -1, 0)) + (y1 - y0))
            h0 = h0 - ((x0 - at(x0, -1, 0)) + (y0 - dv_ * v_))
            h2 = h2 - ((x2 - at(x2, -1, 0)) + (dv2 * v2 - y1))
            p0, p1, p2 = u0 + at(u0, -1, 0), u1 + at(u1, -1, 0), u2 + at(u2, -1, 0)
            q0, q1 = v0 + v_, v1 + v0
            u0 = (u0 + fu0) + (cu0 * (q0 + at(q0, 1, 0)) - gu0 * (at(h0, 1, 0) - h0))
            u1 = (u1 + fu1) + (cu1 * (q1 + at(q1, 1, 0)) - gu1 * (at(h1, 1, 0) - h1))
            v0 = (v0 + fv0) + (cv0 * (p0 + p1) - gv0 * (h1 - h0))
            v1 = (v1 + fv1) + (cv1 * (p1 + p2) - gv1 * (h2 - h1))
            sums = [a + b[centre : centre + 8] for a, b in zip(sums, (u0, u1, v0, v1))]
            return (h0, h1, h2, u0, u1, v0, v1, *sums)

        *state, a0, a1, a2, a3 = lax.fori_loop(
            0, steps, advance, (*state, *total), unroll=True
        )
        total = (a0, a1, a2, a3)
    height = [x[8:16] for x in state[:2]]
    average = [x * (1.0 / SUBSTEPS) for x in total]
    transport = [
        (-thickness * count_u[i][HALO : HALO + 8]) * average[i] for i in range(2)
    ]
    square = (COLS, COLS)
    before = (ids(square, 0) < ids(square, 1)).astype(f32)
    south = jnp.dot(
        transport[0] + transport[1],
        before,
        precision=lax.Precision.HIGHEST,
        preferred_element_type=f32,
    )
    stream = [south + transport[0], south + (transport[0] + transport[1])]
    results = [*height, *stream, *average]
    moved = [at(values, -8 * n, 1) for n, values in enumerate(results)]
    for e in range(MEMBERS):
        packed = moved[0]
        for n in range(1, 8):
            packed = jnp.where(block == (e + n) % 16, moved[n], packed)
        out_ref[e, 0:8] = packed
        out_ref[e, 8:16] = in_ref[(e + 15) % MEMBERS, MAIL_N:MAIL_S]
        out_ref[e, 16:24] = in_ref[(e + 1) % MEMBERS, MAIL_S:EDGE]


def gain(values, axis, flow, diffusion):
    ahead = at(values, 1, axis)
    sides = at(values, -1, axis) + at(values, 2, axis)
    far = at(values, -2, axis) + at(values, 3, axis)
    face = (37.0 * (values + ahead) - 8.0 * sides + far) * (1.0 / 60.0)
    flux = diffusion * (ahead - values) - flow * face
    return flux - at(flux, -1, axis)


def inner_kernel(own_ref, out_ref):
    bottom = own_ref[OWN_BOTTOM]
    c = tracer_planes(own_ref)
    count = jnp.minimum(bottom, at(bottom, 1, 1))
    values = jnp.concatenate([plane for tracer in c for plane in tracer], axis=0)
    flow, diffusion = [], []
    for k in range(LEVELS):
        flow.append(jnp.where(count > k, own_ref[OWN_EAST + k], 0.0))
        diffusion.append(jnp.where(count > k, tracer_diffusion, 0.0))
    flow, diffusion = (jnp.concatenate(x * TRACERS, axis=0) for x in (flow, diffusion))
    lane = ids(values.shape, 1)

    def moved(step):
        inside = lane < COLS - step if step > 0 else lane >= -step
        return jnp.where(inside, at(values, step, 1), 0.0)

    ahead = moved(1)
    face = (37.0 * (values + ahead) - 8.0 * (moved(-1) + moved(2)) + (moved(-2) + moved(3))) * (
        1.0 / 60.0
    )
    flux = jnp.where(lane < COLS - 1, diffusion * (ahead - values) - flow * face, 0.0)
    out_ref[...] = flux - at(flux, -1, 1)


def outer(west, east, left, right, flow_w, flow_l, flow_r, diff_w, diff_r):
    q = ids((ROWS, COLS), 1) % 4
    sixtieth = 1.0 / 60.0
    w1, w2, w3 = at(west, 3, 1), at(west, 2, 1), at(west, 1, 1)
    face = 37.0 * (w1 + left) - 8.0 * (w2 + at(left, 1, 1)) + (w3 + at(left, 2, 1))
    through = at(diff_w, 3, 1) * (left - w1) - at(flow_w, 3, 1) * (face * sixtieth)
    flux = jnp.where(q == 0, w2 - 8.0 * w1, jnp.where(q == 1, w2, 0.0)) * (-sixtieth) * flow_l
    low = flux - at(flux, -1, 1) - jnp.where(q == 0, through, 0.0)
    e1, e2, e3 = at(east, -3, 1), at(east, -2, 1), at(east, -1, 1)
    face = 37.0 * (right + e1) - 8.0 * (at(right, -1, 1) + e2) + (at(right, -2, 1) + e3)
    through = diff_r * (e1 - right) - flow_r * (face * sixtieth)
    flux = jnp.where(q == 2, e3 - 8.0 * e2, jnp.where(q == 1, e3, 0.0)) * (-sixtieth) * flow_r
    high = flux - at(flux, -1, 1) + jnp.where(q == 3, through, 0.0)
    return low, high


def finish_kernel(
    place_ref, in_ref, own_ref, west_ref, east_ref, along_ref,
    tracers_out, velocity_out, height_out, stream_out, turned_ref, rows_ref,
):
    place = place_ref[0]
    turned_ref[...] = in_ref[:, 0:8].reshape(COLS, COLS).T

    for q in range(8):
        spot = pl.multiple_of(lax.rem(q + place, 16) * 8, 8)
        rows_ref[pl.ds(ROWS * (q // 2) + q % 2, 8, 2), :] = turned_ref[pl.ds(spot, 8)]
    height_out[...] = rows_ref[:ROWS]
    stream_out[...] = rows_ref[ROWS : 2 * ROWS]
    average_u, average_v = rows_ref[2 * ROWS : 3 * ROWS], rows_ref[3 * ROWS :]

    sub = ids((8, COLS), 0)
    tall = (ROWS + 8, 2 * COLS)
    row = ids(tall, 0)
    first, last = place == 0, place == MEMBERS - 1

    def lat_tile(n):
        south = jnp.where(first, 0.0, in_ref[n // 2, 8:16])
        north = jnp.where(last, 0.0, in_ref[n // 2, 16:24])
        if n % 2 == 0:
            return jnp.where(sub < 4, north, south)
        return at(jnp.where(sub < 4, south, north), 4, 0)

    def spare_north(tile):
        return jnp.where(sub == 0, at(tile, 3, 0), 0.0)

    def spare_south(tile):
        return jnp.where(sub == 7, at(tile, -3, 0), 0.0)

    def tallen(own, tile):
        return jnp.concatenate([own, tile], axis=0)

    def whole(own, plane):
        return wide(own, beside_plane(west_ref, east_ref, plane))

    tiles = [[lat_tile(LEVELS * t + k) for k in range(LEVELS)] for t in range(TRACERS)]
    bottom_own = own_ref[OWN_BOTTOM]
    c = tracer_planes(own_ref)
    p_own = pressures(c[1], c[0])
    p_tile = pressures(tiles[1], tiles[0])
    both = wide(
        spare_north(tiles[3][0]) + spare_south(tiles[3][0]),
        spare_north(tiles[3][1]) + spare_south(tiles[3][1]),
    )
    bottom = tallen(whole(bottom_own, BOTTOM), both)
    count_u = jnp.minimum(bottom, at(bottom, 1, 1))
    count_v = jnp.minimum(bottom, at(bottom, 1, 0))
    f_u = coriolis(place * ROWS + row, 0.5)
    f_v = coriolis(place * ROWS + row, 1.0)
    none = jnp.zeros((8, COLS), f32)
    wind = [tallen(wide(own_ref[OWN_WIND + d], jnp.zeros((ROWS, COLS), f32)), jnp.zeros((8, 2 * COLS), f32)) for d in range(2)]

    def up(x):
        return at(x, 1, 0)

    def down(x):
        return at(x, -1, 0)

    stars_u, stars_v, gains = [], [], [None] * (TRACERS * LEVELS)
    own_u, own_v = count_u[:ROWS, :COLS], count_v[:ROWS, :COLS]
    mean_u = mean_v = jnp.zeros((ROWS, COLS), f32)
    for k in range(LEVELS):
        east, north = count_u > k, count_v > k
        t0, t1, t2 = tiles[0][k], tiles[1][k], tiles[2][k]
        u_lat = wide(spare_north(t0) + spare_south(t0), spare_north(t2))
        v_lat = wide(spare_north(t1) + spare_south(t1), spare_south(t2))
        u = tallen(whole(own_ref[OWN_EAST + k], EAST + k), u_lat)
        u = jnp.where(east | (row >= ROWS), u, 0.0)
        v = tallen(whole(own_ref[OWN_NORTH + k], NORTH + k), v_lat)
        v = jnp.where(north | (row == ROWS), v, 0.0)
        p = tallen(whole(p_own[k], PRESSURE + k), wide(p_tile[k], none))
        tend_u, tend_v = momentum(k, u, v, p, wind, east, north, f_u, f_v, up, down)
        star_u = (u + time_step * tend_u)[:ROWS, :COLS]
        star_v = (v + time_step * tend_v)[:ROWS, :COLS]
        stars_u.append(star_u)
        stars_v.append(star_v)
        mean_u = mean_u + star_u
        mean_v = mean_v + star_v

        diffusion = jnp.where(north[:, :COLS], tracer_diffusion, 0.0)
        for t in range(TRACERS):
            cn = tallen(c[t][k], tiles[t][k])
            gains[LEVELS * t + k] = gain(cn, 0, v[:, :COLS], diffusion)[:ROWS]
    for n in range(TRACERS * LEVELS):
        t, k = divmod(n, LEVELS)
        change = along_ref[ROWS * n : ROWS * (n + 1)] + gains[n]
        tracers_out[t, k] = jnp.where(bottom_own > k, c[t][k] + time_step * change, 0.0)
    shift_u = average_u - mean_u / jnp.maximum(own_u, 1.0)
    shift_v = average_v - mean_v / jnp.maximum(own_v, 1.0)
    for k in range(LEVELS):
        velocity_out[0, k] = jnp.where(own_u > k, stars_u[k] + shift_u, 0.0)
        velocity_out[1, k] = jnp.where(own_v > k, stars_v[k] + shift_v, 0.0)


def ring(axis, step):
    count = lax.axis_size(axis)
    return [(i, (i + step) % count) for i in range(count)]


def struct(*shape):
    return jax.ShapeDtypeStruct(shape, f32)


def vmem(*shape):
    return pltpu.VMEM(shape, f32)


def specs(count, scalars=0):
    return [pl.BlockSpec(memory_space=pltpu.SMEM)] * scalars + [
        pl.BlockSpec(memory_space=pltpu.VMEM)
    ] * count


PARAMS = pltpu.CompilerParams(vmem_limit_bytes=32 * 1024 * 1024)


def stacked(tracers, velocity, surface, wind, bottom):
    def put(values, first):
        values = values.reshape(-1, ROWS, COLS)
        after = OWN - first - values.shape[0]
        return lax.pad(
            values, jnp.zeros((), values.dtype), ((first, after, 0), (0, 0, 0), (0, 0, 0))
        )

    return (
        put(tracers, 0)
        + put(velocity, OWN_EAST)
        + put(surface, OWN_SURFACE)
        + put(wind, OWN_WIND)
        + put(bottom, OWN_BOTTOM).astype(f32)
    )


def shards(tracers, velocity, surface, wind, bottom):
    place = lax.axis_index("lat").astype(jnp.int32).reshape(1)
    own = stacked(tracers, velocity, surface, wind, bottom)
    payload = struct(PLANES // 4 + 1, ROWS, COLS)
    to_right, to_left = pl.pallas_call(
        pack_kernel,
        out_shape=(payload, payload),
        in_specs=specs(1),
        out_specs=tuple(specs(2)),
        compiler_params=PARAMS,
        name="pack",
    )(own)
    west = lax.ppermute(to_right, "lon", ring("lon", 1))
    east = lax.ppermute(to_left, "lon", ring("lon", -1))
    inner = pl.pallas_call(
        inner_kernel,
        out_shape=struct(TRACERS * LEVELS * ROWS, COLS),
        in_specs=specs(1),
        out_specs=specs(1)[0],
        compiler_params=PARAMS,
        cost_estimate=pl.CostEstimate(flops=1500000, bytes_accessed=3000000, transcendentals=0),
        name="inner",
    )(own)
    chunks, along = pl.pallas_call(
        send_kernel,
        out_shape=(
            struct(MEMBERS, CHUNK, COLS),
            struct(TRACERS * LEVELS * ROWS, COLS),
        ),
        in_specs=specs(6, 1),
        out_specs=tuple(specs(2)),
        scratch_shapes=[
            vmem(12 * ROWS, COLS),
            vmem(2, COLS, COLS),
            vmem(40, 2 * COLS),
            vmem(COLS + 2 * HALO, COLS),
        ],
        compiler_params=PARAMS,
        name="columns",
    )(place, own, west, east, to_right, to_left, inner)
    slabs = lax.all_to_all(chunks, "lat", 0, 0, tiled=True)
    answers = pl.pallas_call(
        slab_kernel,
        out_shape=struct(MEMBERS, BACK, COLS),
        in_specs=specs(1),
        out_specs=specs(1)[0],
        scratch_shapes=[vmem(COLS, COLS)],
        compiler_params=PARAMS,
        name="substeps",
    )(slabs)
    home = lax.all_to_all(answers, "lat", 0, 0, tiled=True)
    return pl.pallas_call(
        finish_kernel,
        out_shape=(
            struct(TRACERS, LEVELS, ROWS, COLS),
            struct(2, LEVELS, ROWS, COLS),
            struct(ROWS, COLS),
            struct(ROWS, COLS),
        ),
        in_specs=specs(5, 1),
        out_specs=tuple(specs(4)),
        scratch_shapes=[vmem(COLS, COLS), vmem(4 * ROWS, COLS)],
        compiler_params=PARAMS,
        name="finish",
    )(place, home, own, west, east, along)


def solution(mesh):
    placed = (
        P(None, None, "lat", "lon"),
        P(None, None, "lat", "lon"),
        P("lat", "lon"),
        P(None, "lat", "lon"),
        P("lat", "lon"),
    )
    return jax.shard_map(
        shards,
        mesh=mesh,
        in_specs=placed,
        out_specs=(
            P(None, None, "lat", "lon"),
            P(None, None, "lat", "lon"),
            P("lat", "lon"),
            P("lat", "lon"),
        ),
        check_vma=False,
    )
```

```python
import jax
import jax.numpy as jnp
from jax import lax
from jax.experimental import pallas as pl
from jax.experimental.pallas import tpu as pltpu
from jax.sharding import PartitionSpec as P

TRACERS = 4
LEVELS = 8
SUBSTEPS = 30
ROWS = 16
COLS = 128
MEMBERS = 16
HALO = 32
SLAB = 72
NLAT = ROWS * MEMBERS

time_step = 0.2
tracer_diffusion = 0.2
viscosity = 0.2
thermal_expansion = 2.0
haline_contraction = 1.5
coriolis_base = 1.0
gravity = 140.0
surface_scale = 40.0
thickness = 1.0 / LEVELS
f32 = jnp.float32

PRESSURE, EAST, NORTH, WIND, SURFACE, BOTTOM = 0, 8, 16, 24, 26, 27
PLANES = 28
OWN_EAST, OWN_NORTH, OWN_SURFACE, OWN_WIND, OWN_BOTTOM, OWN = 32, 40, 48, 49, 51, 52
MAIL_N, MAIL_S, CHUNK = SLAB, SLAB + 8, SLAB + 16
BACK = 24


def at(values, step, axis):
    size = values.shape[axis]
    step %= size
    return values if step == 0 else pltpu.roll(values, size - step, axis)


def ids(shape, axis):
    return lax.broadcasted_iota(jnp.int32, shape, axis)


def wide(own, beside):
    return jnp.concatenate([own, beside], axis=1)


def tracer_planes(own_ref):
    bottom = own_ref[OWN_BOTTOM]
    return [
        [jnp.where(bottom > k, own_ref[LEVELS * t + k], 0.0) for k in range(LEVELS)]
        for t in range(TRACERS)
    ]


def pressures(salt, heat):
    total, out = None, []
    for k in range(LEVELS):
        density = haline_contraction * salt[k] - thermal_expansion * heat[k]
        total = density if total is None else total + density
        out.append(thickness * total)
    return out


def pack_kernel(own_ref, right_ref, left_ref):
    c = tracer_planes(own_ref)
    planes = pressures(c[1], c[0])
    planes += [own_ref[n] for n in range(OWN_EAST, OWN_SURFACE)]
    planes += [own_ref[n] for n in (OWN_WIND, OWN_WIND + 1, OWN_SURFACE, OWN_BOTTOM)]
    lane = ids((ROWS, COLS), 1)
    for q in range(PLANES // 4):
        right = left = jnp.zeros((ROWS, COLS), f32)
        for s in range(4):
            moved = at(planes[4 * q + s], -32 * s, 1)
            right = jnp.where(lane // 32 == (s + 3) % 4, moved, right)
            left = jnp.where(lane // 32 == s, moved, left)
        right_ref[q] = right
        left_ref[q] = left
    right = left = jnp.zeros((ROWS, COLS), f32)
    for n in range(TRACERS * LEVELS):
        moved = at(c[n // LEVELS][n % LEVELS], -4 * n, 1)
        right = jnp.where(lane // 4 == (n + 31) % 32, moved, right)
        left = jnp.where(lane // 4 == n, moved, left)
    right_ref[PLANES // 4] = right
    left_ref[PLANES // 4] = left


def beside_plane(west_ref, east_ref, plane):
    q, s = divmod(plane, 4)
    block = ids((ROWS, COLS), 1) // 32
    both = jnp.where(
        block == s, east_ref[q], jnp.where(block == (s + 3) % 4, west_ref[q], 0.0)
    )
    return at(both, 32 * s, 1)


def momentum(k, u, v, p, wind, east, north, f_u, f_v, up, down):
    pair_v = v + down(v)
    pair_u = u + at(u, -1, 1)
    tend_u = (
        (0.25 * f_u) * (pair_v + at(pair_v, 1, 1))
        - (at(p, 1, 1) - p)
        + viscosity * (at(u, 1, 1) + at(u, -1, 1) + up(u) + down(u) - 4.0 * u)
    )
    tend_v = (
        (-0.25 * f_v) * (pair_u + up(pair_u))
        - (up(p) - p)
        + viscosity * (at(v, 1, 1) + at(v, -1, 1) + up(v) + down(v) - 4.0 * v)
    )
    if k == 0:
        tend_u = tend_u + wind[0]
        tend_v = tend_v + wind[1]
    return jnp.where(east, tend_u, 0.0), jnp.where(north, tend_v, 0.0)


def coriolis(rows, offset):
    return coriolis_base * (0.5 + (rows.astype(f32) + offset) / NLAT)


def send_kernel(
    place_ref, own_ref, west_ref, east_ref, right_ref, left_ref, inner_ref,
    out_ref, along_ref, split_ref, stack_ref, edge_ref, turned_ref,
):
    place = place_ref[0]
    c = tracer_planes(own_ref)
    p_own = pressures(c[1], c[0])

    def whole(own, plane):
        return wide(own, beside_plane(west_ref, east_ref, plane))

    shape = (ROWS, 2 * COLS)
    row = ids(shape, 0)
    bottom = whole(own_ref[OWN_BOTTOM], BOTTOM)
    wind = [whole(own_ref[OWN_WIND + d], WIND + d) for d in range(2)]

    def up(x):
        return jnp.where(row == ROWS - 1, 0.0, at(x, 1, 0))

    def down(x):
        return jnp.where(row == 0, 0.0, at(x, -1, 0))

    count_u = jnp.minimum(bottom, at(bottom, 1, 1))
    count_v = jnp.minimum(bottom, up(bottom))
    f_u = coriolis(place * ROWS + row, 0.5)
    f_v = coriolis(place * ROWS + row, 1.0)
    sums = [jnp.zeros(shape, f32) for _ in range(4)]
    us, vs, raws = [], [], []
    for k in range(LEVELS):
        east, north = count_u > k, count_v > k
        u = jnp.where(east, whole(own_ref[OWN_EAST + k], EAST + k), 0.0)
        raw = jnp.where(bottom > k, whole(own_ref[OWN_NORTH + k], NORTH + k), 0.0)
        v = jnp.where(north, raw, 0.0)
        p = whole(p_own[k], PRESSURE + k)
        tend_u, tend_v = momentum(k, u, v, p, wind, east, north, f_u, f_v, up, down)
        sums = [a + b for a, b in zip(sums, (u, v, tend_u, tend_v))]
        us.append(u)
        vs.append(v)
        raws.append(raw)
        pair = u + at(u, -1, 1)
        last = p[8:] + (-0.25 * f_v[8:]) * pair[8:] + viscosity * at(v, -1, 0)[8:]
        if k == 0:
            last = last + wind[1][8:]
        first = (-0.25 * (f_v[:8] - 1.0 / NLAT)) * pair[:8] - p[:8] + viscosity * v[:8]
        edge_ref[k : k + 1] = u[15:16]
        edge_ref[8 + k : 9 + k] = raw[15:16]
        edge_ref[16 + k : 17 + k] = last[7:8]
        edge_ref[24 + k : 25 + k] = u[0:1]
        edge_ref[32 + k : 33 + k] = first[0:1]
    surface = whole(own_ref[OWN_SURFACE], SURFACE)
    for n, values in enumerate((surface, *sums, bottom)):
        split_ref[ROWS * n : ROWS * (n + 1)] = values[:, :COLS]
        split_ref[ROWS * (6 + n) : ROWS * (7 + n)] = values[:, COLS:]
    for q in range(16):
        spot = pl.multiple_of(lax.rem(q + place, 16) * 8, 8)
        for half in range(2):
            if q < 12:
                rows = split_ref[pl.ds(ROWS * (6 * half + q // 2) + q % 2, 8, 2), :]
            else:
                rows = edge_ref[8 * (q - 12) : 8 * (q - 11), COLS * half : COLS * (half + 1)]
            stack_ref[half, pl.ds(spot, 8)] = rows
    turned_ref[HALO : HALO + COLS] = stack_ref[0].T
    beyond = stack_ref[1].T
    turned_ref[:HALO] = beyond[COLS - HALO :]
    turned_ref[HALO + COLS :] = beyond[:HALO]
    edge = edge_ref[32:40]
    sub = ids((8, COLS), 0)
    tile_lane = ids((8, COLS), 1)
    spare_block = tile_lane // 8 == lax.rem(6 + place, 16)
    for d in range(MEMBERS):
        moved = at(edge, 8 * d - HALO + 4, 1)[:, :COLS]
        pairs = jnp.where(tile_lane < 64, moved, at(at(moved, 64, 1), 1, 0))
        rest = jnp.where(tile_lane % 8 == sub, moved[:, 64:65], 0.0)
        for step in (1, 2, 4):
            rest = rest + at(rest, step, 0)
        out_ref[d, :8] = jnp.where(
            sub == 0, pairs, jnp.where(sub == 1, at(pairs, 1, 0), turned_ref[8 * d : 8 * d + 8])
        )
        out_ref[d, 8 : SLAB - 8] = turned_ref[8 * d + 8 : 8 * d + SLAB - 8]
        end = turned_ref[8 * d + SLAB - 8 : 8 * d + SLAB]
        end = jnp.where((sub == 5) & spare_block, rest, end)
        end = jnp.where(sub == 6, at(pairs, -2, 0), end)
        out_ref[d, SLAB - 8 : SLAB] = jnp.where(sub == 7, at(pairs, -1, 0), end)

    block = ids((ROWS, COLS), 1) // 4
    flows = [(us[k], jnp.where(count_u > k, tracer_diffusion, 0.0)) for k in range(LEVELS)]

    def packed(which, half, ahead):
        tile = jnp.zeros((ROWS, COLS), f32)
        for k in range(LEVELS):
            values = flows[k][which][:, COLS * half : COLS * (half + 1)]
            tile = jnp.where(block % LEVELS == k, at(values, -4 * (k + ahead), 1), tile)
        for step in (32, 64):
            tile = jnp.where(block * 4 % (2 * step) < step, tile, at(tile, -step, 1))
        return tile

    last = PLANES // 4
    low, high = outer(
        at(west_ref[last], -4, 1), east_ref[last], left_ref[last], at(right_ref[last], -4, 1),
        packed(0, 1, 1), packed(0, 0, 0), packed(0, 0, 1), packed(1, 1, 1), packed(1, 0, 1),
    )
    high = at(high, 4, 1)
    for n in range(TRACERS * LEVELS):
        both = jnp.where(block == n, low, jnp.where(block == (n + 31) % 32, high, 0.0))
        rows = slice(ROWS * n, ROWS * (n + 1))
        along_ref[rows] = inner_ref[rows] + at(both, 4 * n, 1)


    def spare(n):
        t, k = divmod(n, LEVELS)
        if t == 0:
            return us[k][:, :COLS], us[k][:, :COLS]
        if t == 1:
            return raws[k][:, :COLS], vs[k][:, :COLS]
        if t == 2:
            return raws[k][:, COLS:], us[k][:, COLS:]
        if k < 2:
            own = bottom[:, COLS * k : COLS * (k + 1)]
            return own, own
        return None

    def tops(n):
        own = c[n // LEVELS][n % LEVELS][8:]
        more = spare(n)
        return own if more is None else jnp.where(sub == 4, at(more[0][8:], 3, 0), own)

    def bottoms(n):
        own = c[n // LEVELS][n % LEVELS][:8]
        more = spare(n)
        return own if more is None else jnp.where(sub == 3, at(more[1][:8], -3, 0), own)

    for m in range(MEMBERS):
        out_ref[m, MAIL_N:MAIL_S] = jnp.where(sub >= 4, tops(2 * m), at(tops(2 * m + 1), 4, 0))
        out_ref[m, MAIL_S:CHUNK] = jnp.where(sub < 4, bottoms(2 * m), at(bottoms(2 * m + 1), 4, 0))


def slab_kernel(in_ref, out_ref, edge_ref):
    shape = (SLAB, COLS)
    lane = ids(shape, 1)
    r = lane % 8
    block = ids((8, COLS), 1) // 8

    tiles = []
    for t in range(SLAB // 8):
        now = [in_ref[a, 8 * t : 8 * t + 8] for a in range(MEMBERS)]
        for bit in (1, 2, 4, 8):
            odd = (block & bit) > 0
            now = [jnp.where(odd, now[(a + bit) % MEMBERS], now[a]) for a in range(MEMBERS)]
        tiles.append([at(now[-q % MEMBERS], 8 * q, 1) for q in range(16)])
    blocks = [jnp.concatenate([tile[q] for tile in tiles], axis=0) for q in range(16)]
    surface, start_u, start_v, force_u, force_v, bottom = (blocks[2 * n : 2 * n + 2] for n in range(6))
    u_a, v_raw, near, u_next = blocks[12:]
    zeros = jnp.zeros((8, COLS), f32)
    sub = ids((8, COLS), 0)
    edge_ref[COLS - 8 :] = zeros
    for a in range(1, MEMBERS):
        begin, end = in_ref[a, :8], in_ref[a, SLAB - 8 : SLAB]
        rows = jnp.where(sub < 2, begin, at(begin, -1, 0))
        rows = jnp.where(sub < 4, rows, jnp.where(sub < 6, at(end, 2, 0), at(end, 1, 0)))
        edge_ref[8 * a - 8 : 8 * a] = jnp.where(sub % 2 == 0, rows, at(at(rows, 64, 1), -1, 0))
    column = ids(shape, 0)
    far = at(edge_ref[...].T[:SLAB], -4, 0)
    far = jnp.where(column == 68, at(at(force_u[0], 1, 0), 8, 1), far)
    unused = (column < 2) | (column >= SLAB - 2)
    bottom = [jnp.where(unused, float(LEVELS), b) for b in bottom]

    top = lane == COLS - 1
    count_u = [jnp.minimum(b, at(b, 1, 0)) for b in bottom]
    count_v = [
        jnp.minimum(*bottom),
        jnp.where(top, 0.0, jnp.minimum(bottom[1], at(bottom[0], 1, 1))),
    ]

    ahead = jnp.concatenate([count_u[0], count_v[0]], axis=0)
    first = (ids(ahead.shape, 1) % 8 == 0) & (ids(ahead.shape, 1) > 0)
    counts = jnp.concatenate(
        [
            jnp.where(r == 7, count_u[1], 0.0),
            jnp.where(r == 7, count_v[1], 0.0),
            jnp.where(r == 7, count_v[0], 0.0),
            at(jnp.where(first, ahead, 0.0), 1, 1),
        ],
        axis=0,
    )
    for step in (1, 2, 4):
        counts = counts + at(counts, step, 1)
    count_ua, count_va, count_vc, count_ub, count_vb = (
        counts[SLAB * n : SLAB * (n + 1)] for n in range(5)
    )
    level = r.astype(f32)
    last = lane >= COLS - 8
    v_a = jnp.where(count_va > level, v_raw, 0.0)
    u_a = jnp.where(last, 0.0, u_a)
    u_b = jnp.where(last, 0.0, at(u_next, 8, 1))
    f_a = 0.25 * coriolis(lane // 8 * ROWS + 15, 0.5)
    f_b = f_a + 0.25 * coriolis_base / NLAT
    pair = v_a + at(v_a, 1, 0)
    spread = viscosity * (at(v_a, 1, 0) + at(v_a, -1, 0) - 4.0 * v_a)
    terms = jnp.concatenate(
        [
            jnp.where(count_ua > level, f_a * pair + viscosity * u_b, 0.0),
            jnp.where(count_ub > level, f_b * pair + viscosity * u_a, 0.0),
            jnp.where(count_vb > level, viscosity * v_a, 0.0),
            jnp.where(count_vc > level, viscosity * v_a, 0.0),
            jnp.where(count_va > level, near + far + spread, 0.0),
            v_a,
        ],
        axis=0,
    )
    for step in (1, 2, 4):
        terms = terms + at(terms, -step, 1)
    shifted = at(terms[SLAB : 3 * SLAB], -1, 1)
    u_15, v_14, v_15, begin_15 = (
        jnp.where(r == 7, terms[SLAB * n : SLAB * (n + 1)], 0.0) for n in (0, 3, 4, 5)
    )
    u_16, v_16 = (jnp.where(r == 0, shifted[SLAB * n : SLAB * (n + 1)], 0.0) for n in range(2))
    force_u = [force_u[0] + u_16, force_u[1] + u_15]
    force_v = [force_v[0] + (v_14 + v_16), force_v[1] + v_15]
    start_v = [start_v[0], start_v[1] + begin_15]

    sub_step = time_step / SUBSTEPS
    held_u, held_v, flux_u, flux_v, begin_u, begin_v = [], [], [], [], [], []
    for i in range(2):
        per = 1.0 / jnp.maximum(count_u[i], 1.0)
        open_face = jnp.where(count_u[i] > 0.0, sub_step, 0.0)
        flux_u.append((sub_step * surface_scale * thickness) * count_u[i])
        held_u.append(
            (
                (0.25 * open_face) * coriolis(2 * lane + i, 0.5),
                gravity * open_face,
                open_face * (force_u[i] * per),
            )
        )
        begin_u.append(start_u[i] * per)
        per = 1.0 / jnp.maximum(count_v[i], 1.0)
        open_face = jnp.where(count_v[i] > 0.0, sub_step, 0.0)
        flux_v.append((sub_step * surface_scale * thickness) * count_v[i])
        held_v.append(
            (
                (-0.25 * open_face) * coriolis(2 * lane + i, 1.0),
                gravity * open_face,
                open_face * (force_v[i] * per),
            )
        )
        begin_v.append(start_v[i] * per)
    held = (
        *flux_u, at(flux_u[0], 1, 1), *flux_v, at(flux_v[0], 1, 1), at(flux_v[1], -1, 1),
        *held_u[0], *held_u[1], *held_v[0], *held_v[1],
    )
    state = (*surface, at(surface[0], 1, 1), *begin_u, *begin_v)
    total = (zeros,) * 4
    for low, steps in ((0, 6), (8, 8), (16, 8), (24, 8)):
        cut = 8 if low else 0
        state = tuple(x[cut : x.shape[0] - cut] for x in state)
        (
            du0, du1, du2, dv0, dv1, dv2, dv_, cu0, gu0, fu0, cu1, gu1, fu1,
            cv0, gv0, fv0, cv1, gv1, fv1,
        ) = (x[low : SLAB - low] for x in held)
        centre = HALO - low

        def advance(_, carry):
            h0, h1, h2, u0, u1, v0, v1, *sums = carry
            v_ = at(v1, -1, 1)
            u2 = at(u0, 1, 1)
            v2 = at(v0, 1, 1)
            x0, x1, x2 = du0 * u0, du1 * u1, du2 * u2
            y0, y1 = dv0 * v0, dv1 * v1
            h1 = h1 - ((x1 - at(x1, -1, 0)) + (y1 - y0))
            h0 = h0 - ((x0 - at(x0, -1, 0)) + (y0 - dv_ * v_))
            h2 = h2 - ((x2 - at(x2, -1, 0)) + (dv2 * v2 - y1))
            p0, p1, p2 = u0 + at(u0, -1, 0), u1 + at(u1, -1, 0), u2 + at(u2, -1, 0)
            q0, q1 = v0 + v_, v1 + v0
            u0 = (u0 + fu0) + (cu0 * (q0 + at(q0, 1, 0)) - gu0 * (at(h0, 1, 0) - h0))
            u1 = (u1 + fu1) + (cu1 * (q1 + at(q1, 1, 0)) - gu1 * (at(h1, 1, 0) - h1))
            v0 = (v0 + fv0) + (cv0 * (p0 + p1) - gv0 * (h1 - h0))
            v1 = (v1 + fv1) + (cv1 * (p1 + p2) - gv1 * (h2 - h1))
            sums = [a + b[centre : centre + 8] for a, b in zip(sums, (u0, u1, v0, v1))]
            return (h0, h1, h2, u0, u1, v0, v1, *sums)

        *state, a0, a1, a2, a3 = lax.fori_loop(
            0, steps, advance, (*state, *total), unroll=True
        )
        total = (a0, a1, a2, a3)
    height = [x[8:16] for x in state[:2]]
    average = [x * (1.0 / SUBSTEPS) for x in total]
    transport = [
        (-thickness * count_u[i][HALO : HALO + 8]) * average[i] for i in range(2)
    ]
    square = (COLS, COLS)
    before = (ids(square, 0) < ids(square, 1)).astype(f32)
    south = jnp.dot(
        transport[0] + transport[1],
        before,
        precision=lax.Precision.HIGHEST,
        preferred_element_type=f32,
    )
    stream = [south + transport[0], south + (transport[0] + transport[1])]
    results = [*height, *stream, *average]
    moved = [at(values, -8 * n, 1) for n, values in enumerate(results)]
    for e in range(MEMBERS):
        packed = moved[0]
        for n in range(1, 8):
            packed = jnp.where(block == (e + n) % 16, moved[n], packed)
        out_ref[e, 0:8] = packed
        out_ref[e, 8:16] = in_ref[(e + 15) % MEMBERS, MAIL_N:MAIL_S]
        out_ref[e, 16:24] = in_ref[(e + 1) % MEMBERS, MAIL_S:CHUNK]


def gain(values, axis, flow, diffusion):
    ahead = at(values, 1, axis)
    sides = at(values, -1, axis) + at(values, 2, axis)
    far = at(values, -2, axis) + at(values, 3, axis)
    face = (37.0 * (values + ahead) - 8.0 * sides + far) * (1.0 / 60.0)
    flux = diffusion * (ahead - values) - flow * face
    return flux - at(flux, -1, axis)


def inner_kernel(own_ref, out_ref):
    bottom = own_ref[OWN_BOTTOM]
    c = tracer_planes(own_ref)
    count = jnp.minimum(bottom, at(bottom, 1, 1))
    values = jnp.concatenate([plane for tracer in c for plane in tracer], axis=0)
    flow, diffusion = [], []
    for k in range(LEVELS):
        flow.append(jnp.where(count > k, own_ref[OWN_EAST + k], 0.0))
        diffusion.append(jnp.where(count > k, tracer_diffusion, 0.0))
    flow, diffusion = (jnp.concatenate(x * TRACERS, axis=0) for x in (flow, diffusion))
    lane = ids(values.shape, 1)

    def moved(step):
        inside = lane < COLS - step if step > 0 else lane >= -step
        return jnp.where(inside, at(values, step, 1), 0.0)

    ahead = moved(1)
    face = (37.0 * (values + ahead) - 8.0 * (moved(-1) + moved(2)) + (moved(-2) + moved(3))) * (
        1.0 / 60.0
    )
    flux = jnp.where(lane < COLS - 1, diffusion * (ahead - values) - flow * face, 0.0)
    out_ref[...] = flux - at(flux, -1, 1)


def outer(west, east, left, right, flow_w, flow_l, flow_r, diff_w, diff_r):
    q = ids((ROWS, COLS), 1) % 4
    sixtieth = 1.0 / 60.0
    w1, w2, w3 = at(west, 3, 1), at(west, 2, 1), at(west, 1, 1)
    face = 37.0 * (w1 + left) - 8.0 * (w2 + at(left, 1, 1)) + (w3 + at(left, 2, 1))
    through = at(diff_w, 3, 1) * (left - w1) - at(flow_w, 3, 1) * (face * sixtieth)
    flux = jnp.where(q == 0, w2 - 8.0 * w1, jnp.where(q == 1, w2, 0.0)) * (-sixtieth) * flow_l
    low = flux - at(flux, -1, 1) - jnp.where(q == 0, through, 0.0)
    e1, e2, e3 = at(east, -3, 1), at(east, -2, 1), at(east, -1, 1)
    face = 37.0 * (right + e1) - 8.0 * (at(right, -1, 1) + e2) + (at(right, -2, 1) + e3)
    through = diff_r * (e1 - right) - flow_r * (face * sixtieth)
    flux = jnp.where(q == 2, e3 - 8.0 * e2, jnp.where(q == 1, e3, 0.0)) * (-sixtieth) * flow_r
    high = flux - at(flux, -1, 1) + jnp.where(q == 3, through, 0.0)
    return low, high


def finish_kernel(
    place_ref, in_ref, own_ref, west_ref, east_ref, along_ref,
    tracers_out, velocity_out, height_out, stream_out, turned_ref, rows_ref,
):
    place = place_ref[0]
    turned_ref[...] = in_ref[:, 0:8].reshape(COLS, COLS).T

    for q in range(8):
        spot = pl.multiple_of(lax.rem(q + place, 16) * 8, 8)
        rows_ref[pl.ds(ROWS * (q // 2) + q % 2, 8, 2), :] = turned_ref[pl.ds(spot, 8)]
    height_out[...] = rows_ref[:ROWS]
    stream_out[...] = rows_ref[ROWS : 2 * ROWS]
    average_u, average_v = rows_ref[2 * ROWS : 3 * ROWS], rows_ref[3 * ROWS :]

    sub = ids((8, COLS), 0)
    tall = (ROWS + 8, 2 * COLS)
    row = ids(tall, 0)
    first, last = place == 0, place == MEMBERS - 1

    def lat_tile(n):
        south = jnp.where(first, 0.0, in_ref[n // 2, 8:16])
        north = jnp.where(last, 0.0, in_ref[n // 2, 16:24])
        if n % 2 == 0:
            return jnp.where(sub < 4, north, south)
        return at(jnp.where(sub < 4, south, north), 4, 0)

    def spare_north(tile):
        return jnp.where(sub == 0, at(tile, 3, 0), 0.0)

    def spare_south(tile):
        return jnp.where(sub == 7, at(tile, -3, 0), 0.0)

    def tallen(own, tile):
        return jnp.concatenate([own, tile], axis=0)

    def whole(own, plane):
        return wide(own, beside_plane(west_ref, east_ref, plane))

    tiles = [[lat_tile(LEVELS * t + k) for k in range(LEVELS)] for t in range(TRACERS)]
    bottom_own = own_ref[OWN_BOTTOM]
    c = tracer_planes(own_ref)
    p_own = pressures(c[1], c[0])
    p_tile = pressures(tiles[1], tiles[0])
    both = wide(
        spare_north(tiles[3][0]) + spare_south(tiles[3][0]),
        spare_north(tiles[3][1]) + spare_south(tiles[3][1]),
    )
    bottom = tallen(whole(bottom_own, BOTTOM), both)
    count_u = jnp.minimum(bottom, at(bottom, 1, 1))
    count_v = jnp.minimum(bottom, at(bottom, 1, 0))
    f_u = coriolis(place * ROWS + row, 0.5)
    f_v = coriolis(place * ROWS + row, 1.0)
    none = jnp.zeros((8, COLS), f32)
    wind = [tallen(wide(own_ref[OWN_WIND + d], jnp.zeros((ROWS, COLS), f32)), jnp.zeros((8, 2 * COLS), f32)) for d in range(2)]

    def up(x):
        return at(x, 1, 0)

    def down(x):
        return at(x, -1, 0)

    stars_u, stars_v, gains = [], [], [None] * (TRACERS * LEVELS)
    own_u, own_v = count_u[:ROWS, :COLS], count_v[:ROWS, :COLS]
    mean_u = mean_v = jnp.zeros((ROWS, COLS), f32)
    for k in range(LEVELS):
        east, north = count_u > k, count_v > k
        t0, t1, t2 = tiles[0][k], tiles[1][k], tiles[2][k]
        u_lat = wide(spare_north(t0) + spare_south(t0), spare_north(t2))
        v_lat = wide(spare_north(t1) + spare_south(t1), spare_south(t2))
        u = tallen(whole(own_ref[OWN_EAST + k], EAST + k), u_lat)
        u = jnp.where(east | (row >= ROWS), u, 0.0)
        v = tallen(whole(own_ref[OWN_NORTH + k], NORTH + k), v_lat)
        v = jnp.where(north | (row == ROWS), v, 0.0)
        p = tallen(whole(p_own[k], PRESSURE + k), wide(p_tile[k], none))
        tend_u, tend_v = momentum(k, u, v, p, wind, east, north, f_u, f_v, up, down)
        star_u = (u + time_step * tend_u)[:ROWS, :COLS]
        star_v = (v + time_step * tend_v)[:ROWS, :COLS]
        stars_u.append(star_u)
        stars_v.append(star_v)
        mean_u = mean_u + star_u
        mean_v = mean_v + star_v

        diffusion = jnp.where(north[:, :COLS], tracer_diffusion, 0.0)
        for t in range(TRACERS):
            cn = tallen(c[t][k], tiles[t][k])
            gains[LEVELS * t + k] = gain(cn, 0, v[:, :COLS], diffusion)[:ROWS]
    for n in range(TRACERS * LEVELS):
        t, k = divmod(n, LEVELS)
        change = along_ref[ROWS * n : ROWS * (n + 1)] + gains[n]
        tracers_out[t, k] = jnp.where(bottom_own > k, c[t][k] + time_step * change, 0.0)
    shift_u = average_u - mean_u / jnp.maximum(own_u, 1.0)
    shift_v = average_v - mean_v / jnp.maximum(own_v, 1.0)
    for k in range(LEVELS):
        velocity_out[0, k] = jnp.where(own_u > k, stars_u[k] + shift_u, 0.0)
        velocity_out[1, k] = jnp.where(own_v > k, stars_v[k] + shift_v, 0.0)


def ring(axis, step):
    count = lax.axis_size(axis)
    return [(i, (i + step) % count) for i in range(count)]


def struct(*shape):
    return jax.ShapeDtypeStruct(shape, f32)


def vmem(*shape):
    return pltpu.VMEM(shape, f32)


def specs(count, scalars=0):
    return [pl.BlockSpec(memory_space=pltpu.SMEM)] * scalars + [
        pl.BlockSpec(memory_space=pltpu.VMEM)
    ] * count


PARAMS = pltpu.CompilerParams(vmem_limit_bytes=32 * 1024 * 1024)


def stacked(tracers, velocity, surface, wind, bottom):
    def put(values, first):
        values = values.reshape(-1, ROWS, COLS)
        after = OWN - first - values.shape[0]
        return lax.pad(
            values, jnp.zeros((), values.dtype), ((first, after, 0), (0, 0, 0), (0, 0, 0))
        )

    return (
        put(tracers, 0)
        + put(velocity, OWN_EAST)
        + put(surface, OWN_SURFACE)
        + put(wind, OWN_WIND)
        + put(bottom, OWN_BOTTOM).astype(f32)
    )


def shards(tracers, velocity, surface, wind, bottom):
    place = lax.axis_index("lat").astype(jnp.int32).reshape(1)
    own = stacked(tracers, velocity, surface, wind, bottom)
    payload = struct(PLANES // 4 + 1, ROWS, COLS)
    to_right, to_left = pl.pallas_call(
        pack_kernel,
        out_shape=(payload, payload),
        in_specs=specs(1),
        out_specs=tuple(specs(2)),
        compiler_params=PARAMS,
        name="pack",
    )(own)
    west = lax.ppermute(to_right, "lon", ring("lon", 1))
    east = lax.ppermute(to_left, "lon", ring("lon", -1))
    inner = pl.pallas_call(
        inner_kernel,
        out_shape=struct(TRACERS * LEVELS * ROWS, COLS),
        in_specs=specs(1),
        out_specs=specs(1)[0],
        compiler_params=PARAMS,
        cost_estimate=pl.CostEstimate(flops=1500000, bytes_accessed=3000000, transcendentals=0),
        name="inner",
    )(own)
    chunks, along = pl.pallas_call(
        send_kernel,
        out_shape=(
            struct(MEMBERS, CHUNK, COLS),
            struct(TRACERS * LEVELS * ROWS, COLS),
        ),
        in_specs=specs(6, 1),
        out_specs=tuple(specs(2)),
        scratch_shapes=[
            vmem(12 * ROWS, COLS),
            vmem(2, COLS, COLS),
            vmem(40, 2 * COLS),
            vmem(COLS + 2 * HALO, COLS),
        ],
        compiler_params=PARAMS,
        name="columns",
    )(place, own, west, east, to_right, to_left, inner)
    slabs = lax.all_to_all(chunks, "lat", 0, 0, tiled=True)
    answers = pl.pallas_call(
        slab_kernel,
        out_shape=struct(MEMBERS, BACK, COLS),
        in_specs=specs(1),
        out_specs=specs(1)[0],
        scratch_shapes=[vmem(COLS, COLS)],
        compiler_params=PARAMS,
        name="substeps",
    )(slabs)
    home = lax.all_to_all(answers, "lat", 0, 0, tiled=True)
    return pl.pallas_call(
        finish_kernel,
        out_shape=(
            struct(TRACERS, LEVELS, ROWS, COLS),
            struct(2, LEVELS, ROWS, COLS),
            struct(ROWS, COLS),
            struct(ROWS, COLS),
        ),
        in_specs=specs(5, 1),
        out_specs=tuple(specs(4)),
        scratch_shapes=[vmem(COLS, COLS), vmem(4 * ROWS, COLS)],
        compiler_params=PARAMS,
        name="finish",
    )(place, home, own, west, east, along)


def solution(mesh):
    placed = (
        P(None, None, "lat", "lon"),
        P(None, None, "lat", "lon"),
        P("lat", "lon"),
        P(None, "lat", "lon"),
        P("lat", "lon"),
    )
    return jax.shard_map(
        shards,
        mesh=mesh,
        in_specs=placed,
        out_specs=(
            P(None, None, "lat", "lon"),
            P(None, None, "lat", "lon"),
            P("lat", "lon"),
            P("lat", "lon"),
        ),
        check_vma=False,
    )
```

```python
import jax
import jax.numpy as jnp
from jax import lax
from jax.experimental import pallas as pl
from jax.experimental.pallas import tpu as pltpu
from jax.sharding import PartitionSpec as P

TRACERS = 4
LEVELS = 8
SUBSTEPS = 30
ROWS = 16
COLS = 128
MEMBERS = 16
HALO = 32
SLAB = 72
NLAT = ROWS * MEMBERS

time_step = 0.2
tracer_diffusion = 0.2
viscosity = 0.2
thermal_expansion = 2.0
haline_contraction = 1.5
coriolis_base = 1.0
gravity = 140.0
surface_scale = 40.0
thickness = 1.0 / LEVELS
f32 = jnp.float32

PRESSURE, EAST, NORTH, WIND, SURFACE, BOTTOM = 0, 8, 16, 24, 26, 27
PLANES = 28
OWN_EAST, OWN_NORTH, OWN_SURFACE, OWN_WIND, OWN_BOTTOM, OWN = 32, 40, 48, 49, 51, 52
MAIL_N, MAIL_S, CHUNK = SLAB, SLAB + 8, SLAB + 16
BACK = 24


def at(values, step, axis):
    size = values.shape[axis]
    step %= size
    return values if step == 0 else pltpu.roll(values, size - step, axis)


def ids(shape, axis):
    return lax.broadcasted_iota(jnp.int32, shape, axis)


def wide(own, beside):
    return jnp.concatenate([own, beside], axis=1)


def tracer_planes(own_ref):
    bottom = own_ref[OWN_BOTTOM]
    return [
        [jnp.where(bottom > k, own_ref[LEVELS * t + k], 0.0) for k in range(LEVELS)]
        for t in range(TRACERS)
    ]


def pressures(salt, heat):
    total, out = None, []
    for k in range(LEVELS):
        density = haline_contraction * salt[k] - thermal_expansion * heat[k]
        total = density if total is None else total + density
        out.append(thickness * total)
    return out


def pack_kernel(own_ref, right_ref, left_ref):
    c = tracer_planes(own_ref)
    planes = pressures(c[1], c[0])
    planes += [own_ref[n] for n in range(OWN_EAST, OWN_SURFACE)]
    planes += [own_ref[n] for n in (OWN_WIND, OWN_WIND + 1, OWN_SURFACE, OWN_BOTTOM)]
    lane = ids((ROWS, COLS), 1)
    for q in range(PLANES // 4):
        right = left = jnp.zeros((ROWS, COLS), f32)
        for s in range(4):
            moved = at(planes[4 * q + s], -32 * s, 1)
            right = jnp.where(lane // 32 == (s + 3) % 4, moved, right)
            left = jnp.where(lane // 32 == s, moved, left)
        right_ref[q] = right
        left_ref[q] = left
    right = left = jnp.zeros((ROWS, COLS), f32)
    for n in range(TRACERS * LEVELS):
        moved = at(c[n // LEVELS][n % LEVELS], -4 * n, 1)
        right = jnp.where(lane // 4 == (n + 31) % 32, moved, right)
        left = jnp.where(lane // 4 == n, moved, left)
    right_ref[PLANES // 4] = right
    left_ref[PLANES // 4] = left


def beside_plane(west_ref, east_ref, plane):
    q, s = divmod(plane, 4)
    block = ids((ROWS, COLS), 1) // 32
    both = jnp.where(
        block == s, east_ref[q], jnp.where(block == (s + 3) % 4, west_ref[q], 0.0)
    )
    return at(both, 32 * s, 1)


def momentum(k, u, v, p, wind, east, north, f_u, f_v, up, down):
    pair_v = v + down(v)
    pair_u = u + at(u, -1, 1)
    tend_u = (
        (0.25 * f_u) * (pair_v + at(pair_v, 1, 1))
        - (at(p, 1, 1) - p)
        + viscosity * (at(u, 1, 1) + at(u, -1, 1) + up(u) + down(u) - 4.0 * u)
    )
    tend_v = (
        (-0.25 * f_v) * (pair_u + up(pair_u))
        - (up(p) - p)
        + viscosity * (at(v, 1, 1) + at(v, -1, 1) + up(v) + down(v) - 4.0 * v)
    )
    if k == 0:
        tend_u = tend_u + wind[0]
        tend_v = tend_v + wind[1]
    return jnp.where(east, tend_u, 0.0), jnp.where(north, tend_v, 0.0)


def coriolis(rows, offset):
    return coriolis_base * (0.5 + (rows.astype(f32) + offset) / NLAT)


def send_kernel(
    place_ref, own_ref, west_ref, east_ref, right_ref, left_ref, inner_ref,
    out_ref, along_ref, split_ref, stack_ref, edge_ref, turned_ref,
):
    place = place_ref[0]
    c = tracer_planes(own_ref)
    p_own = pressures(c[1], c[0])

    def whole(own, plane):
        return wide(own, beside_plane(west_ref, east_ref, plane))

    shape = (ROWS, 2 * COLS)
    row = ids(shape, 0)
    bottom = whole(own_ref[OWN_BOTTOM], BOTTOM)
    wind = [whole(own_ref[OWN_WIND + d], WIND + d) for d in range(2)]

    def up(x):
        return jnp.where(row == ROWS - 1, 0.0, at(x, 1, 0))

    def down(x):
        return jnp.where(row == 0, 0.0, at(x, -1, 0))

    count_u = jnp.minimum(bottom, at(bottom, 1, 1))
    count_v = jnp.minimum(bottom, up(bottom))
    f_u = coriolis(place * ROWS + row, 0.5)
    f_v = coriolis(place * ROWS + row, 1.0)
    sums = [jnp.zeros(shape, f32) for _ in range(4)]
    us, vs, raws = [], [], []
    for k in range(LEVELS):
        east, north = count_u > k, count_v > k
        u = jnp.where(east, whole(own_ref[OWN_EAST + k], EAST + k), 0.0)
        raw = jnp.where(bottom > k, whole(own_ref[OWN_NORTH + k], NORTH + k), 0.0)
        v = jnp.where(north, raw, 0.0)
        p = whole(p_own[k], PRESSURE + k)
        tend_u, tend_v = momentum(k, u, v, p, wind, east, north, f_u, f_v, up, down)
        sums = [a + b for a, b in zip(sums, (u, v, tend_u, tend_v))]
        us.append(u)
        vs.append(v)
        raws.append(raw)
        pair = u + at(u, -1, 1)
        last = p[8:] + (-0.25 * f_v[8:]) * pair[8:] + viscosity * at(v, -1, 0)[8:]
        if k == 0:
            last = last + wind[1][8:]
        first = (-0.25 * (f_v[:8] - 1.0 / NLAT)) * pair[:8] - p[:8] + viscosity * v[:8]
        edge_ref[k : k + 1] = u[15:16]
        edge_ref[8 + k : 9 + k] = raw[15:16]
        edge_ref[16 + k : 17 + k] = last[7:8]
        edge_ref[24 + k : 25 + k] = u[0:1]
        edge_ref[32 + k : 33 + k] = first[0:1]
    surface = whole(own_ref[OWN_SURFACE], SURFACE)
    for n, values in enumerate((surface, *sums, bottom)):
        split_ref[ROWS * n : ROWS * (n + 1)] = values[:, :COLS]
        split_ref[ROWS * (6 + n) : ROWS * (7 + n)] = values[:, COLS:]
    for q in range(16):
        spot = pl.multiple_of(lax.rem(q + place, 16) * 8, 8)
        for half in range(2):
            if q < 12:
                rows = split_ref[pl.ds(ROWS * (6 * half + q // 2) + q % 2, 8, 2), :]
            else:
                rows = edge_ref[8 * (q - 12) : 8 * (q - 11), COLS * half : COLS * (half + 1)]
            stack_ref[half, pl.ds(spot, 8)] = rows
    turned_ref[HALO : HALO + COLS] = stack_ref[0].T
    beyond = stack_ref[1].T
    turned_ref[:HALO] = beyond[COLS - HALO :]
    turned_ref[HALO + COLS :] = beyond[:HALO]
    edge = edge_ref[32:40]
    sub = ids((8, COLS), 0)
    tile_lane = ids((8, COLS), 1)
    spare_block = tile_lane // 8 == lax.rem(6 + place, 16)
    moved = [at(edge, 8 * d - HALO + 4, 1)[:, :COLS] for d in range(MEMBERS)]
    halves = [at(x, 64, 1) for x in moved]
    rests = [jnp.where(tile_lane % 8 == sub, x[:, 64:65], 0.0) for x in moved]
    for step in (1, 2, 4):
        rests = [x + at(x, step, 0) for x in rests]
    for d in range(MEMBERS):
        pairs = jnp.where(tile_lane < 64, moved[d], at(halves[d], 1, 0))
        rest = rests[d]
        out_ref[d, :8] = jnp.where(
            sub == 0, pairs, jnp.where(sub == 1, at(pairs, 1, 0), turned_ref[8 * d : 8 * d + 8])
        )
        out_ref[d, 8 : SLAB - 8] = turned_ref[8 * d + 8 : 8 * d + SLAB - 8]
        end = turned_ref[8 * d + SLAB - 8 : 8 * d + SLAB]
        end = jnp.where((sub == 5) & spare_block, rest, end)
        end = jnp.where(sub == 6, at(pairs, -2, 0), end)
        out_ref[d, SLAB - 8 : SLAB] = jnp.where(sub == 7, at(pairs, -1, 0), end)

    block = ids((ROWS, COLS), 1) // 4
    flows = [(us[k], jnp.where(count_u > k, tracer_diffusion, 0.0)) for k in range(LEVELS)]

    def packed(which, half, ahead):
        tile = jnp.zeros((ROWS, COLS), f32)
        for k in range(LEVELS):
            values = flows[k][which][:, COLS * half : COLS * (half + 1)]
            tile = jnp.where(block % LEVELS == k, at(values, -4 * (k + ahead), 1), tile)
        for step in (32, 64):
            tile = jnp.where(block * 4 % (2 * step) < step, tile, at(tile, -step, 1))
        return tile

    last = PLANES // 4
    low, high = outer(
        at(west_ref[last], -4, 1), east_ref[last], left_ref[last], at(right_ref[last], -4, 1),
        packed(0, 1, 1), packed(0, 0, 0), packed(0, 0, 1), packed(1, 1, 1), packed(1, 0, 1),
    )
    high = at(high, 4, 1)
    planes = range(TRACERS * LEVELS)
    sides = [
        at(jnp.where(block == n, low, jnp.where(block == (n + 31) % 32, high, 0.0)), 4 * n, 1)
        for n in planes
    ]
    for n in planes:
        rows = slice(ROWS * n, ROWS * (n + 1))
        along_ref[rows] = inner_ref[rows] + sides[n]


    def spare(n):
        t, k = divmod(n, LEVELS)
        if t == 0:
            return us[k][:, :COLS], us[k][:, :COLS]
        if t == 1:
            return raws[k][:, :COLS], vs[k][:, :COLS]
        if t == 2:
            return raws[k][:, COLS:], us[k][:, COLS:]
        if k < 2:
            own = bottom[:, COLS * k : COLS * (k + 1)]
            return own, own
        return None

    def tops(n):
        own = c[n // LEVELS][n % LEVELS][8:]
        more = spare(n)
        return own if more is None else jnp.where(sub == 4, at(more[0][8:], 3, 0), own)

    def bottoms(n):
        own = c[n // LEVELS][n % LEVELS][:8]
        more = spare(n)
        return own if more is None else jnp.where(sub == 3, at(more[1][:8], -3, 0), own)

    for m in range(MEMBERS):
        out_ref[m, MAIL_N:MAIL_S] = jnp.where(sub >= 4, tops(2 * m), at(tops(2 * m + 1), 4, 0))
        out_ref[m, MAIL_S:CHUNK] = jnp.where(sub < 4, bottoms(2 * m), at(bottoms(2 * m + 1), 4, 0))


def slab_kernel(in_ref, out_ref, edge_ref):
    shape = (SLAB, COLS)
    lane = ids(shape, 1)
    r = lane % 8
    block = ids((8, COLS), 1) // 8

    tiles = []
    for t in range(SLAB // 8):
        now = [in_ref[a, 8 * t : 8 * t + 8] for a in range(MEMBERS)]
        for bit in (1, 2, 4, 8):
            odd = (block & bit) > 0
            now = [jnp.where(odd, now[(a + bit) % MEMBERS], now[a]) for a in range(MEMBERS)]
        tiles.append([at(now[-q % MEMBERS], 8 * q, 1) for q in range(16)])
    blocks = [jnp.concatenate([tile[q] for tile in tiles], axis=0) for q in range(16)]
    surface, start_u, start_v, force_u, force_v, bottom = (blocks[2 * n : 2 * n + 2] for n in range(6))
    u_a, v_raw, near, u_next = blocks[12:]
    zeros = jnp.zeros((8, COLS), f32)
    sub = ids((8, COLS), 0)
    edge_ref[COLS - 8 :] = zeros
    for a in range(1, MEMBERS):
        begin, end = in_ref[a, :8], in_ref[a, SLAB - 8 : SLAB]
        rows = jnp.where(sub < 2, begin, at(begin, -1, 0))
        rows = jnp.where(sub < 4, rows, jnp.where(sub < 6, at(end, 2, 0), at(end, 1, 0)))
        edge_ref[8 * a - 8 : 8 * a] = jnp.where(sub % 2 == 0, rows, at(at(rows, 64, 1), -1, 0))
    column = ids(shape, 0)
    far = at(edge_ref[...].T[:SLAB], -4, 0)
    far = jnp.where(column == 68, at(at(force_u[0], 1, 0), 8, 1), far)
    unused = (column < 2) | (column >= SLAB - 2)
    bottom = [jnp.where(unused, float(LEVELS), b) for b in bottom]

    top = lane == COLS - 1
    count_u = [jnp.minimum(b, at(b, 1, 0)) for b in bottom]
    count_v = [
        jnp.minimum(*bottom),
        jnp.where(top, 0.0, jnp.minimum(bottom[1], at(bottom[0], 1, 1))),
    ]

    ahead = jnp.concatenate([count_u[0], count_v[0]], axis=0)
    first = (ids(ahead.shape, 1) % 8 == 0) & (ids(ahead.shape, 1) > 0)
    counts = jnp.concatenate(
        [
            jnp.where(r == 7, count_u[1], 0.0),
            jnp.where(r == 7, count_v[1], 0.0),
            jnp.where(r == 7, count_v[0], 0.0),
            at(jnp.where(first, ahead, 0.0), 1, 1),
        ],
        axis=0,
    )
    for step in (1, 2, 4):
        counts = counts + at(counts, step, 1)
    count_ua, count_va, count_vc, count_ub, count_vb = (
        counts[SLAB * n : SLAB * (n + 1)] for n in range(5)
    )
    level = r.astype(f32)
    last = lane >= COLS - 8
    v_a = jnp.where(count_va > level, v_raw, 0.0)
    u_a = jnp.where(last, 0.0, u_a)
    u_b = jnp.where(last, 0.0, at(u_next, 8, 1))
    f_a = 0.25 * coriolis(lane // 8 * ROWS + 15, 0.5)
    f_b = f_a + 0.25 * coriolis_base / NLAT
    pair = v_a + at(v_a, 1, 0)
    spread = viscosity * (at(v_a, 1, 0) + at(v_a, -1, 0) - 4.0 * v_a)
    terms = jnp.concatenate(
        [
            jnp.where(count_ua > level, f_a * pair + viscosity * u_b, 0.0),
            jnp.where(count_ub > level, f_b * pair + viscosity * u_a, 0.0),
            jnp.where(count_vb > level, viscosity * v_a, 0.0),
            jnp.where(count_vc > level, viscosity * v_a, 0.0),
            jnp.where(count_va > level, near + far + spread, 0.0),
            v_a,
        ],
        axis=0,
    )
    for step in (1, 2, 4):
        terms = terms + at(terms, -step, 1)
    shifted = at(terms[SLAB : 3 * SLAB], -1, 1)
    u_15, v_14, v_15, begin_15 = (
        jnp.where(r == 7, terms[SLAB * n : SLAB * (n + 1)], 0.0) for n in (0, 3, 4, 5)
    )
    u_16, v_16 = (jnp.where(r == 0, shifted[SLAB * n : SLAB * (n + 1)], 0.0) for n in range(2))
    force_u = [force_u[0] + u_16, force_u[1] + u_15]
    force_v = [force_v[0] + (v_14 + v_16), force_v[1] + v_15]
    start_v = [start_v[0], start_v[1] + begin_15]

    sub_step = time_step / SUBSTEPS
    held_u, held_v, flux_u, flux_v, begin_u, begin_v = [], [], [], [], [], []
    for i in range(2):
        per = 1.0 / jnp.maximum(count_u[i], 1.0)
        open_face = jnp.where(count_u[i] > 0.0, sub_step, 0.0)
        flux_u.append((sub_step * surface_scale * thickness) * count_u[i])
        held_u.append(
            (
                (0.25 * open_face) * coriolis(2 * lane + i, 0.5),
                gravity * open_face,
                open_face * (force_u[i] * per),
            )
        )
        begin_u.append(start_u[i] * per)
        per = 1.0 / jnp.maximum(count_v[i], 1.0)
        open_face = jnp.where(count_v[i] > 0.0, sub_step, 0.0)
        flux_v.append((sub_step * surface_scale * thickness) * count_v[i])
        held_v.append(
            (
                (-0.25 * open_face) * coriolis(2 * lane + i, 1.0),
                gravity * open_face,
                open_face * (force_v[i] * per),
            )
        )
        begin_v.append(start_v[i] * per)
    held = (
        *flux_u, at(flux_u[0], 1, 1), *flux_v, at(flux_v[0], 1, 1), at(flux_v[1], -1, 1),
        *held_u[0], *held_u[1], *held_v[0], *held_v[1],
    )
    state = (*surface, at(surface[0], 1, 1), *begin_u, *begin_v)
    total = (zeros,) * 4
    for low, steps in ((0, 6), (8, 8), (16, 8), (24, 8)):
        cut = 8 if low else 0
        state = tuple(x[cut : x.shape[0] - cut] for x in state)
        (
            du0, du1, du2, dv0, dv1, dv2, dv_, cu0, gu0, fu0, cu1, gu1, fu1,
            cv0, gv0, fv0, cv1, gv1, fv1,
        ) = (x[low : SLAB - low] for x in held)
        centre = HALO - low

        def advance(_, carry):
            h0, h1, h2, u0, u1, v0, v1, *sums = carry
            v_ = at(v1, -1, 1)
            u2 = at(u0, 1, 1)
            v2 = at(v0, 1, 1)
            x0, x1, x2 = du0 * u0, du1 * u1, du2 * u2
            y0, y1 = dv0 * v0, dv1 * v1
            h1 = h1 - ((x1 - at(x1, -1, 0)) + (y1 - y0))
            h0 = h0 - ((x0 - at(x0, -1, 0)) + (y0 - dv_ * v_))
            h2 = h2 - ((x2 - at(x2, -1, 0)) + (dv2 * v2 - y1))
            p0, p1, p2 = u0 + at(u0, -1, 0), u1 + at(u1, -1, 0), u2 + at(u2, -1, 0)
            q0, q1 = v0 + v_, v1 + v0
            u0 = (u0 + fu0) + (cu0 * (q0 + at(q0, 1, 0)) - gu0 * (at(h0, 1, 0) - h0))
            u1 = (u1 + fu1) + (cu1 * (q1 + at(q1, 1, 0)) - gu1 * (at(h1, 1, 0) - h1))
            v0 = (v0 + fv0) + (cv0 * (p0 + p1) - gv0 * (h1 - h0))
            v1 = (v1 + fv1) + (cv1 * (p1 + p2) - gv1 * (h2 - h1))
            sums = [a + b[centre : centre + 8] for a, b in zip(sums, (u0, u1, v0, v1))]
            return (h0, h1, h2, u0, u1, v0, v1, *sums)

        *state, a0, a1, a2, a3 = lax.fori_loop(
            0, steps, advance, (*state, *total), unroll=True
        )
        total = (a0, a1, a2, a3)
    height = [x[8:16] for x in state[:2]]
    average = [x * (1.0 / SUBSTEPS) for x in total]
    transport = [
        (-thickness * count_u[i][HALO : HALO + 8]) * average[i] for i in range(2)
    ]
    square = (COLS, COLS)
    before = (ids(square, 0) < ids(square, 1)).astype(f32)
    south = jnp.dot(
        transport[0] + transport[1],
        before,
        precision=lax.Precision.HIGHEST,
        preferred_element_type=f32,
    )
    stream = [south + transport[0], south + (transport[0] + transport[1])]
    results = [*height, *stream, *average]
    moved = [at(values, -8 * n, 1) for n, values in enumerate(results)]
    for e in range(MEMBERS):
        packed = moved[0]
        for n in range(1, 8):
            packed = jnp.where(block == (e + n) % 16, moved[n], packed)
        out_ref[e, 0:8] = packed
        out_ref[e, 8:16] = in_ref[(e + 15) % MEMBERS, MAIL_N:MAIL_S]
        out_ref[e, 16:24] = in_ref[(e + 1) % MEMBERS, MAIL_S:CHUNK]


def gain(values, axis, flow, diffusion):
    ahead = at(values, 1, axis)
    sides = at(values, -1, axis) + at(values, 2, axis)
    far = at(values, -2, axis) + at(values, 3, axis)
    face = (37.0 * (values + ahead) - 8.0 * sides + far) * (1.0 / 60.0)
    flux = diffusion * (ahead - values) - flow * face
    return flux - at(flux, -1, axis)


def inner_kernel(own_ref, out_ref):
    bottom = own_ref[OWN_BOTTOM]
    c = tracer_planes(own_ref)
    count = jnp.minimum(bottom, at(bottom, 1, 1))
    values = jnp.concatenate([plane for tracer in c for plane in tracer], axis=0)
    flow, diffusion = [], []
    for k in range(LEVELS):
        flow.append(jnp.where(count > k, own_ref[OWN_EAST + k], 0.0))
        diffusion.append(jnp.where(count > k, tracer_diffusion, 0.0))
    flow, diffusion = (jnp.concatenate(x * TRACERS, axis=0) for x in (flow, diffusion))
    lane = ids(values.shape, 1)

    def moved(step):
        inside = lane < COLS - step if step > 0 else lane >= -step
        return jnp.where(inside, at(values, step, 1), 0.0)

    ahead = moved(1)
    face = (37.0 * (values + ahead) - 8.0 * (moved(-1) + moved(2)) + (moved(-2) + moved(3))) * (
        1.0 / 60.0
    )
    flux = jnp.where(lane < COLS - 1, diffusion * (ahead - values) - flow * face, 0.0)
    out_ref[...] = flux - at(flux, -1, 1)


def outer(west, east, left, right, flow_w, flow_l, flow_r, diff_w, diff_r):
    q = ids((ROWS, COLS), 1) % 4
    sixtieth = 1.0 / 60.0
    w1, w2, w3 = at(west, 3, 1), at(west, 2, 1), at(west, 1, 1)
    face = 37.0 * (w1 + left) - 8.0 * (w2 + at(left, 1, 1)) + (w3 + at(left, 2, 1))
    through = at(diff_w, 3, 1) * (left - w1) - at(flow_w, 3, 1) * (face * sixtieth)
    flux = jnp.where(q == 0, w2 - 8.0 * w1, jnp.where(q == 1, w2, 0.0)) * (-sixtieth) * flow_l
    low = flux - at(flux, -1, 1) - jnp.where(q == 0, through, 0.0)
    e1, e2, e3 = at(east, -3, 1), at(east, -2, 1), at(east, -1, 1)
    face = 37.0 * (right + e1) - 8.0 * (at(right, -1, 1) + e2) + (at(right, -2, 1) + e3)
    through = diff_r * (e1 - right) - flow_r * (face * sixtieth)
    flux = jnp.where(q == 2, e3 - 8.0 * e2, jnp.where(q == 1, e3, 0.0)) * (-sixtieth) * flow_r
    high = flux - at(flux, -1, 1) + jnp.where(q == 3, through, 0.0)
    return low, high


def finish_kernel(
    place_ref, in_ref, own_ref, west_ref, east_ref, along_ref,
    tracers_out, velocity_out, height_out, stream_out, turned_ref, rows_ref,
):
    place = place_ref[0]
    turned_ref[...] = in_ref[:, 0:8].reshape(COLS, COLS).T

    for q in range(8):
        spot = pl.multiple_of(lax.rem(q + place, 16) * 8, 8)
        rows_ref[pl.ds(ROWS * (q // 2) + q % 2, 8, 2), :] = turned_ref[pl.ds(spot, 8)]
    height_out[...] = rows_ref[:ROWS]
    stream_out[...] = rows_ref[ROWS : 2 * ROWS]
    average_u, average_v = rows_ref[2 * ROWS : 3 * ROWS], rows_ref[3 * ROWS :]

    sub = ids((8, COLS), 0)
    tall = (ROWS + 8, 2 * COLS)
    row = ids(tall, 0)
    first, last = place == 0, place == MEMBERS - 1

    def lat_tile(n):
        south = jnp.where(first, 0.0, in_ref[n // 2, 8:16])
        north = jnp.where(last, 0.0, in_ref[n // 2, 16:24])
        if n % 2 == 0:
            return jnp.where(sub < 4, north, south)
        return at(jnp.where(sub < 4, south, north), 4, 0)

    def spare_north(tile):
        return jnp.where(sub == 0, at(tile, 3, 0), 0.0)

    def spare_south(tile):
        return jnp.where(sub == 7, at(tile, -3, 0), 0.0)

    def tallen(own, tile):
        return jnp.concatenate([own, tile], axis=0)

    def whole(own, plane):
        return wide(own, beside_plane(west_ref, east_ref, plane))

    tiles = [[lat_tile(LEVELS * t + k) for k in range(LEVELS)] for t in range(TRACERS)]
    bottom_own = own_ref[OWN_BOTTOM]
    c = tracer_planes(own_ref)
    p_own = pressures(c[1], c[0])
    p_tile = pressures(tiles[1], tiles[0])
    both = wide(
        spare_north(tiles[3][0]) + spare_south(tiles[3][0]),
        spare_north(tiles[3][1]) + spare_south(tiles[3][1]),
    )
    bottom = tallen(whole(bottom_own, BOTTOM), both)
    count_u = jnp.minimum(bottom, at(bottom, 1, 1))
    count_v = jnp.minimum(bottom, at(bottom, 1, 0))
    f_u = coriolis(place * ROWS + row, 0.5)
    f_v = coriolis(place * ROWS + row, 1.0)
    none = jnp.zeros((8, COLS), f32)
    wind = [tallen(wide(own_ref[OWN_WIND + d], jnp.zeros((ROWS, COLS), f32)), jnp.zeros((8, 2 * COLS), f32)) for d in range(2)]

    def up(x):
        return at(x, 1, 0)

    def down(x):
        return at(x, -1, 0)

    stars_u, stars_v, gains = [], [], [None] * (TRACERS * LEVELS)
    own_u, own_v = count_u[:ROWS, :COLS], count_v[:ROWS, :COLS]
    mean_u = mean_v = jnp.zeros((ROWS, COLS), f32)
    for k in range(LEVELS):
        east, north = count_u > k, count_v > k
        t0, t1, t2 = tiles[0][k], tiles[1][k], tiles[2][k]
        u_lat = wide(spare_north(t0) + spare_south(t0), spare_north(t2))
        v_lat = wide(spare_north(t1) + spare_south(t1), spare_south(t2))
        u = tallen(whole(own_ref[OWN_EAST + k], EAST + k), u_lat)
        u = jnp.where(east | (row >= ROWS), u, 0.0)
        v = tallen(whole(own_ref[OWN_NORTH + k], NORTH + k), v_lat)
        v = jnp.where(north | (row == ROWS), v, 0.0)
        p = tallen(whole(p_own[k], PRESSURE + k), wide(p_tile[k], none))
        tend_u, tend_v = momentum(k, u, v, p, wind, east, north, f_u, f_v, up, down)
        star_u = (u + time_step * tend_u)[:ROWS, :COLS]
        star_v = (v + time_step * tend_v)[:ROWS, :COLS]
        stars_u.append(star_u)
        stars_v.append(star_v)
        mean_u = mean_u + star_u
        mean_v = mean_v + star_v

        diffusion = jnp.where(north[:, :COLS], tracer_diffusion, 0.0)
        for t in range(TRACERS):
            cn = tallen(c[t][k], tiles[t][k])
            gains[LEVELS * t + k] = gain(cn, 0, v[:, :COLS], diffusion)[:ROWS]
    for n in range(TRACERS * LEVELS):
        t, k = divmod(n, LEVELS)
        change = along_ref[ROWS * n : ROWS * (n + 1)] + gains[n]
        tracers_out[t, k] = jnp.where(bottom_own > k, c[t][k] + time_step * change, 0.0)
    shift_u = average_u - mean_u / jnp.maximum(own_u, 1.0)
    shift_v = average_v - mean_v / jnp.maximum(own_v, 1.0)
    for k in range(LEVELS):
        velocity_out[0, k] = jnp.where(own_u > k, stars_u[k] + shift_u, 0.0)
        velocity_out[1, k] = jnp.where(own_v > k, stars_v[k] + shift_v, 0.0)


def ring(axis, step):
    count = lax.axis_size(axis)
    return [(i, (i + step) % count) for i in range(count)]


def struct(*shape):
    return jax.ShapeDtypeStruct(shape, f32)


def vmem(*shape):
    return pltpu.VMEM(shape, f32)


def specs(count, scalars=0):
    return [pl.BlockSpec(memory_space=pltpu.SMEM)] * scalars + [
        pl.BlockSpec(memory_space=pltpu.VMEM)
    ] * count


PARAMS = pltpu.CompilerParams(vmem_limit_bytes=32 * 1024 * 1024)


def stacked(tracers, velocity, surface, wind, bottom):
    def put(values, first):
        values = values.reshape(-1, ROWS, COLS)
        after = OWN - first - values.shape[0]
        return lax.pad(
            values, jnp.zeros((), values.dtype), ((first, after, 0), (0, 0, 0), (0, 0, 0))
        )

    return (
        put(tracers, 0)
        + put(velocity, OWN_EAST)
        + put(surface, OWN_SURFACE)
        + put(wind, OWN_WIND)
        + put(bottom, OWN_BOTTOM).astype(f32)
    )


def shards(tracers, velocity, surface, wind, bottom):
    place = lax.axis_index("lat").astype(jnp.int32).reshape(1)
    own = stacked(tracers, velocity, surface, wind, bottom)
    payload = struct(PLANES // 4 + 1, ROWS, COLS)
    to_right, to_left = pl.pallas_call(
        pack_kernel,
        out_shape=(payload, payload),
        in_specs=specs(1),
        out_specs=tuple(specs(2)),
        compiler_params=PARAMS,
        name="pack",
    )(own)
    west = lax.ppermute(to_right, "lon", ring("lon", 1))
    east = lax.ppermute(to_left, "lon", ring("lon", -1))
    inner = pl.pallas_call(
        inner_kernel,
        out_shape=struct(TRACERS * LEVELS * ROWS, COLS),
        in_specs=specs(1),
        out_specs=specs(1)[0],
        compiler_params=PARAMS,
        cost_estimate=pl.CostEstimate(flops=1500000, bytes_accessed=3000000, transcendentals=0),
        name="inner",
    )(own)
    chunks, along = pl.pallas_call(
        send_kernel,
        out_shape=(
            struct(MEMBERS, CHUNK, COLS),
            struct(TRACERS * LEVELS * ROWS, COLS),
        ),
        in_specs=specs(6, 1),
        out_specs=tuple(specs(2)),
        scratch_shapes=[
            vmem(12 * ROWS, COLS),
            vmem(2, COLS, COLS),
            vmem(40, 2 * COLS),
            vmem(COLS + 2 * HALO, COLS),
        ],
        compiler_params=PARAMS,
        name="columns",
    )(place, own, west, east, to_right, to_left, inner)
    slabs = lax.all_to_all(chunks, "lat", 0, 0, tiled=True)
    answers = pl.pallas_call(
        slab_kernel,
        out_shape=struct(MEMBERS, BACK, COLS),
        in_specs=specs(1),
        out_specs=specs(1)[0],
        scratch_shapes=[vmem(COLS, COLS)],
        compiler_params=PARAMS,
        name="substeps",
    )(slabs)
    home = lax.all_to_all(answers, "lat", 0, 0, tiled=True)
    return pl.pallas_call(
        finish_kernel,
        out_shape=(
            struct(TRACERS, LEVELS, ROWS, COLS),
            struct(2, LEVELS, ROWS, COLS),
            struct(ROWS, COLS),
            struct(ROWS, COLS),
        ),
        in_specs=specs(5, 1),
        out_specs=tuple(specs(4)),
        scratch_shapes=[vmem(COLS, COLS), vmem(4 * ROWS, COLS)],
        compiler_params=PARAMS,
        name="finish",
    )(place, home, own, west, east, along)


def solution(mesh):
    placed = (
        P(None, None, "lat", "lon"),
        P(None, None, "lat", "lon"),
        P("lat", "lon"),
        P(None, "lat", "lon"),
        P("lat", "lon"),
    )
    return jax.shard_map(
        shards,
        mesh=mesh,
        in_specs=placed,
        out_specs=(
            P(None, None, "lat", "lon"),
            P(None, None, "lat", "lon"),
            P("lat", "lon"),
            P("lat", "lon"),
        ),
        check_vma=False,
    )
```

```python
import jax
import jax.numpy as jnp
from jax import lax
from jax.experimental import pallas as pl
from jax.experimental.pallas import tpu as pltpu
from jax.sharding import PartitionSpec as P

TRACERS = 4
LEVELS = 8
SUBSTEPS = 30
ROWS = 16
COLS = 128
MEMBERS = 16
HALO = 32
SLAB = 72
NLAT = ROWS * MEMBERS

time_step = 0.2
tracer_diffusion = 0.2
viscosity = 0.2
thermal_expansion = 2.0
haline_contraction = 1.5
coriolis_base = 1.0
gravity = 140.0
surface_scale = 40.0
thickness = 1.0 / LEVELS
f32 = jnp.float32

PRESSURE, EAST, NORTH, WIND, SURFACE, BOTTOM = 0, 8, 16, 24, 26, 27
PLANES = 28
OWN_EAST, OWN_NORTH, OWN_SURFACE, OWN_WIND, OWN_BOTTOM, OWN = 32, 40, 48, 49, 51, 52
MAIL_N, MAIL_S, CHUNK = SLAB, SLAB + 8, SLAB + 16
BACK = 24


def at(values, step, axis):
    size = values.shape[axis]
    step %= size
    return values if step == 0 else pltpu.roll(values, size - step, axis)


def ids(shape, axis):
    return lax.broadcasted_iota(jnp.int32, shape, axis)


def wide(own, beside):
    return jnp.concatenate([own, beside], axis=1)


def tracer_planes(own_ref):
    bottom = own_ref[OWN_BOTTOM]
    return [
        [jnp.where(bottom > k, own_ref[LEVELS * t + k], 0.0) for k in range(LEVELS)]
        for t in range(TRACERS)
    ]


def pressures(salt, heat):
    total, out = None, []
    for k in range(LEVELS):
        density = haline_contraction * salt[k] - thermal_expansion * heat[k]
        total = density if total is None else total + density
        out.append(thickness * total)
    return out


def pack_kernel(own_ref, right_ref, left_ref):
    c = tracer_planes(own_ref)
    planes = pressures(c[1], c[0])
    planes += [own_ref[n] for n in range(OWN_EAST, OWN_SURFACE)]
    planes += [own_ref[n] for n in (OWN_WIND, OWN_WIND + 1, OWN_SURFACE, OWN_BOTTOM)]
    lane = ids((ROWS, COLS), 1)
    for q in range(PLANES // 4):
        right = left = jnp.zeros((ROWS, COLS), f32)
        for s in range(4):
            moved = at(planes[4 * q + s], -32 * s, 1)
            right = jnp.where(lane // 32 == (s + 3) % 4, moved, right)
            left = jnp.where(lane // 32 == s, moved, left)
        right_ref[q] = right
        left_ref[q] = left
    right = left = jnp.zeros((ROWS, COLS), f32)
    for n in range(TRACERS * LEVELS):
        moved = at(c[n // LEVELS][n % LEVELS], -4 * n, 1)
        right = jnp.where(lane // 4 == (n + 31) % 32, moved, right)
        left = jnp.where(lane // 4 == n, moved, left)
    right_ref[PLANES // 4] = right
    left_ref[PLANES // 4] = left


def beside_plane(west_ref, east_ref, plane):
    q, s = divmod(plane, 4)
    block = ids((ROWS, COLS), 1) // 32
    both = jnp.where(
        block == s, east_ref[q], jnp.where(block == (s + 3) % 4, west_ref[q], 0.0)
    )
    return at(both, 32 * s, 1)


def momentum(k, u, v, p, wind, east, north, f_u, f_v, up, down):
    pair_v = v + down(v)
    pair_u = u + at(u, -1, 1)
    tend_u = (
        (0.25 * f_u) * (pair_v + at(pair_v, 1, 1))
        - (at(p, 1, 1) - p)
        + viscosity * (at(u, 1, 1) + at(u, -1, 1) + up(u) + down(u) - 4.0 * u)
    )
    tend_v = (
        (-0.25 * f_v) * (pair_u + up(pair_u))
        - (up(p) - p)
        + viscosity * (at(v, 1, 1) + at(v, -1, 1) + up(v) + down(v) - 4.0 * v)
    )
    if k == 0:
        tend_u = tend_u + wind[0]
        tend_v = tend_v + wind[1]
    return jnp.where(east, tend_u, 0.0), jnp.where(north, tend_v, 0.0)


def coriolis(rows, offset):
    return coriolis_base * (0.5 + (rows.astype(f32) + offset) / NLAT)


def send_kernel(
    place_ref, own_ref, west_ref, east_ref, _,
    out_ref, flows_ref, split_ref, stack_ref, edge_ref, turned_ref,
):
    place = place_ref[0]
    c = tracer_planes(own_ref)
    p_own = pressures(c[1], c[0])

    def whole(own, plane):
        return wide(own, beside_plane(west_ref, east_ref, plane))

    shape = (ROWS, 2 * COLS)
    row = ids(shape, 0)
    bottom = whole(own_ref[OWN_BOTTOM], BOTTOM)
    wind = [whole(own_ref[OWN_WIND + d], WIND + d) for d in range(2)]

    def up(x):
        return jnp.where(row == ROWS - 1, 0.0, at(x, 1, 0))

    def down(x):
        return jnp.where(row == 0, 0.0, at(x, -1, 0))

    count_u = jnp.minimum(bottom, at(bottom, 1, 1))
    count_v = jnp.minimum(bottom, up(bottom))
    f_u = coriolis(place * ROWS + row, 0.5)
    f_v = coriolis(place * ROWS + row, 1.0)
    sums = [jnp.zeros(shape, f32) for _ in range(4)]
    us, vs, raws = [], [], []
    for k in range(LEVELS):
        east, north = count_u > k, count_v > k
        u = jnp.where(east, whole(own_ref[OWN_EAST + k], EAST + k), 0.0)
        raw = jnp.where(bottom > k, whole(own_ref[OWN_NORTH + k], NORTH + k), 0.0)
        v = jnp.where(north, raw, 0.0)
        p = whole(p_own[k], PRESSURE + k)
        tend_u, tend_v = momentum(k, u, v, p, wind, east, north, f_u, f_v, up, down)
        sums = [a + b for a, b in zip(sums, (u, v, tend_u, tend_v))]
        us.append(u)
        vs.append(v)
        raws.append(raw)
        pair = u + at(u, -1, 1)
        last = p[8:] + (-0.25 * f_v[8:]) * pair[8:] + viscosity * at(v, -1, 0)[8:]
        if k == 0:
            last = last + wind[1][8:]
        first = (-0.25 * (f_v[:8] - 1.0 / NLAT)) * pair[:8] - p[:8] + viscosity * v[:8]
        edge_ref[k : k + 1] = u[15:16]
        edge_ref[8 + k : 9 + k] = raw[15:16]
        edge_ref[16 + k : 17 + k] = last[7:8]
        edge_ref[24 + k : 25 + k] = u[0:1]
        edge_ref[32 + k : 33 + k] = first[0:1]
    surface = whole(own_ref[OWN_SURFACE], SURFACE)
    for n, values in enumerate((surface, *sums, bottom)):
        split_ref[ROWS * n : ROWS * (n + 1)] = values[:, :COLS]
        split_ref[ROWS * (6 + n) : ROWS * (7 + n)] = values[:, COLS:]
    for q in range(16):
        spot = pl.multiple_of(lax.rem(q + place, 16) * 8, 8)
        for half in range(2):
            if q < 12:
                rows = split_ref[pl.ds(ROWS * (6 * half + q // 2) + q % 2, 8, 2), :]
            else:
                rows = edge_ref[8 * (q - 12) : 8 * (q - 11), COLS * half : COLS * (half + 1)]
            stack_ref[half, pl.ds(spot, 8)] = rows
    turned_ref[HALO : HALO + COLS] = stack_ref[0].T
    beyond = stack_ref[1].T
    turned_ref[:HALO] = beyond[COLS - HALO :]
    turned_ref[HALO + COLS :] = beyond[:HALO]
    edge = edge_ref[32:40]
    sub = ids((8, COLS), 0)
    tile_lane = ids((8, COLS), 1)
    spare_block = tile_lane // 8 == lax.rem(6 + place, 16)
    moved = [at(edge, 8 * d - HALO + 4, 1)[:, :COLS] for d in range(MEMBERS)]
    halves = [at(x, 64, 1) for x in moved]
    rests = [jnp.where(tile_lane % 8 == sub, x[:, 64:65], 0.0) for x in moved]
    for step in (1, 2, 4):
        rests = [x + at(x, step, 0) for x in rests]
    for d in range(MEMBERS):
        pairs = jnp.where(tile_lane < 64, moved[d], at(halves[d], 1, 0))
        rest = rests[d]
        out_ref[d, :8] = jnp.where(
            sub == 0, pairs, jnp.where(sub == 1, at(pairs, 1, 0), turned_ref[8 * d : 8 * d + 8])
        )
        out_ref[d, 8 : SLAB - 8] = turned_ref[8 * d + 8 : 8 * d + SLAB - 8]
        end = turned_ref[8 * d + SLAB - 8 : 8 * d + SLAB]
        end = jnp.where((sub == 5) & spare_block, rest, end)
        end = jnp.where(sub == 6, at(pairs, -2, 0), end)
        out_ref[d, SLAB - 8 : SLAB] = jnp.where(sub == 7, at(pairs, -1, 0), end)

    for n, values in enumerate((*us, count_u)):
        flows_ref[ROWS * n : ROWS * (n + 1)] = values


    def spare(n):
        t, k = divmod(n, LEVELS)
        if t == 0:
            return us[k][:, :COLS], us[k][:, :COLS]
        if t == 1:
            return raws[k][:, :COLS], vs[k][:, :COLS]
        if t == 2:
            return raws[k][:, COLS:], us[k][:, COLS:]
        if k < 2:
            own = bottom[:, COLS * k : COLS * (k + 1)]
            return own, own
        return None

    def tops(n):
        own = c[n // LEVELS][n % LEVELS][8:]
        more = spare(n)
        return own if more is None else jnp.where(sub == 4, at(more[0][8:], 3, 0), own)

    def bottoms(n):
        own = c[n // LEVELS][n % LEVELS][:8]
        more = spare(n)
        return own if more is None else jnp.where(sub == 3, at(more[1][:8], -3, 0), own)

    for m in range(MEMBERS):
        out_ref[m, MAIL_N:MAIL_S] = jnp.where(sub >= 4, tops(2 * m), at(tops(2 * m + 1), 4, 0))
        out_ref[m, MAIL_S:CHUNK] = jnp.where(sub < 4, bottoms(2 * m), at(bottoms(2 * m + 1), 4, 0))


def edge_steps(flows_ref, west_ref, east_ref, right_ref, left_ref, inner_ref, along_ref):
    block = ids((ROWS, COLS), 1) // 4
    count = flows_ref[ROWS * LEVELS :]

    def packed(of_level, half, ahead):
        tile = jnp.zeros((ROWS, COLS), f32)
        for k in range(LEVELS):
            values = of_level(k)[:, COLS * half : COLS * (half + 1)]
            tile = jnp.where(block % LEVELS == k, at(values, -4 * (k + ahead), 1), tile)
        return tile

    def repeated(tile):
        for step in (32, 64):
            tile = jnp.where(block * 4 % (2 * step) < step, tile, at(tile, -step, 1))
        return tile

    def flow(k):
        return flows_ref[ROWS * k : ROWS * (k + 1)]

    def diffusion(k):
        return jnp.where(count > k, tracer_diffusion, 0.0)

    tiles = []
    for what in ((flow, 1, 1), (flow, 0, 0), (flow, 0, 1), (diffusion, 1, 1), (diffusion, 0, 1)):
        tiles.append(packed(*what))
        yield
    tiles = [repeated(tile) for tile in tiles]
    yield
    last = PLANES // 4
    low, high = outer(
        at(west_ref[last], -4, 1), east_ref[last], left_ref[last], at(right_ref[last], -4, 1),
        *tiles,
    )
    high = at(high, 4, 1)
    yield
    waiting = []
    for n in range(TRACERS * LEVELS):
        both = jnp.where(block == n, low, jnp.where(block == (n + 31) % 32, high, 0.0))
        waiting.append((slice(ROWS * n, ROWS * (n + 1)), at(both, 4 * n, 1)))
        if n % 2:
            yield
    for rows, side in waiting:
        along_ref[rows] = inner_ref[rows] + side


def slab_kernel(
    in_ref, flows_ref, west_ref, east_ref, right_ref, left_ref, inner_ref,
    out_ref, along_ref, edge_ref,
):
    shape = (SLAB, COLS)
    lane = ids(shape, 1)
    r = lane % 8
    block = ids((8, COLS), 1) // 8

    tiles = []
    for t in range(SLAB // 8):
        now = [in_ref[a, 8 * t : 8 * t + 8] for a in range(MEMBERS)]
        for bit in (1, 2, 4, 8):
            odd = (block & bit) > 0
            now = [jnp.where(odd, now[(a + bit) % MEMBERS], now[a]) for a in range(MEMBERS)]
        tiles.append([at(now[-q % MEMBERS], 8 * q, 1) for q in range(16)])
    blocks = [jnp.concatenate([tile[q] for tile in tiles], axis=0) for q in range(16)]
    surface, start_u, start_v, force_u, force_v, bottom = (blocks[2 * n : 2 * n + 2] for n in range(6))
    u_a, v_raw, near, u_next = blocks[12:]
    zeros = jnp.zeros((8, COLS), f32)
    sub = ids((8, COLS), 0)
    edge_ref[COLS - 8 :] = zeros
    for a in range(1, MEMBERS):
        begin, end = in_ref[a, :8], in_ref[a, SLAB - 8 : SLAB]
        rows = jnp.where(sub < 2, begin, at(begin, -1, 0))
        rows = jnp.where(sub < 4, rows, jnp.where(sub < 6, at(end, 2, 0), at(end, 1, 0)))
        edge_ref[8 * a - 8 : 8 * a] = jnp.where(sub % 2 == 0, rows, at(at(rows, 64, 1), -1, 0))
    column = ids(shape, 0)
    far = at(edge_ref[...].T[:SLAB], -4, 0)
    far = jnp.where(column == 68, at(at(force_u[0], 1, 0), 8, 1), far)
    unused = (column < 2) | (column >= SLAB - 2)
    bottom = [jnp.where(unused, float(LEVELS), b) for b in bottom]

    top = lane == COLS - 1
    count_u = [jnp.minimum(b, at(b, 1, 0)) for b in bottom]
    count_v = [
        jnp.minimum(*bottom),
        jnp.where(top, 0.0, jnp.minimum(bottom[1], at(bottom[0], 1, 1))),
    ]

    square = (COLS, COLS)

    def spread_from(lane_at, values):
        chosen = ids(square, 0) == ids(square, 1) // 8 * 8 + lane_at
        spread = jnp.dot(
            jnp.concatenate(values, axis=0).astype(jnp.bfloat16),
            chosen.astype(f32).astype(jnp.bfloat16),
            preferred_element_type=f32,
        )
        return [spread[SLAB * n : SLAB * (n + 1)] for n in range(len(values))]

    count_ua, count_va, count_vc = spread_from(7, [count_u[1], count_v[1], count_v[0]])
    count_ub, count_vb = spread_from(8, [count_u[0], count_v[0]])
    level = r.astype(f32)
    last = lane >= COLS - 8
    v_a = jnp.where(count_va > level, v_raw, 0.0)
    u_a = jnp.where(last, 0.0, u_a)
    u_b = jnp.where(last, 0.0, at(u_next, 8, 1))
    f_a = 0.25 * coriolis(lane // 8 * ROWS + 15, 0.5)
    f_b = f_a + 0.25 * coriolis_base / NLAT
    pair = v_a + at(v_a, 1, 0)
    spread = viscosity * (at(v_a, 1, 0) + at(v_a, -1, 0) - 4.0 * v_a)
    terms = jnp.concatenate(
        [
            jnp.where(count_ua > level, f_a * pair + viscosity * u_b, 0.0),
            jnp.where(count_ub > level, f_b * pair + viscosity * u_a, 0.0),
            jnp.where(count_vb > level, viscosity * v_a, 0.0),
            jnp.where(count_vc > level, viscosity * v_a, 0.0),
            jnp.where(count_va > level, near + far + spread, 0.0),
            v_a,
        ],
        axis=0,
    )
    for step in (1, 2, 4):
        terms = terms + at(terms, -step, 1)
    shifted = at(terms[SLAB : 3 * SLAB], -1, 1)
    u_15, v_14, v_15, begin_15 = (
        jnp.where(r == 7, terms[SLAB * n : SLAB * (n + 1)], 0.0) for n in (0, 3, 4, 5)
    )
    u_16, v_16 = (jnp.where(r == 0, shifted[SLAB * n : SLAB * (n + 1)], 0.0) for n in range(2))
    force_u = [force_u[0] + u_16, force_u[1] + u_15]
    force_v = [force_v[0] + (v_14 + v_16), force_v[1] + v_15]
    start_v = [start_v[0], start_v[1] + begin_15]

    sub_step = time_step / SUBSTEPS
    held_u, held_v, flux_u, flux_v, begin_u, begin_v = [], [], [], [], [], []
    for i in range(2):
        per = 1.0 / jnp.maximum(count_u[i], 1.0)
        open_face = jnp.where(count_u[i] > 0.0, sub_step, 0.0)
        flux_u.append((sub_step * surface_scale * thickness) * count_u[i])
        held_u.append(
            (
                (0.25 * open_face) * coriolis(2 * lane + i, 0.5),
                gravity * open_face,
                open_face * (force_u[i] * per),
            )
        )
        begin_u.append(start_u[i] * per)
        per = 1.0 / jnp.maximum(count_v[i], 1.0)
        open_face = jnp.where(count_v[i] > 0.0, sub_step, 0.0)
        flux_v.append((sub_step * surface_scale * thickness) * count_v[i])
        held_v.append(
            (
                (-0.25 * open_face) * coriolis(2 * lane + i, 1.0),
                gravity * open_face,
                open_face * (force_v[i] * per),
            )
        )
        begin_v.append(start_v[i] * per)
    held = (
        *flux_u, at(flux_u[0], 1, 1), *flux_v, at(flux_v[0], 1, 1), at(flux_v[1], -1, 1),
        *held_u[0], *held_u[1], *held_v[0], *held_v[1],
    )
    state = (*surface, at(surface[0], 1, 1), *begin_u, *begin_v)
    total = (zeros,) * 4
    beside = edge_steps(flows_ref, west_ref, east_ref, right_ref, left_ref, inner_ref, along_ref)
    for low, steps in ((0, 6), (8, 8), (16, 8), (24, 8)):
        cut = 8 if low else 0
        state = tuple(x[cut : x.shape[0] - cut] for x in state)
        (
            du0, du1, du2, dv0, dv1, dv2, dv_, cu0, gu0, fu0, cu1, gu1, fu1,
            cv0, gv0, fv0, cv1, gv1, fv1,
        ) = (x[low : SLAB - low] for x in held)
        centre = HALO - low

        def advance(_, carry):
            h0, h1, h2, u0, u1, v0, v1, *sums = carry
            v_ = at(v1, -1, 1)
            u2 = at(u0, 1, 1)
            v2 = at(v0, 1, 1)
            x0, x1, x2 = du0 * u0, du1 * u1, du2 * u2
            y0, y1 = dv0 * v0, dv1 * v1
            h1 = h1 - ((x1 - at(x1, -1, 0)) + (y1 - y0))
            h0 = h0 - ((x0 - at(x0, -1, 0)) + (y0 - dv_ * v_))
            h2 = h2 - ((x2 - at(x2, -1, 0)) + (dv2 * v2 - y1))
            p0, p1, p2 = u0 + at(u0, -1, 0), u1 + at(u1, -1, 0), u2 + at(u2, -1, 0)
            q0, q1 = v0 + v_, v1 + v0
            u0 = (u0 + fu0) + (cu0 * (q0 + at(q0, 1, 0)) - gu0 * (at(h0, 1, 0) - h0))
            u1 = (u1 + fu1) + (cu1 * (q1 + at(q1, 1, 0)) - gu1 * (at(h1, 1, 0) - h1))
            v0 = (v0 + fv0) + (cv0 * (p0 + p1) - gv0 * (h1 - h0))
            v1 = (v1 + fv1) + (cv1 * (p1 + p2) - gv1 * (h2 - h1))
            sums = [a + b[centre : centre + 8] for a, b in zip(sums, (u0, u1, v0, v1))]
            return (h0, h1, h2, u0, u1, v0, v1, *sums)

        carry = (*state, *total)
        for step in range(steps):
            carry = advance(step, carry)
            if low:
                next(beside, None)
        state, total = carry[:7], carry[7:]
    for _ in beside:
        pass
    height = [x[8:16] for x in state[:2]]
    average = [x * (1.0 / SUBSTEPS) for x in total]
    transport = [
        (-thickness * count_u[i][HALO : HALO + 8]) * average[i] for i in range(2)
    ]
    before = (ids(square, 0) < ids(square, 1)).astype(f32)
    south = jnp.dot(
        transport[0] + transport[1],
        before,
        precision=lax.Precision.HIGHEST,
        preferred_element_type=f32,
    )
    stream = [south + transport[0], south + (transport[0] + transport[1])]
    results = [*height, *stream, *average]
    moved = [at(values, -8 * n, 1) for n, values in enumerate(results)]
    for e in range(MEMBERS):
        packed = moved[0]
        for n in range(1, 8):
            packed = jnp.where(block == (e + n) % 16, moved[n], packed)
        out_ref[e, 0:8] = packed
        out_ref[e, 8:16] = in_ref[(e + 15) % MEMBERS, MAIL_N:MAIL_S]
        out_ref[e, 16:24] = in_ref[(e + 1) % MEMBERS, MAIL_S:CHUNK]


def gain(values, axis, flow, diffusion):
    ahead = at(values, 1, axis)
    sides = at(values, -1, axis) + at(values, 2, axis)
    far = at(values, -2, axis) + at(values, 3, axis)
    face = (37.0 * (values + ahead) - 8.0 * sides + far) * (1.0 / 60.0)
    flux = diffusion * (ahead - values) - flow * face
    return flux - at(flux, -1, axis)


def inner_kernel(own_ref, out_ref):
    bottom = own_ref[OWN_BOTTOM]
    c = tracer_planes(own_ref)
    count = jnp.minimum(bottom, at(bottom, 1, 1))
    values = jnp.concatenate([plane for tracer in c for plane in tracer], axis=0)
    flow, diffusion = [], []
    for k in range(LEVELS):
        flow.append(jnp.where(count > k, own_ref[OWN_EAST + k], 0.0))
        diffusion.append(jnp.where(count > k, tracer_diffusion, 0.0))
    flow, diffusion = (jnp.concatenate(x * TRACERS, axis=0) for x in (flow, diffusion))
    lane = ids(values.shape, 1)

    def moved(step):
        inside = lane < COLS - step if step > 0 else lane >= -step
        return jnp.where(inside, at(values, step, 1), 0.0)

    ahead = moved(1)
    face = (37.0 * (values + ahead) - 8.0 * (moved(-1) + moved(2)) + (moved(-2) + moved(3))) * (
        1.0 / 60.0
    )
    flux = jnp.where(lane < COLS - 1, diffusion * (ahead - values) - flow * face, 0.0)
    out_ref[...] = flux - at(flux, -1, 1)


def outer(west, east, left, right, flow_w, flow_l, flow_r, diff_w, diff_r):
    q = ids((ROWS, COLS), 1) % 4
    sixtieth = 1.0 / 60.0
    w1, w2, w3 = at(west, 3, 1), at(west, 2, 1), at(west, 1, 1)
    face = 37.0 * (w1 + left) - 8.0 * (w2 + at(left, 1, 1)) + (w3 + at(left, 2, 1))
    through = at(diff_w, 3, 1) * (left - w1) - at(flow_w, 3, 1) * (face * sixtieth)
    flux = jnp.where(q == 0, w2 - 8.0 * w1, jnp.where(q == 1, w2, 0.0)) * (-sixtieth) * flow_l
    low = flux - at(flux, -1, 1) - jnp.where(q == 0, through, 0.0)
    e1, e2, e3 = at(east, -3, 1), at(east, -2, 1), at(east, -1, 1)
    face = 37.0 * (right + e1) - 8.0 * (at(right, -1, 1) + e2) + (at(right, -2, 1) + e3)
    through = diff_r * (e1 - right) - flow_r * (face * sixtieth)
    flux = jnp.where(q == 2, e3 - 8.0 * e2, jnp.where(q == 1, e3, 0.0)) * (-sixtieth) * flow_r
    high = flux - at(flux, -1, 1) + jnp.where(q == 3, through, 0.0)
    return low, high


def finish_kernel(
    place_ref, in_ref, own_ref, west_ref, east_ref, along_ref,
    tracers_out, velocity_out, height_out, stream_out, turned_ref, rows_ref,
):
    place = place_ref[0]
    turned_ref[...] = in_ref[:, 0:8].reshape(COLS, COLS).T

    for q in range(8):
        spot = pl.multiple_of(lax.rem(q + place, 16) * 8, 8)
        rows_ref[pl.ds(ROWS * (q // 2) + q % 2, 8, 2), :] = turned_ref[pl.ds(spot, 8)]
    height_out[...] = rows_ref[:ROWS]
    stream_out[...] = rows_ref[ROWS : 2 * ROWS]
    average_u, average_v = rows_ref[2 * ROWS : 3 * ROWS], rows_ref[3 * ROWS :]

    sub = ids((8, COLS), 0)
    tall = (ROWS + 8, 2 * COLS)
    row = ids(tall, 0)
    first, last = place == 0, place == MEMBERS - 1

    def lat_tile(n):
        south = jnp.where(first, 0.0, in_ref[n // 2, 8:16])
        north = jnp.where(last, 0.0, in_ref[n // 2, 16:24])
        if n % 2 == 0:
            return jnp.where(sub < 4, north, south)
        return at(jnp.where(sub < 4, south, north), 4, 0)

    def spare_north(tile):
        return jnp.where(sub == 0, at(tile, 3, 0), 0.0)

    def spare_south(tile):
        return jnp.where(sub == 7, at(tile, -3, 0), 0.0)

    def tallen(own, tile):
        return jnp.concatenate([own, tile], axis=0)

    def whole(own, plane):
        return wide(own, beside_plane(west_ref, east_ref, plane))

    tiles = [[lat_tile(LEVELS * t + k) for k in range(LEVELS)] for t in range(TRACERS)]
    bottom_own = own_ref[OWN_BOTTOM]
    c = tracer_planes(own_ref)
    p_own = pressures(c[1], c[0])
    p_tile = pressures(tiles[1], tiles[0])
    both = wide(
        spare_north(tiles[3][0]) + spare_south(tiles[3][0]),
        spare_north(tiles[3][1]) + spare_south(tiles[3][1]),
    )
    bottom = tallen(whole(bottom_own, BOTTOM), both)
    count_u = jnp.minimum(bottom, at(bottom, 1, 1))
    count_v = jnp.minimum(bottom, at(bottom, 1, 0))
    f_u = coriolis(place * ROWS + row, 0.5)
    f_v = coriolis(place * ROWS + row, 1.0)
    none = jnp.zeros((8, COLS), f32)
    wind = [tallen(wide(own_ref[OWN_WIND + d], jnp.zeros((ROWS, COLS), f32)), jnp.zeros((8, 2 * COLS), f32)) for d in range(2)]

    def up(x):
        return at(x, 1, 0)

    def down(x):
        return at(x, -1, 0)

    stars_u, stars_v, gains = [], [], [None] * (TRACERS * LEVELS)
    own_u, own_v = count_u[:ROWS, :COLS], count_v[:ROWS, :COLS]
    mean_u = mean_v = jnp.zeros((ROWS, COLS), f32)
    for k in range(LEVELS):
        east, north = count_u > k, count_v > k
        t0, t1, t2 = tiles[0][k], tiles[1][k], tiles[2][k]
        u_lat = wide(spare_north(t0) + spare_south(t0), spare_north(t2))
        v_lat = wide(spare_north(t1) + spare_south(t1), spare_south(t2))
        u = tallen(whole(own_ref[OWN_EAST + k], EAST + k), u_lat)
        u = jnp.where(east | (row >= ROWS), u, 0.0)
        v = tallen(whole(own_ref[OWN_NORTH + k], NORTH + k), v_lat)
        v = jnp.where(north | (row == ROWS), v, 0.0)
        p = tallen(whole(p_own[k], PRESSURE + k), wide(p_tile[k], none))
        tend_u, tend_v = momentum(k, u, v, p, wind, east, north, f_u, f_v, up, down)
        star_u = (u + time_step * tend_u)[:ROWS, :COLS]
        star_v = (v + time_step * tend_v)[:ROWS, :COLS]
        stars_u.append(star_u)
        stars_v.append(star_v)
        mean_u = mean_u + star_u
        mean_v = mean_v + star_v

        diffusion = jnp.where(north[:, :COLS], tracer_diffusion, 0.0)
        for t in range(TRACERS):
            cn = tallen(c[t][k], tiles[t][k])
            gains[LEVELS * t + k] = gain(cn, 0, v[:, :COLS], diffusion)[:ROWS]
    for n in range(TRACERS * LEVELS):
        t, k = divmod(n, LEVELS)
        change = along_ref[ROWS * n : ROWS * (n + 1)] + gains[n]
        tracers_out[t, k] = jnp.where(bottom_own > k, c[t][k] + time_step * change, 0.0)
    shift_u = average_u - mean_u / jnp.maximum(own_u, 1.0)
    shift_v = average_v - mean_v / jnp.maximum(own_v, 1.0)
    for k in range(LEVELS):
        velocity_out[0, k] = jnp.where(own_u > k, stars_u[k] + shift_u, 0.0)
        velocity_out[1, k] = jnp.where(own_v > k, stars_v[k] + shift_v, 0.0)


def ring(axis, step):
    count = lax.axis_size(axis)
    return [(i, (i + step) % count) for i in range(count)]


def struct(*shape):
    return jax.ShapeDtypeStruct(shape, f32)


def vmem(*shape):
    return pltpu.VMEM(shape, f32)


def specs(count, scalars=0):
    return [pl.BlockSpec(memory_space=pltpu.SMEM)] * scalars + [
        pl.BlockSpec(memory_space=pltpu.VMEM)
    ] * count


PARAMS = pltpu.CompilerParams(vmem_limit_bytes=32 * 1024 * 1024)


def stacked(tracers, velocity, surface, wind, bottom):
    def put(values, first):
        values = values.reshape(-1, ROWS, COLS)
        after = OWN - first - values.shape[0]
        return lax.pad(
            values, jnp.zeros((), values.dtype), ((first, after, 0), (0, 0, 0), (0, 0, 0))
        )

    return (
        put(tracers, 0)
        + put(velocity, OWN_EAST)
        + put(surface, OWN_SURFACE)
        + put(wind, OWN_WIND)
        + put(bottom, OWN_BOTTOM).astype(f32)
    )


def shards(tracers, velocity, surface, wind, bottom):
    place = lax.axis_index("lat").astype(jnp.int32).reshape(1)
    own = stacked(tracers, velocity, surface, wind, bottom)
    payload = struct(PLANES // 4 + 1, ROWS, COLS)
    to_right, to_left = pl.pallas_call(
        pack_kernel,
        out_shape=(payload, payload),
        in_specs=specs(1),
        out_specs=tuple(specs(2)),
        compiler_params=PARAMS,
        name="pack",
    )(own)
    west = lax.ppermute(to_right, "lon", ring("lon", 1))
    east = lax.ppermute(to_left, "lon", ring("lon", -1))
    inner = pl.pallas_call(
        inner_kernel,
        out_shape=struct(TRACERS * LEVELS * ROWS, COLS),
        in_specs=specs(1),
        out_specs=specs(1)[0],
        compiler_params=PARAMS,
        cost_estimate=pl.CostEstimate(flops=1500000, bytes_accessed=3000000, transcendentals=0),
        name="inner",
    )(own)
    chunks, flows = pl.pallas_call(
        send_kernel,
        out_shape=(
            struct(MEMBERS, CHUNK, COLS),
            struct((LEVELS + 1) * ROWS, 2 * COLS),
        ),
        in_specs=specs(3, 1) + [pl.BlockSpec(memory_space=pl.ANY)],
        out_specs=tuple(specs(2)),
        scratch_shapes=[
            vmem(12 * ROWS, COLS),
            vmem(2, COLS, COLS),
            vmem(40, 2 * COLS),
            vmem(COLS + 2 * HALO, COLS),
        ],
        compiler_params=PARAMS,
        name="columns",
    )(place, own, west, east, inner)
    slabs = lax.all_to_all(chunks, "lat", 0, 0, tiled=True)
    answers, along = pl.pallas_call(
        slab_kernel,
        out_shape=(
            struct(MEMBERS, BACK, COLS),
            struct(TRACERS * LEVELS * ROWS, COLS),
        ),
        in_specs=specs(7),
        out_specs=tuple(specs(2)),
        scratch_shapes=[vmem(COLS, COLS)],
        compiler_params=PARAMS,
        name="substeps",
    )(slabs, flows, west, east, to_right, to_left, inner)
    home = lax.all_to_all(answers, "lat", 0, 0, tiled=True)
    return pl.pallas_call(
        finish_kernel,
        out_shape=(
            struct(TRACERS, LEVELS, ROWS, COLS),
            struct(2, LEVELS, ROWS, COLS),
            struct(ROWS, COLS),
            struct(ROWS, COLS),
        ),
        in_specs=specs(5, 1),
        out_specs=tuple(specs(4)),
        scratch_shapes=[vmem(COLS, COLS), vmem(4 * ROWS, COLS)],
        compiler_params=PARAMS,
        name="finish",
    )(place, home, own, west, east, along)


def solution(mesh):
    placed = (
        P(None, None, "lat", "lon"),
        P(None, None, "lat", "lon"),
        P("lat", "lon"),
        P(None, "lat", "lon"),
        P("lat", "lon"),
    )
    return jax.shard_map(
        shards,
        mesh=mesh,
        in_specs=placed,
        out_specs=(
            P(None, None, "lat", "lon"),
            P(None, None, "lat", "lon"),
            P("lat", "lon"),
            P("lat", "lon"),
        ),
        check_vma=False,
    )
```

```python
import jax
import jax.numpy as jnp
from jax import lax
from jax.experimental import pallas as pl
from jax.experimental.pallas import tpu as pltpu
from jax.sharding import PartitionSpec as P

TRACERS = 4
LEVELS = 8
SUBSTEPS = 30
ROWS = 16
COLS = 128
MEMBERS = 16
HALO = 32
SLAB = 72
NLAT = ROWS * MEMBERS

time_step = 0.2
tracer_diffusion = 0.2
viscosity = 0.2
thermal_expansion = 2.0
haline_contraction = 1.5
coriolis_base = 1.0
gravity = 140.0
surface_scale = 40.0
thickness = 1.0 / LEVELS
f32 = jnp.float32

PRESSURE, EAST, NORTH, WIND, SURFACE, BOTTOM = 0, 8, 16, 24, 26, 27
PLANES = 28
OWN_EAST, OWN_NORTH, OWN_SURFACE, OWN_WIND, OWN_BOTTOM, OWN = 32, 40, 48, 49, 51, 52
MAIL_N, MAIL_S, CHUNK = SLAB, SLAB + 8, SLAB + 16
BACK = 24


def at(values, step, axis):
    size = values.shape[axis]
    step %= size
    return values if step == 0 else pltpu.roll(values, size - step, axis)


def ids(shape, axis):
    return lax.broadcasted_iota(jnp.int32, shape, axis)


def wide(own, beside):
    return jnp.concatenate([own, beside], axis=1)


def tracer_planes(own_ref):
    bottom = own_ref[OWN_BOTTOM]
    return [
        [jnp.where(bottom > k, own_ref[LEVELS * t + k], 0.0) for k in range(LEVELS)]
        for t in range(TRACERS)
    ]


def pressures(salt, heat):
    total, out = None, []
    for k in range(LEVELS):
        density = haline_contraction * salt[k] - thermal_expansion * heat[k]
        total = density if total is None else total + density
        out.append(thickness * total)
    return out


def pack_kernel(own_ref, right_ref, left_ref):
    c = tracer_planes(own_ref)
    planes = pressures(c[1], c[0])
    planes += [own_ref[n] for n in range(OWN_EAST, OWN_SURFACE)]
    planes += [own_ref[n] for n in (OWN_WIND, OWN_WIND + 1, OWN_SURFACE, OWN_BOTTOM)]
    lane = ids((ROWS, COLS), 1)
    for q in range(PLANES // 4):
        right = left = jnp.zeros((ROWS, COLS), f32)
        for s in range(4):
            moved = at(planes[4 * q + s], -32 * s, 1)
            right = jnp.where(lane // 32 == (s + 3) % 4, moved, right)
            left = jnp.where(lane // 32 == s, moved, left)
        right_ref[q] = right
        left_ref[q] = left
    right = left = jnp.zeros((ROWS, COLS), f32)
    for n in range(TRACERS * LEVELS):
        moved = at(c[n // LEVELS][n % LEVELS], -4 * n, 1)
        right = jnp.where(lane // 4 == (n + 31) % 32, moved, right)
        left = jnp.where(lane // 4 == n, moved, left)
    right_ref[PLANES // 4] = right
    left_ref[PLANES // 4] = left


def beside_plane(west_ref, east_ref, plane):
    q, s = divmod(plane, 4)
    block = ids((ROWS, COLS), 1) // 32
    both = jnp.where(
        block == s, east_ref[q], jnp.where(block == (s + 3) % 4, west_ref[q], 0.0)
    )
    return at(both, 32 * s, 1)


def momentum(k, u, v, p, wind, east, north, f_u, f_v, up, down):
    pair_v = v + down(v)
    pair_u = u + at(u, -1, 1)
    tend_u = (
        (0.25 * f_u) * (pair_v + at(pair_v, 1, 1))
        - (at(p, 1, 1) - p)
        + viscosity * (at(u, 1, 1) + at(u, -1, 1) + up(u) + down(u) - 4.0 * u)
    )
    tend_v = (
        (-0.25 * f_v) * (pair_u + up(pair_u))
        - (up(p) - p)
        + viscosity * (at(v, 1, 1) + at(v, -1, 1) + up(v) + down(v) - 4.0 * v)
    )
    if k == 0:
        tend_u = tend_u + wind[0]
        tend_v = tend_v + wind[1]
    return jnp.where(east, tend_u, 0.0), jnp.where(north, tend_v, 0.0)


def coriolis(rows, offset):
    return coriolis_base * (0.5 + (rows.astype(f32) + offset) / NLAT)


def send_kernel(
    place_ref, own_ref, west_ref, east_ref, _,
    out_ref, flows_ref, split_ref, stack_ref, edge_ref, turned_ref,
):
    place = place_ref[0]
    c = tracer_planes(own_ref)
    p_own = pressures(c[1], c[0])

    def whole(own, plane):
        return wide(own, beside_plane(west_ref, east_ref, plane))

    shape = (ROWS, 2 * COLS)
    row = ids(shape, 0)
    bottom = whole(own_ref[OWN_BOTTOM], BOTTOM)
    wind = [whole(own_ref[OWN_WIND + d], WIND + d) for d in range(2)]

    def up(x):
        return jnp.where(row == ROWS - 1, 0.0, at(x, 1, 0))

    def down(x):
        return jnp.where(row == 0, 0.0, at(x, -1, 0))

    count_u = jnp.minimum(bottom, at(bottom, 1, 1))
    count_v = jnp.minimum(bottom, up(bottom))
    f_u = coriolis(place * ROWS + row, 0.5)
    f_v = coriolis(place * ROWS + row, 1.0)
    sums = [jnp.zeros(shape, f32) for _ in range(4)]
    us, vs, raws = [], [], []
    for k in range(LEVELS):
        east, north = count_u > k, count_v > k
        u = jnp.where(east, whole(own_ref[OWN_EAST + k], EAST + k), 0.0)
        raw = jnp.where(bottom > k, whole(own_ref[OWN_NORTH + k], NORTH + k), 0.0)
        v = jnp.where(north, raw, 0.0)
        p = whole(p_own[k], PRESSURE + k)
        tend_u, tend_v = momentum(k, u, v, p, wind, east, north, f_u, f_v, up, down)
        sums = [a + b for a, b in zip(sums, (u, v, tend_u, tend_v))]
        us.append(u)
        vs.append(v)
        raws.append(raw)
        pair = u + at(u, -1, 1)
        last = p[8:] + (-0.25 * f_v[8:]) * pair[8:] + viscosity * at(v, -1, 0)[8:]
        if k == 0:
            last = last + wind[1][8:]
        first = (-0.25 * (f_v[:8] - 1.0 / NLAT)) * pair[:8] - p[:8] + viscosity * v[:8]
        edge_ref[k : k + 1] = u[15:16]
        edge_ref[8 + k : 9 + k] = raw[15:16]
        edge_ref[16 + k : 17 + k] = last[7:8]
        edge_ref[24 + k : 25 + k] = u[0:1]
        edge_ref[32 + k : 33 + k] = first[0:1]
    surface = whole(own_ref[OWN_SURFACE], SURFACE)
    for n, values in enumerate((surface, *sums, bottom)):
        split_ref[ROWS * n : ROWS * (n + 1)] = values[:, :COLS]
        split_ref[ROWS * (6 + n) : ROWS * (7 + n)] = values[:, COLS:]
    for q in range(16):
        spot = pl.multiple_of(lax.rem(q + place, 16) * 8, 8)
        for half in range(2):
            if q < 12:
                rows = split_ref[pl.ds(ROWS * (6 * half + q // 2) + q % 2, 8, 2), :]
            else:
                rows = edge_ref[8 * (q - 12) : 8 * (q - 11), COLS * half : COLS * (half + 1)]
            stack_ref[half, pl.ds(spot, 8)] = rows
    turned_ref[HALO : HALO + COLS] = stack_ref[0].T
    beyond = stack_ref[1].T
    turned_ref[:HALO] = beyond[COLS - HALO :]
    turned_ref[HALO + COLS :] = beyond[:HALO]
    edge = edge_ref[32:40]
    sub = ids((8, COLS), 0)
    tile_lane = ids((8, COLS), 1)
    spare_block = tile_lane // 8 == lax.rem(6 + place, 16)
    moved = [at(edge, 8 * d - HALO + 4, 1)[:, :COLS] for d in range(MEMBERS)]
    halves = [at(x, 64, 1) for x in moved]
    rests = [jnp.where(tile_lane % 8 == sub, x[:, 64:65], 0.0) for x in moved]
    for step in (1, 2, 4):
        rests = [x + at(x, step, 0) for x in rests]
    for d in range(MEMBERS):
        pairs = jnp.where(tile_lane < 64, moved[d], at(halves[d], 1, 0))
        rest = rests[d]
        out_ref[d, :8] = jnp.where(
            sub == 0, pairs, jnp.where(sub == 1, at(pairs, 1, 0), turned_ref[8 * d : 8 * d + 8])
        )
        out_ref[d, 8 : SLAB - 8] = turned_ref[8 * d + 8 : 8 * d + SLAB - 8]
        end = turned_ref[8 * d + SLAB - 8 : 8 * d + SLAB]
        end = jnp.where((sub == 5) & spare_block, rest, end)
        end = jnp.where(sub == 6, at(pairs, -2, 0), end)
        out_ref[d, SLAB - 8 : SLAB] = jnp.where(sub == 7, at(pairs, -1, 0), end)

    for n, values in enumerate((*us, count_u)):
        flows_ref[ROWS * n : ROWS * (n + 1)] = values


    def spare(n):
        t, k = divmod(n, LEVELS)
        if t == 0:
            return us[k][:, :COLS], us[k][:, :COLS]
        if t == 1:
            return raws[k][:, :COLS], vs[k][:, :COLS]
        if t == 2:
            return raws[k][:, COLS:], us[k][:, COLS:]
        if k < 2:
            own = bottom[:, COLS * k : COLS * (k + 1)]
            return own, own
        return None

    def tops(n):
        own = c[n // LEVELS][n % LEVELS][8:]
        more = spare(n)
        return own if more is None else jnp.where(sub == 4, at(more[0][8:], 3, 0), own)

    def bottoms(n):
        own = c[n // LEVELS][n % LEVELS][:8]
        more = spare(n)
        return own if more is None else jnp.where(sub == 3, at(more[1][:8], -3, 0), own)

    for m in range(MEMBERS):
        out_ref[m, MAIL_N:MAIL_S] = jnp.where(sub >= 4, tops(2 * m), at(tops(2 * m + 1), 4, 0))
        out_ref[m, MAIL_S:CHUNK] = jnp.where(sub < 4, bottoms(2 * m), at(bottoms(2 * m + 1), 4, 0))


def edge_steps(flows_ref, west_ref, east_ref, right_ref, left_ref, inner_ref, along_ref):
    block = ids((ROWS, COLS), 1) // 4
    count = flows_ref[ROWS * LEVELS :]

    def packed(of_level, half, ahead):
        tile = jnp.zeros((ROWS, COLS), f32)
        for k in range(LEVELS):
            values = of_level(k)[:, COLS * half : COLS * (half + 1)]
            tile = jnp.where(block % LEVELS == k, at(values, -4 * (k + ahead), 1), tile)
        return tile

    def repeated(tile):
        for step in (32, 64):
            tile = jnp.where(block * 4 % (2 * step) < step, tile, at(tile, -step, 1))
        return tile

    def flow(k):
        return flows_ref[ROWS * k : ROWS * (k + 1)]

    def diffusion(k):
        return jnp.where(count > k, tracer_diffusion, 0.0)

    tiles = []
    for what in ((flow, 1, 1), (flow, 0, 0), (flow, 0, 1), (diffusion, 1, 1), (diffusion, 0, 1)):
        tiles.append(packed(*what))
        yield
    tiles = [repeated(tile) for tile in tiles]
    yield
    last = PLANES // 4
    low, high = outer(
        at(west_ref[last], -4, 1), east_ref[last], left_ref[last], at(right_ref[last], -4, 1),
        *tiles,
    )
    high = at(high, 4, 1)
    yield
    waiting = []
    for n in range(TRACERS * LEVELS):
        both = jnp.where(block == n, low, jnp.where(block == (n + 31) % 32, high, 0.0))
        waiting.append((slice(ROWS * n, ROWS * (n + 1)), at(both, 4 * n, 1)))
        if n % 2:
            yield
    for rows, side in waiting:
        along_ref[rows] = inner_ref[rows] + side


def slab_kernel(
    in_ref, flows_ref, west_ref, east_ref, right_ref, left_ref, inner_ref,
    out_ref, along_ref, edge_ref,
):
    shape = (SLAB, COLS)
    lane = ids(shape, 1)
    r = lane % 8
    block = ids((8, COLS), 1) // 8

    tiles = []
    for t in range(SLAB // 8):
        now = [in_ref[a, 8 * t : 8 * t + 8] for a in range(MEMBERS)]
        for bit in (1, 2, 4, 8):
            odd = (block & bit) > 0
            now = [jnp.where(odd, now[(a + bit) % MEMBERS], now[a]) for a in range(MEMBERS)]
        tiles.append([at(now[-q % MEMBERS], 8 * q, 1) for q in range(16)])
    blocks = [jnp.concatenate([tile[q] for tile in tiles], axis=0) for q in range(16)]
    surface, start_u, start_v, force_u, force_v, bottom = (blocks[2 * n : 2 * n + 2] for n in range(6))
    u_a, v_raw, near, u_next = blocks[12:]
    zeros = jnp.zeros((8, COLS), f32)
    sub = ids((8, COLS), 0)
    edge_ref[COLS - 8 :] = zeros
    for a in range(1, MEMBERS):
        begin, end = in_ref[a, :8], in_ref[a, SLAB - 8 : SLAB]
        rows = jnp.where(sub < 2, begin, at(begin, -1, 0))
        rows = jnp.where(sub < 4, rows, jnp.where(sub < 6, at(end, 2, 0), at(end, 1, 0)))
        edge_ref[8 * a - 8 : 8 * a] = jnp.where(sub % 2 == 0, rows, at(at(rows, 64, 1), -1, 0))
    column = ids(shape, 0)
    far = at(edge_ref[...].T[:SLAB], -4, 0)
    far = jnp.where(column == 68, at(at(force_u[0], 1, 0), 8, 1), far)
    unused = (column < 2) | (column >= SLAB - 2)
    bottom = [jnp.where(unused, float(LEVELS), b) for b in bottom]

    top = lane == COLS - 1
    count_u = [jnp.minimum(b, at(b, 1, 0)) for b in bottom]
    count_v = [
        jnp.minimum(*bottom),
        jnp.where(top, 0.0, jnp.minimum(bottom[1], at(bottom[0], 1, 1))),
    ]

    square = (COLS, COLS)

    def spread_from(lane_at, values):
        chosen = ids(square, 0) == ids(square, 1) // 8 * 8 + lane_at
        spread = jnp.dot(
            jnp.concatenate(values, axis=0).astype(jnp.bfloat16),
            chosen.astype(f32).astype(jnp.bfloat16),
            preferred_element_type=f32,
        )
        return [spread[SLAB * n : SLAB * (n + 1)] for n in range(len(values))]

    count_ua, count_va, count_vc = spread_from(7, [count_u[1], count_v[1], count_v[0]])
    count_ub, count_vb = spread_from(8, [count_u[0], count_v[0]])
    level = r.astype(f32)
    last = lane >= COLS - 8
    v_a = jnp.where(count_va > level, v_raw, 0.0)
    u_a = jnp.where(last, 0.0, u_a)
    u_b = jnp.where(last, 0.0, at(u_next, 8, 1))
    f_a = 0.25 * coriolis(lane // 8 * ROWS + 15, 0.5)
    f_b = f_a + 0.25 * coriolis_base / NLAT
    pair = v_a + at(v_a, 1, 0)
    spread = viscosity * (at(v_a, 1, 0) + at(v_a, -1, 0) - 4.0 * v_a)
    terms = jnp.concatenate(
        [
            jnp.where(count_ua > level, f_a * pair + viscosity * u_b, 0.0),
            jnp.where(count_ub > level, f_b * pair + viscosity * u_a, 0.0),
            jnp.where(count_vb > level, viscosity * v_a, 0.0),
            jnp.where(count_vc > level, viscosity * v_a, 0.0),
            jnp.where(count_va > level, near + far + spread, 0.0),
            v_a,
        ],
        axis=0,
    )
    for step in (1, 2, 4):
        terms = terms + at(terms, -step, 1)
    shifted = at(terms[SLAB : 3 * SLAB], -1, 1)
    u_15, v_14, v_15, begin_15 = (
        jnp.where(r == 7, terms[SLAB * n : SLAB * (n + 1)], 0.0) for n in (0, 3, 4, 5)
    )
    u_16, v_16 = (jnp.where(r == 0, shifted[SLAB * n : SLAB * (n + 1)], 0.0) for n in range(2))
    force_u = [force_u[0] + u_16, force_u[1] + u_15]
    force_v = [force_v[0] + (v_14 + v_16), force_v[1] + v_15]
    start_v = [start_v[0], start_v[1] + begin_15]

    sub_step = time_step / SUBSTEPS
    held_u, held_v, flux_u, flux_v, begin_u, begin_v = [], [], [], [], [], []
    for i in range(2):
        per = 1.0 / jnp.maximum(count_u[i], 1.0)
        open_face = jnp.where(count_u[i] > 0.0, sub_step, 0.0)
        flux_u.append((sub_step * surface_scale * thickness) * count_u[i])
        held_u.append(
            (
                (0.25 * open_face) * coriolis(2 * lane + i, 0.5),
                gravity * open_face,
                open_face * (force_u[i] * per),
            )
        )
        begin_u.append(start_u[i] * per)
        per = 1.0 / jnp.maximum(count_v[i], 1.0)
        open_face = jnp.where(count_v[i] > 0.0, sub_step, 0.0)
        flux_v.append((sub_step * surface_scale * thickness) * count_v[i])
        held_v.append(
            (
                (-0.25 * open_face) * coriolis(2 * lane + i, 1.0),
                gravity * open_face,
                open_face * (force_v[i] * per),
            )
        )
        begin_v.append(start_v[i] * per)
    held = (
        *flux_u, at(flux_u[0], 1, 1), *flux_v, at(flux_v[0], 1, 1), at(flux_v[1], -1, 1),
        *held_u[0], *held_u[1], *held_v[0], *held_v[1],
    )
    state = (*surface, at(surface[0], 1, 1), *begin_u, *begin_v)
    total = (zeros,) * 4
    beside = edge_steps(flows_ref, west_ref, east_ref, right_ref, left_ref, inner_ref, along_ref)
    for low, steps in ((0, 6), (8, 8), (16, 8), (24, 8)):
        cut = 8 if low else 0
        state = tuple(x[cut : x.shape[0] - cut] for x in state)
        (
            du0, du1, du2, dv0, dv1, dv2, dv_, cu0, gu0, fu0, cu1, gu1, fu1,
            cv0, gv0, fv0, cv1, gv1, fv1,
        ) = (x[low : SLAB - low] for x in held)
        centre = HALO - low

        def advance(_, carry):
            h0, h1, h2, u0, u1, v0, v1, *sums = carry
            v_ = at(v1, -1, 1)
            u2 = at(u0, 1, 1)
            v2 = at(v0, 1, 1)
            x0, x1, x2 = du0 * u0, du1 * u1, du2 * u2
            y0, y1 = dv0 * v0, dv1 * v1
            h1 = h1 - ((x1 - at(x1, -1, 0)) + (y1 - y0))
            h0 = h0 - ((x0 - at(x0, -1, 0)) + (y0 - dv_ * v_))
            h2 = h2 - ((x2 - at(x2, -1, 0)) + (dv2 * v2 - y1))
            p0, p1, p2 = u0 + at(u0, -1, 0), u1 + at(u1, -1, 0), u2 + at(u2, -1, 0)
            q0, q1 = v0 + v_, v1 + v0
            u0 = (u0 + fu0) + (cu0 * (q0 + at(q0, 1, 0)) - gu0 * (at(h0, 1, 0) - h0))
            u1 = (u1 + fu1) + (cu1 * (q1 + at(q1, 1, 0)) - gu1 * (at(h1, 1, 0) - h1))
            v0 = (v0 + fv0) + (cv0 * (p0 + p1) - gv0 * (h1 - h0))
            v1 = (v1 + fv1) + (cv1 * (p1 + p2) - gv1 * (h2 - h1))
            sums = [a + b[centre : centre + 8] for a, b in zip(sums, (u0, u1, v0, v1))]
            return (h0, h1, h2, u0, u1, v0, v1, *sums)

        carry = (*state, *total)
        for step in range(steps):
            carry = advance(step, carry)
            if low:
                next(beside, None)
        state, total = carry[:7], carry[7:]
    for _ in beside:
        pass
    height = [x[8:16] for x in state[:2]]
    average = [x * (1.0 / SUBSTEPS) for x in total]
    transport = [
        (-thickness * count_u[i][HALO : HALO + 8]) * average[i] for i in range(2)
    ]
    before = jnp.concatenate(
        [
            (ids(square, 0) < (ids(square, 1) - 8 * n) % COLS).astype(f32).astype(jnp.bfloat16)
            for n in (2, 3)
        ],
        axis=1,
    )
    rest = jnp.concatenate([transport[0] + transport[1], zeros], axis=0)
    parts = []
    for _ in range(3):
        parts.append(rest.astype(jnp.bfloat16).astype(f32))
        rest = rest - parts[-1]
    sums = jnp.dot(
        jnp.concatenate(parts, axis=0).astype(jnp.bfloat16),
        before,
        preferred_element_type=f32,
    )
    south = (sums[32:40] + sums[16:24]) + sums[:8]
    stream = [transport[0], transport[0] + transport[1]]
    results = [*height, *stream, *average]
    moved = [at(values, -8 * n, 1) for n, values in enumerate(results)]
    moved[2] = south[:, :COLS] + moved[2]
    moved[3] = south[:, COLS:] + moved[3]
    for e in range(MEMBERS):
        packed = moved[0]
        for n in range(1, 8):
            packed = jnp.where(block == (e + n) % 16, moved[n], packed)
        out_ref[e, 0:8] = packed
        out_ref[e, 8:16] = in_ref[(e + 15) % MEMBERS, MAIL_N:MAIL_S]
        out_ref[e, 16:24] = in_ref[(e + 1) % MEMBERS, MAIL_S:CHUNK]


def gain(values, axis, flow, diffusion):
    ahead = at(values, 1, axis)
    sides = at(values, -1, axis) + at(values, 2, axis)
    far = at(values, -2, axis) + at(values, 3, axis)
    face = (37.0 * (values + ahead) - 8.0 * sides + far) * (1.0 / 60.0)
    flux = diffusion * (ahead - values) - flow * face
    return flux - at(flux, -1, axis)


def inner_kernel(own_ref, out_ref):
    bottom = own_ref[OWN_BOTTOM]
    c = tracer_planes(own_ref)
    count = jnp.minimum(bottom, at(bottom, 1, 1))
    values = jnp.concatenate([plane for tracer in c for plane in tracer], axis=0)
    flow, diffusion = [], []
    for k in range(LEVELS):
        flow.append(jnp.where(count > k, own_ref[OWN_EAST + k], 0.0))
        diffusion.append(jnp.where(count > k, tracer_diffusion, 0.0))
    flow, diffusion = (jnp.concatenate(x * TRACERS, axis=0) for x in (flow, diffusion))
    lane = ids(values.shape, 1)

    def moved(step):
        inside = lane < COLS - step if step > 0 else lane >= -step
        return jnp.where(inside, at(values, step, 1), 0.0)

    ahead = moved(1)
    face = (37.0 * (values + ahead) - 8.0 * (moved(-1) + moved(2)) + (moved(-2) + moved(3))) * (
        1.0 / 60.0
    )
    flux = jnp.where(lane < COLS - 1, diffusion * (ahead - values) - flow * face, 0.0)
    out_ref[...] = flux - at(flux, -1, 1)


def outer(west, east, left, right, flow_w, flow_l, flow_r, diff_w, diff_r):
    q = ids((ROWS, COLS), 1) % 4
    sixtieth = 1.0 / 60.0
    w1, w2, w3 = at(west, 3, 1), at(west, 2, 1), at(west, 1, 1)
    face = 37.0 * (w1 + left) - 8.0 * (w2 + at(left, 1, 1)) + (w3 + at(left, 2, 1))
    through = at(diff_w, 3, 1) * (left - w1) - at(flow_w, 3, 1) * (face * sixtieth)
    flux = jnp.where(q == 0, w2 - 8.0 * w1, jnp.where(q == 1, w2, 0.0)) * (-sixtieth) * flow_l
    low = flux - at(flux, -1, 1) - jnp.where(q == 0, through, 0.0)
    e1, e2, e3 = at(east, -3, 1), at(east, -2, 1), at(east, -1, 1)
    face = 37.0 * (right + e1) - 8.0 * (at(right, -1, 1) + e2) + (at(right, -2, 1) + e3)
    through = diff_r * (e1 - right) - flow_r * (face * sixtieth)
    flux = jnp.where(q == 2, e3 - 8.0 * e2, jnp.where(q == 1, e3, 0.0)) * (-sixtieth) * flow_r
    high = flux - at(flux, -1, 1) + jnp.where(q == 3, through, 0.0)
    return low, high


def finish_kernel(
    place_ref, in_ref, own_ref, west_ref, east_ref, along_ref,
    tracers_out, velocity_out, height_out, stream_out, turned_ref, rows_ref,
):
    place = place_ref[0]
    turned_ref[...] = in_ref[:, 0:8].reshape(COLS, COLS).T

    for q in range(8):
        spot = pl.multiple_of(lax.rem(q + place, 16) * 8, 8)
        rows_ref[pl.ds(ROWS * (q // 2) + q % 2, 8, 2), :] = turned_ref[pl.ds(spot, 8)]
    height_out[...] = rows_ref[:ROWS]
    stream_out[...] = rows_ref[ROWS : 2 * ROWS]
    average_u, average_v = rows_ref[2 * ROWS : 3 * ROWS], rows_ref[3 * ROWS :]

    sub = ids((8, COLS), 0)
    tall = (ROWS + 8, 2 * COLS)
    row = ids(tall, 0)
    first, last = place == 0, place == MEMBERS - 1

    def lat_tile(n):
        south = jnp.where(first, 0.0, in_ref[n // 2, 8:16])
        north = jnp.where(last, 0.0, in_ref[n // 2, 16:24])
        if n % 2 == 0:
            return jnp.where(sub < 4, north, south)
        return at(jnp.where(sub < 4, south, north), 4, 0)

    def spare_north(tile):
        return jnp.where(sub == 0, at(tile, 3, 0), 0.0)

    def spare_south(tile):
        return jnp.where(sub == 7, at(tile, -3, 0), 0.0)

    def tallen(own, tile):
        return jnp.concatenate([own, tile], axis=0)

    def whole(own, plane):
        return wide(own, beside_plane(west_ref, east_ref, plane))

    tiles = [[lat_tile(LEVELS * t + k) for k in range(LEVELS)] for t in range(TRACERS)]
    bottom_own = own_ref[OWN_BOTTOM]
    c = tracer_planes(own_ref)
    p_own = pressures(c[1], c[0])
    p_tile = pressures(tiles[1], tiles[0])
    both = wide(
        spare_north(tiles[3][0]) + spare_south(tiles[3][0]),
        spare_north(tiles[3][1]) + spare_south(tiles[3][1]),
    )
    bottom = tallen(whole(bottom_own, BOTTOM), both)
    count_u = jnp.minimum(bottom, at(bottom, 1, 1))
    count_v = jnp.minimum(bottom, at(bottom, 1, 0))
    f_u = coriolis(place * ROWS + row, 0.5)
    f_v = coriolis(place * ROWS + row, 1.0)
    none = jnp.zeros((8, COLS), f32)
    wind = [tallen(wide(own_ref[OWN_WIND + d], jnp.zeros((ROWS, COLS), f32)), jnp.zeros((8, 2 * COLS), f32)) for d in range(2)]

    def up(x):
        return at(x, 1, 0)

    def down(x):
        return at(x, -1, 0)

    stars_u, stars_v, gains = [], [], [None] * (TRACERS * LEVELS)
    own_u, own_v = count_u[:ROWS, :COLS], count_v[:ROWS, :COLS]
    mean_u = mean_v = jnp.zeros((ROWS, COLS), f32)
    for k in range(LEVELS):
        east, north = count_u > k, count_v > k
        t0, t1, t2 = tiles[0][k], tiles[1][k], tiles[2][k]
        u_lat = wide(spare_north(t0) + spare_south(t0), spare_north(t2))
        v_lat = wide(spare_north(t1) + spare_south(t1), spare_south(t2))
        u = tallen(whole(own_ref[OWN_EAST + k], EAST + k), u_lat)
        u = jnp.where(east | (row >= ROWS), u, 0.0)
        v = tallen(whole(own_ref[OWN_NORTH + k], NORTH + k), v_lat)
        v = jnp.where(north | (row == ROWS), v, 0.0)
        p = tallen(whole(p_own[k], PRESSURE + k), wide(p_tile[k], none))
        tend_u, tend_v = momentum(k, u, v, p, wind, east, north, f_u, f_v, up, down)
        star_u = (u + time_step * tend_u)[:ROWS, :COLS]
        star_v = (v + time_step * tend_v)[:ROWS, :COLS]
        stars_u.append(star_u)
        stars_v.append(star_v)
        mean_u = mean_u + star_u
        mean_v = mean_v + star_v

        diffusion = jnp.where(north[:, :COLS], tracer_diffusion, 0.0)
        for t in range(TRACERS):
            cn = tallen(c[t][k], tiles[t][k])
            gains[LEVELS * t + k] = gain(cn, 0, v[:, :COLS], diffusion)[:ROWS]
    for n in range(TRACERS * LEVELS):
        t, k = divmod(n, LEVELS)
        change = along_ref[ROWS * n : ROWS * (n + 1)] + gains[n]
        tracers_out[t, k] = jnp.where(bottom_own > k, c[t][k] + time_step * change, 0.0)
    shift_u = average_u - mean_u / jnp.maximum(own_u, 1.0)
    shift_v = average_v - mean_v / jnp.maximum(own_v, 1.0)
    for k in range(LEVELS):
        velocity_out[0, k] = jnp.where(own_u > k, stars_u[k] + shift_u, 0.0)
        velocity_out[1, k] = jnp.where(own_v > k, stars_v[k] + shift_v, 0.0)


def ring(axis, step):
    count = lax.axis_size(axis)
    return [(i, (i + step) % count) for i in range(count)]


def struct(*shape):
    return jax.ShapeDtypeStruct(shape, f32)


def vmem(*shape):
    return pltpu.VMEM(shape, f32)


def specs(count, scalars=0):
    return [pl.BlockSpec(memory_space=pltpu.SMEM)] * scalars + [
        pl.BlockSpec(memory_space=pltpu.VMEM)
    ] * count


PARAMS = pltpu.CompilerParams(vmem_limit_bytes=32 * 1024 * 1024)


def stacked(tracers, velocity, surface, wind, bottom):
    def put(values, first):
        values = values.reshape(-1, ROWS, COLS)
        after = OWN - first - values.shape[0]
        return lax.pad(
            values, jnp.zeros((), values.dtype), ((first, after, 0), (0, 0, 0), (0, 0, 0))
        )

    return (
        put(tracers, 0)
        + put(velocity, OWN_EAST)
        + put(surface, OWN_SURFACE)
        + put(wind, OWN_WIND)
        + put(bottom, OWN_BOTTOM).astype(f32)
    )


def shards(tracers, velocity, surface, wind, bottom):
    place = lax.axis_index("lat").astype(jnp.int32).reshape(1)
    own = stacked(tracers, velocity, surface, wind, bottom)
    payload = struct(PLANES // 4 + 1, ROWS, COLS)
    to_right, to_left = pl.pallas_call(
        pack_kernel,
        out_shape=(payload, payload),
        in_specs=specs(1),
        out_specs=tuple(specs(2)),
        compiler_params=PARAMS,
        name="pack",
    )(own)
    west = lax.ppermute(to_right, "lon", ring("lon", 1))
    east = lax.ppermute(to_left, "lon", ring("lon", -1))
    inner = pl.pallas_call(
        inner_kernel,
        out_shape=struct(TRACERS * LEVELS * ROWS, COLS),
        in_specs=specs(1),
        out_specs=specs(1)[0],
        compiler_params=PARAMS,
        cost_estimate=pl.CostEstimate(flops=1500000, bytes_accessed=3000000, transcendentals=0),
        name="inner",
    )(own)
    chunks, flows = pl.pallas_call(
        send_kernel,
        out_shape=(
            struct(MEMBERS, CHUNK, COLS),
            struct((LEVELS + 1) * ROWS, 2 * COLS),
        ),
        in_specs=specs(3, 1) + [pl.BlockSpec(memory_space=pl.ANY)],
        out_specs=tuple(specs(2)),
        scratch_shapes=[
            vmem(12 * ROWS, COLS),
            vmem(2, COLS, COLS),
            vmem(40, 2 * COLS),
            vmem(COLS + 2 * HALO, COLS),
        ],
        compiler_params=PARAMS,
        name="columns",
    )(place, own, west, east, inner)
    slabs = lax.all_to_all(chunks, "lat", 0, 0, tiled=True)
    answers, along = pl.pallas_call(
        slab_kernel,
        out_shape=(
            struct(MEMBERS, BACK, COLS),
            struct(TRACERS * LEVELS * ROWS, COLS),
        ),
        in_specs=specs(7),
        out_specs=tuple(specs(2)),
        scratch_shapes=[vmem(COLS, COLS)],
        compiler_params=PARAMS,
        name="substeps",
    )(slabs, flows, west, east, to_right, to_left, inner)
    home = lax.all_to_all(answers, "lat", 0, 0, tiled=True)
    return pl.pallas_call(
        finish_kernel,
        out_shape=(
            struct(TRACERS, LEVELS, ROWS, COLS),
            struct(2, LEVELS, ROWS, COLS),
            struct(ROWS, COLS),
            struct(ROWS, COLS),
        ),
        in_specs=specs(5, 1),
        out_specs=tuple(specs(4)),
        scratch_shapes=[vmem(COLS, COLS), vmem(4 * ROWS, COLS)],
        compiler_params=PARAMS,
        name="finish",
    )(place, home, own, west, east, along)


def solution(mesh):
    placed = (
        P(None, None, "lat", "lon"),
        P(None, None, "lat", "lon"),
        P("lat", "lon"),
        P(None, "lat", "lon"),
        P("lat", "lon"),
    )
    return jax.shard_map(
        shards,
        mesh=mesh,
        in_specs=placed,
        out_specs=(
            P(None, None, "lat", "lon"),
            P(None, None, "lat", "lon"),
            P("lat", "lon"),
            P("lat", "lon"),
        ),
        check_vma=False,
    )
```

```python
import jax
import jax.numpy as jnp
from jax import lax
from jax.experimental import pallas as pl
from jax.experimental.pallas import tpu as pltpu
from jax.sharding import PartitionSpec as P

TRACERS = 4
LEVELS = 8
SUBSTEPS = 30
ROWS = 16
COLS = 128
MEMBERS = 16
HALO = 32
SLAB = 72
NLAT = ROWS * MEMBERS

time_step = 0.2
tracer_diffusion = 0.2
viscosity = 0.2
thermal_expansion = 2.0
haline_contraction = 1.5
coriolis_base = 1.0
gravity = 140.0
surface_scale = 40.0
thickness = 1.0 / LEVELS
f32 = jnp.float32

PRESSURE, EAST, NORTH, WIND, SURFACE, BOTTOM = 0, 8, 16, 24, 26, 27
PLANES = 28
OWN_EAST, OWN_NORTH, OWN_SURFACE, OWN_WIND, OWN_BOTTOM, OWN = 32, 40, 48, 49, 51, 52
MAIL_N, MAIL_S, CHUNK = SLAB, SLAB + 8, SLAB + 16
BACK = 24


def at(values, step, axis):
    size = values.shape[axis]
    step %= size
    return values if step == 0 else pltpu.roll(values, size - step, axis)


def ids(shape, axis):
    return lax.broadcasted_iota(jnp.int32, shape, axis)


def wide(own, beside):
    return jnp.concatenate([own, beside], axis=1)


def tracer_planes(own_ref):
    bottom = own_ref[OWN_BOTTOM]
    return [
        [jnp.where(bottom > k, own_ref[LEVELS * t + k], 0.0) for k in range(LEVELS)]
        for t in range(TRACERS)
    ]


def pressures(salt, heat):
    total, out = None, []
    for k in range(LEVELS):
        density = haline_contraction * salt[k] - thermal_expansion * heat[k]
        total = density if total is None else total + density
        out.append(thickness * total)
    return out


def pack_kernel(own_ref, right_ref, left_ref):
    c = tracer_planes(own_ref)
    planes = pressures(c[1], c[0])
    planes += [own_ref[n] for n in range(OWN_EAST, OWN_SURFACE)]
    planes += [own_ref[n] for n in (OWN_WIND, OWN_WIND + 1, OWN_SURFACE, OWN_BOTTOM)]
    lane = ids((ROWS, COLS), 1)
    for q in range(PLANES // 4):
        right = left = jnp.zeros((ROWS, COLS), f32)
        for s in range(4):
            moved = at(planes[4 * q + s], -32 * s, 1)
            right = jnp.where(lane // 32 == (s + 3) % 4, moved, right)
            left = jnp.where(lane // 32 == s, moved, left)
        right_ref[q] = right
        left_ref[q] = left
    right = left = jnp.zeros((ROWS, COLS), f32)
    for n in range(TRACERS * LEVELS):
        moved = at(c[n // LEVELS][n % LEVELS], -4 * n, 1)
        right = jnp.where(lane // 4 == (n + 31) % 32, moved, right)
        left = jnp.where(lane // 4 == n, moved, left)
    right_ref[PLANES // 4] = right
    left_ref[PLANES // 4] = left


def beside_plane(west_ref, east_ref, plane):
    q, s = divmod(plane, 4)
    block = ids((ROWS, COLS), 1) // 32
    both = jnp.where(
        block == s, east_ref[q], jnp.where(block == (s + 3) % 4, west_ref[q], 0.0)
    )
    return at(both, 32 * s, 1)


def momentum(k, u, v, p, wind, east, north, f_u, f_v, up, down):
    pair_v = v + down(v)
    pair_u = u + at(u, -1, 1)
    tend_u = (
        (0.25 * f_u) * (pair_v + at(pair_v, 1, 1))
        - (at(p, 1, 1) - p)
        + viscosity * (at(u, 1, 1) + at(u, -1, 1) + up(u) + down(u) - 4.0 * u)
    )
    tend_v = (
        (-0.25 * f_v) * (pair_u + up(pair_u))
        - (up(p) - p)
        + viscosity * (at(v, 1, 1) + at(v, -1, 1) + up(v) + down(v) - 4.0 * v)
    )
    if k == 0:
        tend_u = tend_u + wind[0]
        tend_v = tend_v + wind[1]
    return jnp.where(east, tend_u, 0.0), jnp.where(north, tend_v, 0.0)


def coriolis(rows, offset):
    return coriolis_base * (0.5 + (rows.astype(f32) + offset) / NLAT)


def send_kernel(
    place_ref, own_ref, west_ref, east_ref, _,
    out_ref, flows_ref, split_ref, stack_ref, edge_ref, turned_ref,
):
    place = place_ref[0]
    c = tracer_planes(own_ref)
    p_own = pressures(c[1], c[0])

    def whole(own, plane):
        return wide(own, beside_plane(west_ref, east_ref, plane))

    shape = (ROWS, 2 * COLS)
    row = ids(shape, 0)
    bottom = whole(own_ref[OWN_BOTTOM], BOTTOM)
    wind = [whole(own_ref[OWN_WIND + d], WIND + d) for d in range(2)]

    def up(x):
        return jnp.where(row == ROWS - 1, 0.0, at(x, 1, 0))

    def down(x):
        return jnp.where(row == 0, 0.0, at(x, -1, 0))

    count_u = jnp.minimum(bottom, at(bottom, 1, 1))
    count_v = jnp.minimum(bottom, up(bottom))
    f_u = coriolis(place * ROWS + row, 0.5)
    f_v = coriolis(place * ROWS + row, 1.0)
    sums = [jnp.zeros(shape, f32) for _ in range(4)]
    us, vs, raws = [], [], []
    for k in range(LEVELS):
        east, north = count_u > k, count_v > k
        u = jnp.where(east, whole(own_ref[OWN_EAST + k], EAST + k), 0.0)
        raw = jnp.where(bottom > k, whole(own_ref[OWN_NORTH + k], NORTH + k), 0.0)
        v = jnp.where(north, raw, 0.0)
        p = whole(p_own[k], PRESSURE + k)
        tend_u, tend_v = momentum(k, u, v, p, wind, east, north, f_u, f_v, up, down)
        sums = [a + b for a, b in zip(sums, (u, v, tend_u, tend_v))]
        us.append(u)
        vs.append(v)
        raws.append(raw)
        pair = u + at(u, -1, 1)
        last = p[8:] + (-0.25 * f_v[8:]) * pair[8:] + viscosity * at(v, -1, 0)[8:]
        if k == 0:
            last = last + wind[1][8:]
        first = (-0.25 * (f_v[:8] - 1.0 / NLAT)) * pair[:8] - p[:8] + viscosity * v[:8]
        edge_ref[k : k + 1] = u[15:16]
        edge_ref[8 + k : 9 + k] = raw[15:16]
        edge_ref[16 + k : 17 + k] = last[7:8]
        edge_ref[24 + k : 25 + k] = u[0:1]
        edge_ref[32 + k : 33 + k] = first[0:1]
    surface = whole(own_ref[OWN_SURFACE], SURFACE)
    for n, values in enumerate((surface, *sums, bottom)):
        split_ref[ROWS * n : ROWS * (n + 1)] = values[:, :COLS]
        split_ref[ROWS * (6 + n) : ROWS * (7 + n)] = values[:, COLS:]
    for q in range(16):
        spot = pl.multiple_of(lax.rem(q + place, 16) * 8, 8)
        for half in range(2):
            if q < 12:
                rows = split_ref[pl.ds(ROWS * (6 * half + q // 2) + q % 2, 8, 2), :]
            else:
                rows = edge_ref[8 * (q - 12) : 8 * (q - 11), COLS * half : COLS * (half + 1)]
            stack_ref[half, pl.ds(spot, 8)] = rows
    turned_ref[HALO : HALO + COLS] = stack_ref[0].T
    beyond = stack_ref[1].T
    turned_ref[:HALO] = beyond[COLS - HALO :]
    turned_ref[HALO + COLS :] = beyond[:HALO]
    edge = edge_ref[32:40]
    sub = ids((8, COLS), 0)
    tile_lane = ids((8, COLS), 1)
    spare_block = tile_lane // 8 == lax.rem(6 + place, 16)
    moved = [at(edge, 8 * d - HALO + 4, 1)[:, :COLS] for d in range(MEMBERS)]
    halves = [at(edge, 8 * d - HALO + 4 - 64, 1)[:, :COLS] for d in range(MEMBERS)]
    rests = [jnp.where(tile_lane % 8 == sub, x[:, 64:65], 0.0) for x in moved]
    for step in (1, 2, 4):
        rests = [x + at(x, step, 0) for x in rests]
    for d in range(MEMBERS):
        pairs = jnp.where(tile_lane < 64, moved[d], at(halves[d], 1, 0))
        rest = rests[d]
        out_ref[d, :8] = jnp.where(
            sub == 0, pairs, jnp.where(sub == 1, at(pairs, 1, 0), turned_ref[8 * d : 8 * d + 8])
        )
        out_ref[d, 8 : SLAB - 8] = turned_ref[8 * d + 8 : 8 * d + SLAB - 8]
        end = turned_ref[8 * d + SLAB - 8 : 8 * d + SLAB]
        end = jnp.where((sub == 5) & spare_block, rest, end)
        end = jnp.where(sub == 6, at(pairs, -2, 0), end)
        out_ref[d, SLAB - 8 : SLAB] = jnp.where(sub == 7, at(pairs, -1, 0), end)

    for n, values in enumerate((*us, count_u)):
        flows_ref[ROWS * n : ROWS * (n + 1)] = values


    def spare(n):
        t, k = divmod(n, LEVELS)
        if t == 0:
            return us[k][:, :COLS], us[k][:, :COLS]
        if t == 1:
            return raws[k][:, :COLS], vs[k][:, :COLS]
        if t == 2:
            return raws[k][:, COLS:], us[k][:, COLS:]
        if k < 2:
            own = bottom[:, COLS * k : COLS * (k + 1)]
            return own, own
        return None

    def tops(n):
        own = c[n // LEVELS][n % LEVELS][8:]
        more = spare(n)
        return own if more is None else jnp.where(sub == 4, at(more[0][8:], 3, 0), own)

    def bottoms(n):
        own = c[n // LEVELS][n % LEVELS][:8]
        more = spare(n)
        return own if more is None else jnp.where(sub == 3, at(more[1][:8], -3, 0), own)

    for m in range(MEMBERS):
        out_ref[m, MAIL_N:MAIL_S] = jnp.where(sub >= 4, tops(2 * m), at(tops(2 * m + 1), 4, 0))
        out_ref[m, MAIL_S:CHUNK] = jnp.where(sub < 4, bottoms(2 * m), at(bottoms(2 * m + 1), 4, 0))


def edge_steps(flows_ref, west_ref, east_ref, right_ref, left_ref, inner_ref, along_ref):
    block = ids((ROWS, COLS), 1) // 4
    count = flows_ref[ROWS * LEVELS :]

    def packed(of_level, half, ahead):
        tile = jnp.zeros((ROWS, COLS), f32)
        for k in range(LEVELS):
            values = of_level(k)[:, COLS * half : COLS * (half + 1)]
            tile = jnp.where(block % LEVELS == k, at(values, -4 * (k + ahead), 1), tile)
        return tile

    def repeated(tile):
        for step in (32, 64):
            tile = jnp.where(block * 4 % (2 * step) < step, tile, at(tile, -step, 1))
        return tile

    def flow(k):
        return flows_ref[ROWS * k : ROWS * (k + 1)]

    def diffusion(k):
        return jnp.where(count > k, tracer_diffusion, 0.0)

    tiles = []
    for what in ((flow, 1, 1), (flow, 0, 0), (flow, 0, 1), (diffusion, 1, 1), (diffusion, 0, 1)):
        tiles.append(packed(*what))
        yield
    tiles = [repeated(tile) for tile in tiles]
    yield
    last = PLANES // 4
    low, high = outer(
        at(west_ref[last], -4, 1), east_ref[last], left_ref[last], at(right_ref[last], -4, 1),
        *tiles,
    )
    high = at(high, 4, 1)
    yield
    waiting = []
    for n in range(TRACERS * LEVELS):
        both = jnp.where(block == n, low, jnp.where(block == (n + 31) % 32, high, 0.0))
        waiting.append((slice(ROWS * n, ROWS * (n + 1)), at(both, 4 * n, 1)))
        if n % 2:
            yield
    for rows, side in waiting:
        along_ref[rows] = inner_ref[rows] + side


def slab_kernel(
    in_ref, flows_ref, west_ref, east_ref, right_ref, left_ref, inner_ref,
    out_ref, along_ref, edge_ref,
):
    shape = (SLAB, COLS)
    lane = ids(shape, 1)
    r = lane % 8
    block = ids((8, COLS), 1) // 8

    tiles = []
    for t in range(SLAB // 8):
        now = [in_ref[a, 8 * t : 8 * t + 8] for a in range(MEMBERS)]
        for bit in (1, 2, 4, 8):
            odd = (block & bit) > 0
            now = [jnp.where(odd, now[(a + bit) % MEMBERS], now[a]) for a in range(MEMBERS)]
        tiles.append([at(now[-q % MEMBERS], 8 * q, 1) for q in range(16)])
    blocks = [jnp.concatenate([tile[q] for tile in tiles], axis=0) for q in range(16)]
    surface, start_u, start_v, force_u, force_v, bottom = (blocks[2 * n : 2 * n + 2] for n in range(6))
    u_a, v_raw, near, u_next = blocks[12:]
    zeros = jnp.zeros((8, COLS), f32)
    sub = ids((8, COLS), 0)
    edge_ref[COLS - 8 :] = zeros
    for a in range(1, MEMBERS):
        begin, end = in_ref[a, :8], in_ref[a, SLAB - 8 : SLAB]
        rows = jnp.where(sub < 2, begin, at(begin, -1, 0))
        rows = jnp.where(sub < 4, rows, jnp.where(sub < 6, at(end, 2, 0), at(end, 1, 0)))
        edge_ref[8 * a - 8 : 8 * a] = jnp.where(sub % 2 == 0, rows, at(at(rows, 64, 1), -1, 0))
    column = ids(shape, 0)
    far = at(edge_ref[...].T[:SLAB], -4, 0)
    far = jnp.where(column == 68, at(at(force_u[0], 1, 0), 8, 1), far)
    unused = (column < 2) | (column >= SLAB - 2)
    bottom = [jnp.where(unused, float(LEVELS), b) for b in bottom]

    top = lane == COLS - 1
    count_u = [jnp.minimum(b, at(b, 1, 0)) for b in bottom]
    count_v = [
        jnp.minimum(*bottom),
        jnp.where(top, 0.0, jnp.minimum(bottom[1], at(bottom[0], 1, 1))),
    ]

    square = (COLS, COLS)

    def spread_from(lane_at, values):
        chosen = ids(square, 0) == ids(square, 1) // 8 * 8 + lane_at
        spread = jnp.dot(
            jnp.concatenate(values, axis=0).astype(jnp.bfloat16),
            chosen.astype(f32).astype(jnp.bfloat16),
            preferred_element_type=f32,
        )
        return [spread[SLAB * n : SLAB * (n + 1)] for n in range(len(values))]

    count_ua, count_va, count_vc = spread_from(7, [count_u[1], count_v[1], count_v[0]])
    count_ub, count_vb = spread_from(8, [count_u[0], count_v[0]])
    level = r.astype(f32)
    last = lane >= COLS - 8
    v_a = jnp.where(count_va > level, v_raw, 0.0)
    u_a = jnp.where(last, 0.0, u_a)
    u_b = jnp.where(last, 0.0, at(u_next, 8, 1))
    f_a = 0.25 * coriolis(lane // 8 * ROWS + 15, 0.5)
    f_b = f_a + 0.25 * coriolis_base / NLAT
    pair = v_a + at(v_a, 1, 0)
    spread = viscosity * (at(v_a, 1, 0) + at(v_a, -1, 0) - 4.0 * v_a)
    terms = jnp.concatenate(
        [
            jnp.where(count_ua > level, f_a * pair + viscosity * u_b, 0.0),
            jnp.where(count_ub > level, f_b * pair + viscosity * u_a, 0.0),
            jnp.where(count_vb > level, viscosity * v_a, 0.0),
            jnp.where(count_vc > level, viscosity * v_a, 0.0),
            jnp.where(count_va > level, near + far + spread, 0.0),
            v_a,
        ],
        axis=0,
    )
    for step in (1, 2, 4):
        terms = terms + at(terms, -step, 1)
    shifted = at(terms[SLAB : 3 * SLAB], -1, 1)
    u_15, v_14, v_15, begin_15 = (
        jnp.where(r == 7, terms[SLAB * n : SLAB * (n + 1)], 0.0) for n in (0, 3, 4, 5)
    )
    u_16, v_16 = (jnp.where(r == 0, shifted[SLAB * n : SLAB * (n + 1)], 0.0) for n in range(2))
    force_u = [force_u[0] + u_16, force_u[1] + u_15]
    force_v = [force_v[0] + (v_14 + v_16), force_v[1] + v_15]
    start_v = [start_v[0], start_v[1] + begin_15]

    sub_step = time_step / SUBSTEPS
    held_u, held_v, flux_u, flux_v, begin_u, begin_v = [], [], [], [], [], []
    for i in range(2):
        per = 1.0 / jnp.maximum(count_u[i], 1.0)
        open_face = jnp.where(count_u[i] > 0.0, sub_step, 0.0)
        flux_u.append((sub_step * surface_scale * thickness) * count_u[i])
        held_u.append(
            (
                (0.25 * open_face) * coriolis(2 * lane + i, 0.5),
                gravity * open_face,
                open_face * (force_u[i] * per),
            )
        )
        begin_u.append(start_u[i] * per)
        per = 1.0 / jnp.maximum(count_v[i], 1.0)
        open_face = jnp.where(count_v[i] > 0.0, sub_step, 0.0)
        flux_v.append((sub_step * surface_scale * thickness) * count_v[i])
        held_v.append(
            (
                (-0.25 * open_face) * coriolis(2 * lane + i, 1.0),
                gravity * open_face,
                open_face * (force_v[i] * per),
            )
        )
        begin_v.append(start_v[i] * per)
    held = (
        *flux_u, at(flux_u[0], 1, 1), *flux_v, at(flux_v[0], 1, 1), at(flux_v[1], -1, 1),
        *held_u[0], *held_u[1], *held_v[0], *held_v[1],
    )
    state = (*surface, at(surface[0], 1, 1), *begin_u, *begin_v)
    total = (zeros,) * 4
    beside = edge_steps(flows_ref, west_ref, east_ref, right_ref, left_ref, inner_ref, along_ref)
    for low, steps in ((0, 6), (8, 8), (16, 8), (24, 8)):
        cut = 8 if low else 0
        state = tuple(x[cut : x.shape[0] - cut] for x in state)
        (
            du0, du1, du2, dv0, dv1, dv2, dv_, cu0, gu0, fu0, cu1, gu1, fu1,
            cv0, gv0, fv0, cv1, gv1, fv1,
        ) = (x[low : SLAB - low] for x in held)
        centre = HALO - low

        def advance(_, carry):
            h0, h1, h2, u0, u1, v0, v1, *sums = carry
            v_ = at(v1, -1, 1)
            u2 = at(u0, 1, 1)
            v2 = at(v0, 1, 1)
            x0, x1, x2 = du0 * u0, du1 * u1, du2 * u2
            y0, y1 = dv0 * v0, dv1 * v1
            h1 = h1 - ((x1 - at(x1, -1, 0)) + (y1 - y0))
            h0 = h0 - ((x0 - at(x0, -1, 0)) + (y0 - dv_ * v_))
            h2 = h2 - ((x2 - at(x2, -1, 0)) + (dv2 * v2 - y1))
            p0, p1, p2 = u0 + at(u0, -1, 0), u1 + at(u1, -1, 0), u2 + at(u2, -1, 0)
            q0, q1 = v0 + v_, v1 + v0
            u0 = (u0 + fu0) + (cu0 * (q0 + at(q0, 1, 0)) - gu0 * (at(h0, 1, 0) - h0))
            u1 = (u1 + fu1) + (cu1 * (q1 + at(q1, 1, 0)) - gu1 * (at(h1, 1, 0) - h1))
            v0 = (v0 + fv0) + (cv0 * (p0 + p1) - gv0 * (h1 - h0))
            v1 = (v1 + fv1) + (cv1 * (p1 + p2) - gv1 * (h2 - h1))
            sums = [a + b[centre : centre + 8] for a, b in zip(sums, (u0, u1, v0, v1))]
            return (h0, h1, h2, u0, u1, v0, v1, *sums)

        carry = (*state, *total)
        for step in range(steps):
            carry = advance(step, carry)
            if low:
                next(beside, None)
        state, total = carry[:7], carry[7:]
    for _ in beside:
        pass
    height = [x[8:16] for x in state[:2]]
    average = [x * (1.0 / SUBSTEPS) for x in total]
    transport = [
        (-thickness * count_u[i][HALO : HALO + 8]) * average[i] for i in range(2)
    ]
    before = jnp.concatenate(
        [
            (ids(square, 0) < (ids(square, 1) - 8 * n) % COLS).astype(f32).astype(jnp.bfloat16)
            for n in (2, 3)
        ],
        axis=1,
    )
    rest = jnp.concatenate([transport[0] + transport[1], zeros], axis=0)
    parts = []
    for _ in range(3):
        parts.append(rest.astype(jnp.bfloat16).astype(f32))
        rest = rest - parts[-1]
    sums = jnp.dot(
        jnp.concatenate(parts, axis=0).astype(jnp.bfloat16),
        before,
        preferred_element_type=f32,
    )
    south = (sums[32:40] + sums[16:24]) + sums[:8]
    stream = [transport[0], transport[0] + transport[1]]
    results = [*height, *stream, *average]
    moved = [at(values, -8 * n, 1) for n, values in enumerate(results)]
    moved[2] = south[:, :COLS] + moved[2]
    moved[3] = south[:, COLS:] + moved[3]
    for e in range(MEMBERS):
        packed = moved[0]
        for n in range(1, 8):
            packed = jnp.where(block == (e + n) % 16, moved[n], packed)
        out_ref[e, 0:8] = packed
        out_ref[e, 8:16] = in_ref[(e + 15) % MEMBERS, MAIL_N:MAIL_S]
        out_ref[e, 16:24] = in_ref[(e + 1) % MEMBERS, MAIL_S:CHUNK]


def gain(values, axis, flow, diffusion):
    ahead = at(values, 1, axis)
    sides = at(values, -1, axis) + at(values, 2, axis)
    far = at(values, -2, axis) + at(values, 3, axis)
    face = (37.0 * (values + ahead) - 8.0 * sides + far) * (1.0 / 60.0)
    flux = diffusion * (ahead - values) - flow * face
    return flux - at(flux, -1, axis)


def inner_kernel(own_ref, out_ref):
    bottom = own_ref[OWN_BOTTOM]
    c = tracer_planes(own_ref)
    count = jnp.minimum(bottom, at(bottom, 1, 1))
    values = jnp.concatenate([plane for tracer in c for plane in tracer], axis=0)
    flow, diffusion = [], []
    for k in range(LEVELS):
        flow.append(jnp.where(count > k, own_ref[OWN_EAST + k], 0.0))
        diffusion.append(jnp.where(count > k, tracer_diffusion, 0.0))
    flow, diffusion = (jnp.concatenate(x * TRACERS, axis=0) for x in (flow, diffusion))
    lane = ids(values.shape, 1)

    def moved(step):
        inside = lane < COLS - step if step > 0 else lane >= -step
        return jnp.where(inside, at(values, step, 1), 0.0)

    ahead = moved(1)
    face = (37.0 * (values + ahead) - 8.0 * (moved(-1) + moved(2)) + (moved(-2) + moved(3))) * (
        1.0 / 60.0
    )
    flux = jnp.where(lane < COLS - 1, diffusion * (ahead - values) - flow * face, 0.0)
    out_ref[...] = flux - at(flux, -1, 1)


def outer(west, east, left, right, flow_w, flow_l, flow_r, diff_w, diff_r):
    q = ids((ROWS, COLS), 1) % 4
    sixtieth = 1.0 / 60.0
    w1, w2, w3 = at(west, 3, 1), at(west, 2, 1), at(west, 1, 1)
    face = 37.0 * (w1 + left) - 8.0 * (w2 + at(left, 1, 1)) + (w3 + at(left, 2, 1))
    through = at(diff_w, 3, 1) * (left - w1) - at(flow_w, 3, 1) * (face * sixtieth)
    flux = jnp.where(q == 0, w2 - 8.0 * w1, jnp.where(q == 1, w2, 0.0)) * (-sixtieth) * flow_l
    low = flux - at(flux, -1, 1) - jnp.where(q == 0, through, 0.0)
    e1, e2, e3 = at(east, -3, 1), at(east, -2, 1), at(east, -1, 1)
    face = 37.0 * (right + e1) - 8.0 * (at(right, -1, 1) + e2) + (at(right, -2, 1) + e3)
    through = diff_r * (e1 - right) - flow_r * (face * sixtieth)
    flux = jnp.where(q == 2, e3 - 8.0 * e2, jnp.where(q == 1, e3, 0.0)) * (-sixtieth) * flow_r
    high = flux - at(flux, -1, 1) + jnp.where(q == 3, through, 0.0)
    return low, high


def finish_kernel(
    place_ref, in_ref, own_ref, west_ref, east_ref, along_ref,
    tracers_out, velocity_out, height_out, stream_out, turned_ref, rows_ref,
):
    place = place_ref[0]
    turned_ref[...] = in_ref[:, 0:8].reshape(COLS, COLS).T

    for q in range(8):
        spot = pl.multiple_of(lax.rem(q + place, 16) * 8, 8)
        rows_ref[pl.ds(ROWS * (q // 2) + q % 2, 8, 2), :] = turned_ref[pl.ds(spot, 8)]
    height_out[...] = rows_ref[:ROWS]
    stream_out[...] = rows_ref[ROWS : 2 * ROWS]
    average_u, average_v = rows_ref[2 * ROWS : 3 * ROWS], rows_ref[3 * ROWS :]

    sub = ids((8, COLS), 0)
    tall = (ROWS + 8, 2 * COLS)
    row = ids(tall, 0)
    first, last = place == 0, place == MEMBERS - 1

    def lat_tile(n):
        south = jnp.where(first, 0.0, in_ref[n // 2, 8:16])
        north = jnp.where(last, 0.0, in_ref[n // 2, 16:24])
        if n % 2 == 0:
            return jnp.where(sub < 4, north, south)
        return at(jnp.where(sub < 4, south, north), 4, 0)

    def spare_north(tile):
        return jnp.where(sub == 0, at(tile, 3, 0), 0.0)

    def spare_south(tile):
        return jnp.where(sub == 7, at(tile, -3, 0), 0.0)

    def tallen(own, tile):
        return jnp.concatenate([own, tile], axis=0)

    def whole(own, plane):
        return wide(own, beside_plane(west_ref, east_ref, plane))

    tiles = [[lat_tile(LEVELS * t + k) for k in range(LEVELS)] for t in range(TRACERS)]
    bottom_own = own_ref[OWN_BOTTOM]
    c = tracer_planes(own_ref)
    p_own = pressures(c[1], c[0])
    p_tile = pressures(tiles[1], tiles[0])
    both = wide(
        spare_north(tiles[3][0]) + spare_south(tiles[3][0]),
        spare_north(tiles[3][1]) + spare_south(tiles[3][1]),
    )
    bottom = tallen(whole(bottom_own, BOTTOM), both)
    count_u = jnp.minimum(bottom, at(bottom, 1, 1))
    count_v = jnp.minimum(bottom, at(bottom, 1, 0))
    f_u = coriolis(place * ROWS + row, 0.5)
    f_v = coriolis(place * ROWS + row, 1.0)
    none = jnp.zeros((8, COLS), f32)
    wind = [tallen(wide(own_ref[OWN_WIND + d], jnp.zeros((ROWS, COLS), f32)), jnp.zeros((8, 2 * COLS), f32)) for d in range(2)]

    def up(x):
        return at(x, 1, 0)

    def down(x):
        return at(x, -1, 0)

    stars_u, stars_v, gains = [], [], [None] * (TRACERS * LEVELS)
    own_u, own_v = count_u[:ROWS, :COLS], count_v[:ROWS, :COLS]
    mean_u = mean_v = jnp.zeros((ROWS, COLS), f32)
    for k in range(LEVELS):
        east, north = count_u > k, count_v > k
        t0, t1, t2 = tiles[0][k], tiles[1][k], tiles[2][k]
        u_lat = wide(spare_north(t0) + spare_south(t0), spare_north(t2))
        v_lat = wide(spare_north(t1) + spare_south(t1), spare_south(t2))
        u = tallen(whole(own_ref[OWN_EAST + k], EAST + k), u_lat)
        u = jnp.where(east | (row >= ROWS), u, 0.0)
        v = tallen(whole(own_ref[OWN_NORTH + k], NORTH + k), v_lat)
        v = jnp.where(north | (row == ROWS), v, 0.0)
        p = tallen(whole(p_own[k], PRESSURE + k), wide(p_tile[k], none))
        tend_u, tend_v = momentum(k, u, v, p, wind, east, north, f_u, f_v, up, down)
        star_u = (u + time_step * tend_u)[:ROWS, :COLS]
        star_v = (v + time_step * tend_v)[:ROWS, :COLS]
        stars_u.append(star_u)
        stars_v.append(star_v)
        mean_u = mean_u + star_u
        mean_v = mean_v + star_v

        diffusion = jnp.where(north[:, :COLS], tracer_diffusion, 0.0)
        for t in range(TRACERS):
            cn = tallen(c[t][k], tiles[t][k])
            gains[LEVELS * t + k] = gain(cn, 0, v[:, :COLS], diffusion)[:ROWS]
    for n in range(TRACERS * LEVELS):
        t, k = divmod(n, LEVELS)
        change = along_ref[ROWS * n : ROWS * (n + 1)] + gains[n]
        tracers_out[t, k] = jnp.where(bottom_own > k, c[t][k] + time_step * change, 0.0)
    shift_u = average_u - mean_u / jnp.maximum(own_u, 1.0)
    shift_v = average_v - mean_v / jnp.maximum(own_v, 1.0)
    for k in range(LEVELS):
        velocity_out[0, k] = jnp.where(own_u > k, stars_u[k] + shift_u, 0.0)
        velocity_out[1, k] = jnp.where(own_v > k, stars_v[k] + shift_v, 0.0)


def ring(axis, step):
    count = lax.axis_size(axis)
    return [(i, (i + step) % count) for i in range(count)]


def struct(*shape):
    return jax.ShapeDtypeStruct(shape, f32)


def vmem(*shape):
    return pltpu.VMEM(shape, f32)


def specs(count, scalars=0):
    return [pl.BlockSpec(memory_space=pltpu.SMEM)] * scalars + [
        pl.BlockSpec(memory_space=pltpu.VMEM)
    ] * count


PARAMS = pltpu.CompilerParams(vmem_limit_bytes=32 * 1024 * 1024)


def stacked(tracers, velocity, surface, wind, bottom):
    def put(values, first):
        values = values.reshape(-1, ROWS, COLS)
        after = OWN - first - values.shape[0]
        return lax.pad(
            values, jnp.zeros((), values.dtype), ((first, after, 0), (0, 0, 0), (0, 0, 0))
        )

    return (
        put(tracers, 0)
        + put(velocity, OWN_EAST)
        + put(surface, OWN_SURFACE)
        + put(wind, OWN_WIND)
        + put(bottom, OWN_BOTTOM).astype(f32)
    )


def shards(tracers, velocity, surface, wind, bottom):
    place = lax.axis_index("lat").astype(jnp.int32).reshape(1)
    own = stacked(tracers, velocity, surface, wind, bottom)
    payload = struct(PLANES // 4 + 1, ROWS, COLS)
    to_right, to_left = pl.pallas_call(
        pack_kernel,
        out_shape=(payload, payload),
        in_specs=specs(1),
        out_specs=tuple(specs(2)),
        compiler_params=PARAMS,
        name="pack",
    )(own)
    west = lax.ppermute(to_right, "lon", ring("lon", 1))
    east = lax.ppermute(to_left, "lon", ring("lon", -1))
    inner = pl.pallas_call(
        inner_kernel,
        out_shape=struct(TRACERS * LEVELS * ROWS, COLS),
        in_specs=specs(1),
        out_specs=specs(1)[0],
        compiler_params=PARAMS,
        cost_estimate=pl.CostEstimate(flops=1500000, bytes_accessed=3000000, transcendentals=0),
        name="inner",
    )(own)
    chunks, flows = pl.pallas_call(
        send_kernel,
        out_shape=(
            struct(MEMBERS, CHUNK, COLS),
            struct((LEVELS + 1) * ROWS, 2 * COLS),
        ),
        in_specs=specs(3, 1) + [pl.BlockSpec(memory_space=pl.ANY)],
        out_specs=tuple(specs(2)),
        scratch_shapes=[
            vmem(12 * ROWS, COLS),
            vmem(2, COLS, COLS),
            vmem(40, 2 * COLS),
            vmem(COLS + 2 * HALO, COLS),
        ],
        compiler_params=PARAMS,
        name="columns",
    )(place, own, west, east, inner)
    slabs = lax.all_to_all(chunks, "lat", 0, 0, tiled=True)
    answers, along = pl.pallas_call(
        slab_kernel,
        out_shape=(
            struct(MEMBERS, BACK, COLS),
            struct(TRACERS * LEVELS * ROWS, COLS),
        ),
        in_specs=specs(7),
        out_specs=tuple(specs(2)),
        scratch_shapes=[vmem(COLS, COLS)],
        compiler_params=PARAMS,
        name="substeps",
    )(slabs, flows, west, east, to_right, to_left, inner)
    home = lax.all_to_all(answers, "lat", 0, 0, tiled=True)
    return pl.pallas_call(
        finish_kernel,
        out_shape=(
            struct(TRACERS, LEVELS, ROWS, COLS),
            struct(2, LEVELS, ROWS, COLS),
            struct(ROWS, COLS),
            struct(ROWS, COLS),
        ),
        in_specs=specs(5, 1),
        out_specs=tuple(specs(4)),
        scratch_shapes=[vmem(COLS, COLS), vmem(4 * ROWS, COLS)],
        compiler_params=PARAMS,
        name="finish",
    )(place, home, own, west, east, along)


def solution(mesh):
    placed = (
        P(None, None, "lat", "lon"),
        P(None, None, "lat", "lon"),
        P("lat", "lon"),
        P(None, "lat", "lon"),
        P("lat", "lon"),
    )
    return jax.shard_map(
        shards,
        mesh=mesh,
        in_specs=placed,
        out_specs=(
            P(None, None, "lat", "lon"),
            P(None, None, "lat", "lon"),
            P("lat", "lon"),
            P("lat", "lon"),
        ),
        check_vma=False,
    )
```

```python
import jax
import jax.numpy as jnp
from jax import lax
from jax.experimental import pallas as pl
from jax.experimental.pallas import tpu as pltpu
from jax.sharding import PartitionSpec as P

TRACERS = 4
LEVELS = 8
SUBSTEPS = 30
ROWS = 16
COLS = 128
MEMBERS = 16
HALO = 32
SLAB = 72
NLAT = ROWS * MEMBERS

time_step = 0.2
tracer_diffusion = 0.2
viscosity = 0.2
thermal_expansion = 2.0
haline_contraction = 1.5
coriolis_base = 1.0
gravity = 140.0
surface_scale = 40.0
thickness = 1.0 / LEVELS
f32 = jnp.float32

PRESSURE, EAST, NORTH, WIND, SURFACE, BOTTOM = 0, 8, 16, 24, 26, 27
PLANES = 28
OWN_EAST, OWN_NORTH, OWN_SURFACE, OWN_WIND, OWN_BOTTOM, OWN = 32, 40, 48, 49, 51, 52
MAIL_N, MAIL_S, CHUNK = SLAB, SLAB + 8, SLAB + 16
BACK = 24


def at(values, step, axis):
    size = values.shape[axis]
    step %= size
    return values if step == 0 else pltpu.roll(values, size - step, axis)


def ids(shape, axis):
    return lax.broadcasted_iota(jnp.int32, shape, axis)


def wide(own, beside):
    return jnp.concatenate([own, beside], axis=1)


def tracer_planes(own_ref):
    bottom = own_ref[OWN_BOTTOM]
    return [
        [jnp.where(bottom > k, own_ref[LEVELS * t + k], 0.0) for k in range(LEVELS)]
        for t in range(TRACERS)
    ]


def pressures(salt, heat):
    total, out = None, []
    for k in range(LEVELS):
        density = haline_contraction * salt[k] - thermal_expansion * heat[k]
        total = density if total is None else total + density
        out.append(thickness * total)
    return out


def pack_kernel(own_ref, right_ref, left_ref):
    c = tracer_planes(own_ref)
    planes = pressures(c[1], c[0])
    planes += [own_ref[n] for n in range(OWN_EAST, OWN_SURFACE)]
    planes += [own_ref[n] for n in (OWN_WIND, OWN_WIND + 1, OWN_SURFACE, OWN_BOTTOM)]
    lane = ids((ROWS, COLS), 1)
    for q in range(PLANES // 4):
        right = left = jnp.zeros((ROWS, COLS), f32)
        for s in range(4):
            moved = at(planes[4 * q + s], -32 * s, 1)
            right = jnp.where(lane // 32 == (s + 3) % 4, moved, right)
            left = jnp.where(lane // 32 == s, moved, left)
        right_ref[q] = right
        left_ref[q] = left
    right = left = jnp.zeros((ROWS, COLS), f32)
    for n in range(TRACERS * LEVELS):
        moved = at(c[n // LEVELS][n % LEVELS], -4 * n, 1)
        right = jnp.where(lane // 4 == (n + 31) % 32, moved, right)
        left = jnp.where(lane // 4 == n, moved, left)
    right_ref[PLANES // 4] = right
    left_ref[PLANES // 4] = left


def beside_plane(west_ref, east_ref, plane):
    q, s = divmod(plane, 4)
    block = ids((ROWS, COLS), 1) // 32
    both = jnp.where(
        block == s, east_ref[q], jnp.where(block == (s + 3) % 4, west_ref[q], 0.0)
    )
    return at(both, 32 * s, 1)


def momentum(k, u, v, p, wind, east, north, f_u, f_v, up, down):
    pair_v = v + down(v)
    pair_u = u + at(u, -1, 1)
    tend_u = (
        (0.25 * f_u) * (pair_v + at(pair_v, 1, 1))
        - (at(p, 1, 1) - p)
        + viscosity * (at(u, 1, 1) + at(u, -1, 1) + up(u) + down(u) - 4.0 * u)
    )
    tend_v = (
        (-0.25 * f_v) * (pair_u + up(pair_u))
        - (up(p) - p)
        + viscosity * (at(v, 1, 1) + at(v, -1, 1) + up(v) + down(v) - 4.0 * v)
    )
    if k == 0:
        tend_u = tend_u + wind[0]
        tend_v = tend_v + wind[1]
    return jnp.where(east, tend_u, 0.0), jnp.where(north, tend_v, 0.0)


def coriolis(rows, offset):
    return coriolis_base * (0.5 + (rows.astype(f32) + offset) / NLAT)


def send_kernel(
    place_ref, own_ref, west_ref, east_ref, _,
    out_ref, flows_ref, split_ref, stack_ref, edge_ref, turned_ref,
):
    place = place_ref[0]
    c = tracer_planes(own_ref)
    p_own = pressures(c[1], c[0])

    def whole(own, plane):
        return wide(own, beside_plane(west_ref, east_ref, plane))

    shape = (ROWS, 2 * COLS)
    row = ids(shape, 0)
    bottom = whole(own_ref[OWN_BOTTOM], BOTTOM)
    wind = [whole(own_ref[OWN_WIND + d], WIND + d) for d in range(2)]

    def up(x):
        return jnp.where(row == ROWS - 1, 0.0, at(x, 1, 0))

    def down(x):
        return jnp.where(row == 0, 0.0, at(x, -1, 0))

    count_u = jnp.minimum(bottom, at(bottom, 1, 1))
    count_v = jnp.minimum(bottom, up(bottom))
    f_u = coriolis(place * ROWS + row, 0.5)
    f_v = coriolis(place * ROWS + row, 1.0)
    sums = [jnp.zeros(shape, f32) for _ in range(4)]
    us, vs, raws = [], [], []
    for k in range(LEVELS):
        east, north = count_u > k, count_v > k
        u = jnp.where(east, whole(own_ref[OWN_EAST + k], EAST + k), 0.0)
        raw = jnp.where(bottom > k, whole(own_ref[OWN_NORTH + k], NORTH + k), 0.0)
        v = jnp.where(north, raw, 0.0)
        p = whole(p_own[k], PRESSURE + k)
        tend_u, tend_v = momentum(k, u, v, p, wind, east, north, f_u, f_v, up, down)
        sums = [a + b for a, b in zip(sums, (u, v, tend_u, tend_v))]
        us.append(u)
        vs.append(v)
        raws.append(raw)
        pair = u + at(u, -1, 1)
        last = p[8:] + (-0.25 * f_v[8:]) * pair[8:] + viscosity * at(v, -1, 0)[8:]
        if k == 0:
            last = last + wind[1][8:]
        first = (-0.25 * (f_v[:8] - 1.0 / NLAT)) * pair[:8] - p[:8] + viscosity * v[:8]
        edge_ref[k : k + 1] = u[15:16]
        edge_ref[8 + k : 9 + k] = raw[15:16]
        edge_ref[16 + k : 17 + k] = last[7:8]
        edge_ref[24 + k : 25 + k] = u[0:1]
        edge_ref[32 + k : 33 + k] = first[0:1]
    surface = whole(own_ref[OWN_SURFACE], SURFACE)
    for n, values in enumerate((surface, *sums, bottom)):
        split_ref[ROWS * n : ROWS * (n + 1)] = values[:, :COLS]
        split_ref[ROWS * (6 + n) : ROWS * (7 + n)] = values[:, COLS:]
    for q in range(16):
        spot = pl.multiple_of(lax.rem(q + place, 16) * 8, 8)
        for half in range(2):
            if q < 12:
                rows = split_ref[pl.ds(ROWS * (6 * half + q // 2) + q % 2, 8, 2), :]
            else:
                rows = edge_ref[8 * (q - 12) : 8 * (q - 11), COLS * half : COLS * (half + 1)]
            stack_ref[half, pl.ds(spot, 8)] = rows
    turned_ref[HALO : HALO + COLS] = stack_ref[0].T
    beyond = stack_ref[1].T
    turned_ref[:HALO] = beyond[COLS - HALO :]
    turned_ref[HALO + COLS :] = beyond[:HALO]
    edge = edge_ref[32:40]
    sub = ids((8, COLS), 0)
    tile_lane = ids((8, COLS), 1)
    spare_block = tile_lane // 8 == lax.rem(6 + place, 16)
    moved = [at(edge, 8 * d - HALO + 4, 1)[:, :COLS] for d in range(MEMBERS)]
    halves = [at(edge, 8 * d - HALO + 4 - 64, 1)[:, :COLS] for d in range(MEMBERS)]
    rests = [jnp.where(tile_lane % 8 == sub, x[:, 64:65], 0.0) for x in moved]
    for step in (1, 2, 4):
        rests = [x + at(x, step, 0) for x in rests]
    for d in range(MEMBERS):
        pairs = jnp.where(tile_lane < 64, moved[d], at(halves[d], 1, 0))
        rest = rests[d]
        out_ref[d, :8] = jnp.where(
            sub == 0, pairs, jnp.where(sub == 1, at(pairs, 1, 0), turned_ref[8 * d : 8 * d + 8])
        )
        out_ref[d, 8 : SLAB - 8] = turned_ref[8 * d + 8 : 8 * d + SLAB - 8]
        end = turned_ref[8 * d + SLAB - 8 : 8 * d + SLAB]
        end = jnp.where((sub == 5) & spare_block, rest, end)
        end = jnp.where(sub == 6, at(pairs, -2, 0), end)
        out_ref[d, SLAB - 8 : SLAB] = jnp.where(sub == 7, at(pairs, -1, 0), end)

    for n, values in enumerate((*us, count_u)):
        flows_ref[ROWS * n : ROWS * (n + 1)] = values


    def spare(n):
        t, k = divmod(n, LEVELS)
        if t == 0:
            return us[k][:, :COLS], us[k][:, :COLS]
        if t == 1:
            return raws[k][:, :COLS], vs[k][:, :COLS]
        if t == 2:
            return raws[k][:, COLS:], us[k][:, COLS:]
        if k < 2:
            own = bottom[:, COLS * k : COLS * (k + 1)]
            return own, own
        return None

    def tops(n):
        own = c[n // LEVELS][n % LEVELS][8:]
        more = spare(n)
        return own if more is None else jnp.where(sub == 4, at(more[0][8:], 3, 0), own)

    def bottoms(n):
        own = c[n // LEVELS][n % LEVELS][:8]
        more = spare(n)
        return own if more is None else jnp.where(sub == 3, at(more[1][:8], -3, 0), own)

    for m in range(MEMBERS):
        out_ref[m, MAIL_N:MAIL_S] = jnp.where(sub >= 4, tops(2 * m), at(tops(2 * m + 1), 4, 0))
        out_ref[m, MAIL_S:CHUNK] = jnp.where(sub < 4, bottoms(2 * m), at(bottoms(2 * m + 1), 4, 0))


def edge_steps(flows_ref, west_ref, east_ref, right_ref, left_ref, inner_ref, along_ref):
    block = ids((ROWS, COLS), 1) // 4
    count = flows_ref[ROWS * LEVELS :]

    def packed(of_level, half, ahead):
        tile = jnp.zeros((ROWS, COLS), f32)
        for k in range(LEVELS):
            values = of_level(k)[:, COLS * half : COLS * (half + 1)]
            tile = jnp.where(block % LEVELS == k, at(values, -4 * (k + ahead), 1), tile)
        return tile

    def repeated(tile):
        for step in (32, 64):
            tile = jnp.where(block * 4 % (2 * step) < step, tile, at(tile, -step, 1))
        return tile

    def flow(k):
        return flows_ref[ROWS * k : ROWS * (k + 1)]

    def diffusion(k):
        return jnp.where(count > k, tracer_diffusion, 0.0)

    tiles = []
    for what in ((flow, 1, 1), (flow, 0, 0), (flow, 0, 1), (diffusion, 1, 1), (diffusion, 0, 1)):
        tiles.append(packed(*what))
        yield
    tiles = [repeated(tile) for tile in tiles]
    yield
    last = PLANES // 4
    low, high = outer(
        at(west_ref[last], -4, 1), east_ref[last], left_ref[last], at(right_ref[last], -4, 1),
        *tiles,
    )
    high = at(high, 4, 1)
    yield
    waiting = []
    for n in range(TRACERS * LEVELS):
        both = jnp.where(block == n, low, jnp.where(block == (n + 31) % 32, high, 0.0))
        waiting.append((slice(ROWS * n, ROWS * (n + 1)), at(both, 4 * n, 1)))
        if n % 2:
            yield
    for rows, side in waiting:
        along_ref[rows] = inner_ref[rows] + side


def slab_kernel(
    in_ref, flows_ref, west_ref, east_ref, right_ref, left_ref, inner_ref,
    out_ref, along_ref, edge_ref,
):
    shape = (SLAB, COLS)
    lane = ids(shape, 1)
    r = lane % 8
    block = ids((8, COLS), 1) // 8

    tiles = []
    for t in range(SLAB // 8):
        now = [in_ref[a, 8 * t : 8 * t + 8] for a in range(MEMBERS)]
        for bit in (1, 2, 4, 8):
            odd = (block & bit) > 0
            now = [jnp.where(odd, now[(a + bit) % MEMBERS], now[a]) for a in range(MEMBERS)]
        tiles.append([at(now[-q % MEMBERS], 8 * q, 1) for q in range(16)])
    blocks = [jnp.concatenate([tile[q] for tile in tiles], axis=0) for q in range(16)]
    surface, start_u, start_v, force_u, force_v, bottom = (blocks[2 * n : 2 * n + 2] for n in range(6))
    u_a, v_raw, near, u_next = blocks[12:]
    zeros = jnp.zeros((8, COLS), f32)
    sub = ids((8, COLS), 0)
    edge_ref[COLS - 8 :] = zeros
    for a in range(1, MEMBERS):
        begin, end = in_ref[a, :8], in_ref[a, SLAB - 8 : SLAB]
        rows = jnp.where(sub < 2, begin, at(begin, -1, 0))
        rows = jnp.where(sub < 4, rows, jnp.where(sub < 6, at(end, 2, 0), at(end, 1, 0)))
        edge_ref[8 * a - 8 : 8 * a] = jnp.where(sub % 2 == 0, rows, at(at(rows, 64, 1), -1, 0))
    column = ids(shape, 0)
    far = at(edge_ref[...].T[:SLAB], -4, 0)
    far = jnp.where(column == 68, at(at(force_u[0], 1, 0), 8, 1), far)
    unused = (column < 2) | (column >= SLAB - 2)
    bottom = [jnp.where(unused, float(LEVELS), b) for b in bottom]

    top = lane == COLS - 1
    count_u = [jnp.minimum(b, at(b, 1, 0)) for b in bottom]
    count_v = [
        jnp.minimum(*bottom),
        jnp.where(top, 0.0, jnp.minimum(bottom[1], at(bottom[0], 1, 1))),
    ]

    square = (COLS, COLS)

    def spread_from(lane_at, values):
        chosen = ids(square, 0) == ids(square, 1) // 8 * 8 + lane_at
        spread = jnp.dot(
            jnp.concatenate(values, axis=0).astype(jnp.bfloat16),
            chosen.astype(f32).astype(jnp.bfloat16),
            preferred_element_type=f32,
        )
        return [spread[SLAB * n : SLAB * (n + 1)] for n in range(len(values))]

    count_ua, count_va, count_vc = spread_from(7, [count_u[1], count_v[1], count_v[0]])
    count_ub, count_vb = spread_from(8, [count_u[0], count_v[0]])
    level = r.astype(f32)
    last = lane >= COLS - 8
    v_a = jnp.where(count_va > level, v_raw, 0.0)
    u_a = jnp.where(last, 0.0, u_a)
    u_b = jnp.where(last, 0.0, at(u_next, 8, 1))
    f_a = 0.25 * coriolis(lane // 8 * ROWS + 15, 0.5)
    f_b = f_a + 0.25 * coriolis_base / NLAT
    pair = v_a + at(v_a, 1, 0)
    spread = viscosity * (at(v_a, 1, 0) + at(v_a, -1, 0) - 4.0 * v_a)
    terms = jnp.concatenate(
        [
            jnp.where(count_ua > level, f_a * pair + viscosity * u_b, 0.0),
            jnp.where(count_ub > level, f_b * pair + viscosity * u_a, 0.0),
            jnp.where(count_vb > level, viscosity * v_a, 0.0),
            jnp.where(count_vc > level, viscosity * v_a, 0.0),
            jnp.where(count_va > level, near + far + spread, 0.0),
            v_a,
        ],
        axis=0,
    )
    one = at(terms, -1, 1)
    middle = one[SLAB : 3 * SLAB] + at(terms[SLAB : 3 * SLAB], -2, 1)
    terms = terms + one
    terms = jnp.concatenate([terms[:SLAB], middle, terms[3 * SLAB :]], axis=0)
    for step in (2, 4):
        terms = terms + at(terms, -step, 1)
    shifted = terms[SLAB : 3 * SLAB]
    u_15, v_14, v_15, begin_15 = (
        jnp.where(r == 7, terms[SLAB * n : SLAB * (n + 1)], 0.0) for n in (0, 3, 4, 5)
    )
    u_16, v_16 = (jnp.where(r == 0, shifted[SLAB * n : SLAB * (n + 1)], 0.0) for n in range(2))
    force_u = [force_u[0] + u_16, force_u[1] + u_15]
    force_v = [force_v[0] + (v_14 + v_16), force_v[1] + v_15]
    start_v = [start_v[0], start_v[1] + begin_15]

    sub_step = time_step / SUBSTEPS
    held_u, held_v, flux_u, flux_v, begin_u, begin_v = [], [], [], [], [], []
    for i in range(2):
        per = 1.0 / jnp.maximum(count_u[i], 1.0)
        open_face = jnp.where(count_u[i] > 0.0, sub_step, 0.0)
        flux_u.append((sub_step * surface_scale * thickness) * count_u[i])
        held_u.append(
            (
                (0.25 * open_face) * coriolis(2 * lane + i, 0.5),
                gravity * open_face,
                open_face * (force_u[i] * per),
            )
        )
        begin_u.append(start_u[i] * per)
        per = 1.0 / jnp.maximum(count_v[i], 1.0)
        open_face = jnp.where(count_v[i] > 0.0, sub_step, 0.0)
        flux_v.append((sub_step * surface_scale * thickness) * count_v[i])
        held_v.append(
            (
                (-0.25 * open_face) * coriolis(2 * lane + i, 1.0),
                gravity * open_face,
                open_face * (force_v[i] * per),
            )
        )
        begin_v.append(start_v[i] * per)
    held = (
        *flux_u, at(flux_u[0], 1, 1), *flux_v, at(flux_v[0], 1, 1), at(flux_v[1], -1, 1),
        *held_u[0], *held_u[1], *held_v[0], *held_v[1],
    )
    state = (*surface, at(surface[0], 1, 1), *begin_u, *begin_v)
    total = (zeros,) * 4
    beside = edge_steps(flows_ref, west_ref, east_ref, right_ref, left_ref, inner_ref, along_ref)
    for low, steps in ((0, 6), (8, 8), (16, 8), (24, 8)):
        cut = 8 if low else 0
        state = tuple(x[cut : x.shape[0] - cut] for x in state)
        (
            du0, du1, du2, dv0, dv1, dv2, dv_, cu0, gu0, fu0, cu1, gu1, fu1,
            cv0, gv0, fv0, cv1, gv1, fv1,
        ) = (x[low : SLAB - low] for x in held)
        centre = HALO - low

        def advance(_, carry):
            h0, h1, h2, u0, u1, v0, v1, *sums = carry
            v_ = at(v1, -1, 1)
            u2 = at(u0, 1, 1)
            v2 = at(v0, 1, 1)
            x0, x1, x2 = du0 * u0, du1 * u1, du2 * u2
            y0, y1 = dv0 * v0, dv1 * v1
            h1 = h1 - ((x1 - at(x1, -1, 0)) + (y1 - y0))
            h0 = h0 - ((x0 - at(x0, -1, 0)) + (y0 - dv_ * v_))
            h2 = h2 - ((x2 - at(x2, -1, 0)) + (dv2 * v2 - y1))
            p0, p1, p2 = u0 + at(u0, -1, 0), u1 + at(u1, -1, 0), u2 + at(u2, -1, 0)
            q0, q1 = v0 + v_, v1 + v0
            u0 = (u0 + fu0) + (cu0 * (q0 + at(q0, 1, 0)) - gu0 * (at(h0, 1, 0) - h0))
            u1 = (u1 + fu1) + (cu1 * (q1 + at(q1, 1, 0)) - gu1 * (at(h1, 1, 0) - h1))
            v0 = (v0 + fv0) + (cv0 * (p0 + p1) - gv0 * (h1 - h0))
            v1 = (v1 + fv1) + (cv1 * (p1 + p2) - gv1 * (h2 - h1))
            sums = [a + b[centre : centre + 8] for a, b in zip(sums, (u0, u1, v0, v1))]
            return (h0, h1, h2, u0, u1, v0, v1, *sums)

        carry = (*state, *total)
        for step in range(steps):
            carry = advance(step, carry)
            if low:
                next(beside, None)
        state, total = carry[:7], carry[7:]
    for _ in beside:
        pass
    height = [x[8:16] for x in state[:2]]
    average = [x * (1.0 / SUBSTEPS) for x in total]
    transport = [
        (-thickness * count_u[i][HALO : HALO + 8]) * average[i] for i in range(2)
    ]
    before = jnp.concatenate(
        [
            (ids(square, 0) < (ids(square, 1) - 8 * n) % COLS).astype(f32).astype(jnp.bfloat16)
            for n in (2, 3)
        ],
        axis=1,
    )
    rest = jnp.concatenate([transport[0] + transport[1], zeros], axis=0)
    parts = []
    for _ in range(3):
        parts.append(rest.astype(jnp.bfloat16).astype(f32))
        rest = rest - parts[-1]
    sums = jnp.dot(
        jnp.concatenate(parts, axis=0).astype(jnp.bfloat16),
        before,
        preferred_element_type=f32,
    )
    south = (sums[32:40] + sums[16:24]) + sums[:8]
    stream = [transport[0], transport[0] + transport[1]]
    results = [*height, *stream, *average]
    moved = [at(values, -8 * n, 1) for n, values in enumerate(results)]
    moved[2] = south[:, :COLS] + moved[2]
    moved[3] = south[:, COLS:] + moved[3]
    for e in range(MEMBERS):
        packed = moved[0]
        for n in range(1, 8):
            packed = jnp.where(block == (e + n) % 16, moved[n], packed)
        out_ref[e, 0:8] = packed
        out_ref[e, 8:16] = in_ref[(e + 15) % MEMBERS, MAIL_N:MAIL_S]
        out_ref[e, 16:24] = in_ref[(e + 1) % MEMBERS, MAIL_S:CHUNK]


def gain(values, axis, flow, diffusion):
    ahead = at(values, 1, axis)
    sides = at(values, -1, axis) + at(values, 2, axis)
    far = at(values, -2, axis) + at(values, 3, axis)
    face = (37.0 * (values + ahead) - 8.0 * sides + far) * (1.0 / 60.0)
    flux = diffusion * (ahead - values) - flow * face
    return flux - at(flux, -1, axis)


def inner_kernel(own_ref, out_ref):
    bottom = own_ref[OWN_BOTTOM]
    c = tracer_planes(own_ref)
    count = jnp.minimum(bottom, at(bottom, 1, 1))
    values = jnp.concatenate([plane for tracer in c for plane in tracer], axis=0)
    flow, diffusion = [], []
    for k in range(LEVELS):
        flow.append(jnp.where(count > k, own_ref[OWN_EAST + k], 0.0))
        diffusion.append(jnp.where(count > k, tracer_diffusion, 0.0))
    flow, diffusion = (jnp.concatenate(x * TRACERS, axis=0) for x in (flow, diffusion))
    lane = ids(values.shape, 1)

    def moved(step):
        inside = lane < COLS - step if step > 0 else lane >= -step
        return jnp.where(inside, at(values, step, 1), 0.0)

    ahead = moved(1)
    face = (37.0 * (values + ahead) - 8.0 * (moved(-1) + moved(2)) + (moved(-2) + moved(3))) * (
        1.0 / 60.0
    )
    flux = jnp.where(lane < COLS - 1, diffusion * (ahead - values) - flow * face, 0.0)
    out_ref[...] = flux - at(flux, -1, 1)


def outer(west, east, left, right, flow_w, flow_l, flow_r, diff_w, diff_r):
    q = ids((ROWS, COLS), 1) % 4
    sixtieth = 1.0 / 60.0
    w1, w2, w3 = at(west, 3, 1), at(west, 2, 1), at(west, 1, 1)
    face = 37.0 * (w1 + left) - 8.0 * (w2 + at(left, 1, 1)) + (w3 + at(left, 2, 1))
    through = at(diff_w, 3, 1) * (left - w1) - at(flow_w, 3, 1) * (face * sixtieth)
    flux = jnp.where(q == 0, w2 - 8.0 * w1, jnp.where(q == 1, w2, 0.0)) * (-sixtieth) * flow_l
    low = flux - at(flux, -1, 1) - jnp.where(q == 0, through, 0.0)
    e1, e2, e3 = at(east, -3, 1), at(east, -2, 1), at(east, -1, 1)
    face = 37.0 * (right + e1) - 8.0 * (at(right, -1, 1) + e2) + (at(right, -2, 1) + e3)
    through = diff_r * (e1 - right) - flow_r * (face * sixtieth)
    flux = jnp.where(q == 2, e3 - 8.0 * e2, jnp.where(q == 1, e3, 0.0)) * (-sixtieth) * flow_r
    high = flux - at(flux, -1, 1) + jnp.where(q == 3, through, 0.0)
    return low, high


def finish_kernel(
    place_ref, in_ref, own_ref, west_ref, east_ref, along_ref,
    tracers_out, velocity_out, height_out, stream_out, turned_ref, rows_ref,
):
    place = place_ref[0]
    turned_ref[...] = in_ref[:, 0:8].reshape(COLS, COLS).T

    for q in range(8):
        spot = pl.multiple_of(lax.rem(q + place, 16) * 8, 8)
        rows_ref[pl.ds(ROWS * (q // 2) + q % 2, 8, 2), :] = turned_ref[pl.ds(spot, 8)]
    height_out[...] = rows_ref[:ROWS]
    stream_out[...] = rows_ref[ROWS : 2 * ROWS]
    average_u, average_v = rows_ref[2 * ROWS : 3 * ROWS], rows_ref[3 * ROWS :]

    sub = ids((8, COLS), 0)
    tall = (ROWS + 8, 2 * COLS)
    row = ids(tall, 0)
    first, last = place == 0, place == MEMBERS - 1

    def lat_tile(n):
        south = jnp.where(first, 0.0, in_ref[n // 2, 8:16])
        north = jnp.where(last, 0.0, in_ref[n // 2, 16:24])
        if n % 2 == 0:
            return jnp.where(sub < 4, north, south)
        return at(jnp.where(sub < 4, south, north), 4, 0)

    def spare_north(tile):
        return jnp.where(sub == 0, at(tile, 3, 0), 0.0)

    def spare_south(tile):
        return jnp.where(sub == 7, at(tile, -3, 0), 0.0)

    def tallen(own, tile):
        return jnp.concatenate([own, tile], axis=0)

    def whole(own, plane):
        return wide(own, beside_plane(west_ref, east_ref, plane))

    tiles = [[lat_tile(LEVELS * t + k) for k in range(LEVELS)] for t in range(TRACERS)]
    bottom_own = own_ref[OWN_BOTTOM]
    c = tracer_planes(own_ref)
    p_own = pressures(c[1], c[0])
    p_tile = pressures(tiles[1], tiles[0])
    both = wide(
        spare_north(tiles[3][0]) + spare_south(tiles[3][0]),
        spare_north(tiles[3][1]) + spare_south(tiles[3][1]),
    )
    bottom = tallen(whole(bottom_own, BOTTOM), both)
    count_u = jnp.minimum(bottom, at(bottom, 1, 1))
    count_v = jnp.minimum(bottom, at(bottom, 1, 0))
    f_u = coriolis(place * ROWS + row, 0.5)
    f_v = coriolis(place * ROWS + row, 1.0)
    none = jnp.zeros((8, COLS), f32)
    wind = [tallen(wide(own_ref[OWN_WIND + d], jnp.zeros((ROWS, COLS), f32)), jnp.zeros((8, 2 * COLS), f32)) for d in range(2)]

    def up(x):
        return at(x, 1, 0)

    def down(x):
        return at(x, -1, 0)

    stars_u, stars_v, gains = [], [], [None] * (TRACERS * LEVELS)
    own_u, own_v = count_u[:ROWS, :COLS], count_v[:ROWS, :COLS]
    mean_u = mean_v = jnp.zeros((ROWS, COLS), f32)
    for k in range(LEVELS):
        east, north = count_u > k, count_v > k
        t0, t1, t2 = tiles[0][k], tiles[1][k], tiles[2][k]
        u_lat = wide(spare_north(t0) + spare_south(t0), spare_north(t2))
        v_lat = wide(spare_north(t1) + spare_south(t1), spare_south(t2))
        u = tallen(whole(own_ref[OWN_EAST + k], EAST + k), u_lat)
        u = jnp.where(east | (row >= ROWS), u, 0.0)
        v = tallen(whole(own_ref[OWN_NORTH + k], NORTH + k), v_lat)
        v = jnp.where(north | (row == ROWS), v, 0.0)
        p = tallen(whole(p_own[k], PRESSURE + k), wide(p_tile[k], none))
        tend_u, tend_v = momentum(k, u, v, p, wind, east, north, f_u, f_v, up, down)
        star_u = (u + time_step * tend_u)[:ROWS, :COLS]
        star_v = (v + time_step * tend_v)[:ROWS, :COLS]
        stars_u.append(star_u)
        stars_v.append(star_v)
        mean_u = mean_u + star_u
        mean_v = mean_v + star_v

        diffusion = jnp.where(north[:, :COLS], tracer_diffusion, 0.0)
        for t in range(TRACERS):
            cn = tallen(c[t][k], tiles[t][k])
            gains[LEVELS * t + k] = gain(cn, 0, v[:, :COLS], diffusion)[:ROWS]
    for n in range(TRACERS * LEVELS):
        t, k = divmod(n, LEVELS)
        change = along_ref[ROWS * n : ROWS * (n + 1)] + gains[n]
        tracers_out[t, k] = jnp.where(bottom_own > k, c[t][k] + time_step * change, 0.0)
    shift_u = average_u - mean_u / jnp.maximum(own_u, 1.0)
    shift_v = average_v - mean_v / jnp.maximum(own_v, 1.0)
    for k in range(LEVELS):
        velocity_out[0, k] = jnp.where(own_u > k, stars_u[k] + shift_u, 0.0)
        velocity_out[1, k] = jnp.where(own_v > k, stars_v[k] + shift_v, 0.0)


def ring(axis, step):
    count = lax.axis_size(axis)
    return [(i, (i + step) % count) for i in range(count)]


def struct(*shape):
    return jax.ShapeDtypeStruct(shape, f32)


def vmem(*shape):
    return pltpu.VMEM(shape, f32)


def specs(count, scalars=0):
    return [pl.BlockSpec(memory_space=pltpu.SMEM)] * scalars + [
        pl.BlockSpec(memory_space=pltpu.VMEM)
    ] * count


PARAMS = pltpu.CompilerParams(vmem_limit_bytes=32 * 1024 * 1024)


def stacked(tracers, velocity, surface, wind, bottom):
    def put(values, first):
        values = values.reshape(-1, ROWS, COLS)
        after = OWN - first - values.shape[0]
        return lax.pad(
            values, jnp.zeros((), values.dtype), ((first, after, 0), (0, 0, 0), (0, 0, 0))
        )

    return (
        put(tracers, 0)
        + put(velocity, OWN_EAST)
        + put(surface, OWN_SURFACE)
        + put(wind, OWN_WIND)
        + put(bottom, OWN_BOTTOM).astype(f32)
    )


def shards(tracers, velocity, surface, wind, bottom):
    place = lax.axis_index("lat").astype(jnp.int32).reshape(1)
    own = stacked(tracers, velocity, surface, wind, bottom)
    payload = struct(PLANES // 4 + 1, ROWS, COLS)
    to_right, to_left = pl.pallas_call(
        pack_kernel,
        out_shape=(payload, payload),
        in_specs=specs(1),
        out_specs=tuple(specs(2)),
        compiler_params=PARAMS,
        name="pack",
    )(own)
    west = lax.ppermute(to_right, "lon", ring("lon", 1))
    east = lax.ppermute(to_left, "lon", ring("lon", -1))
    inner = pl.pallas_call(
        inner_kernel,
        out_shape=struct(TRACERS * LEVELS * ROWS, COLS),
        in_specs=specs(1),
        out_specs=specs(1)[0],
        compiler_params=PARAMS,
        cost_estimate=pl.CostEstimate(flops=1500000, bytes_accessed=3000000, transcendentals=0),
        name="inner",
    )(own)
    chunks, flows = pl.pallas_call(
        send_kernel,
        out_shape=(
            struct(MEMBERS, CHUNK, COLS),
            struct((LEVELS + 1) * ROWS, 2 * COLS),
        ),
        in_specs=specs(3, 1) + [pl.BlockSpec(memory_space=pl.ANY)],
        out_specs=tuple(specs(2)),
        scratch_shapes=[
            vmem(12 * ROWS, COLS),
            vmem(2, COLS, COLS),
            vmem(40, 2 * COLS),
            vmem(COLS + 2 * HALO, COLS),
        ],
        compiler_params=PARAMS,
        name="columns",
    )(place, own, west, east, inner)
    slabs = lax.all_to_all(chunks, "lat", 0, 0, tiled=True)
    answers, along = pl.pallas_call(
        slab_kernel,
        out_shape=(
            struct(MEMBERS, BACK, COLS),
            struct(TRACERS * LEVELS * ROWS, COLS),
        ),
        in_specs=specs(7),
        out_specs=tuple(specs(2)),
        scratch_shapes=[vmem(COLS, COLS)],
        compiler_params=PARAMS,
        name="substeps",
    )(slabs, flows, west, east, to_right, to_left, inner)
    home = lax.all_to_all(answers, "lat", 0, 0, tiled=True)
    return pl.pallas_call(
        finish_kernel,
        out_shape=(
            struct(TRACERS, LEVELS, ROWS, COLS),
            struct(2, LEVELS, ROWS, COLS),
            struct(ROWS, COLS),
            struct(ROWS, COLS),
        ),
        in_specs=specs(5, 1),
        out_specs=tuple(specs(4)),
        scratch_shapes=[vmem(COLS, COLS), vmem(4 * ROWS, COLS)],
        compiler_params=PARAMS,
        name="finish",
    )(place, home, own, west, east, along)


def solution(mesh):
    placed = (
        P(None, None, "lat", "lon"),
        P(None, None, "lat", "lon"),
        P("lat", "lon"),
        P(None, "lat", "lon"),
        P("lat", "lon"),
    )
    return jax.shard_map(
        shards,
        mesh=mesh,
        in_specs=placed,
        out_specs=(
            P(None, None, "lat", "lon"),
            P(None, None, "lat", "lon"),
            P("lat", "lon"),
            P("lat", "lon"),
        ),
        check_vma=False,
    )
```
